128 devices in a mesh: row: 8 (over x, core), col: 16 (over y, z).
Axes of the slice: x: 4, y: 4, z: 4, core: 2. Of those that a mesh axis runs over, the one named last changes fastest.
Arguments:
- masters: float32 [256, 4096], P('col'), may hold values from -6 to 6
- inst_master: int32 [128, 256], P('row', 'col'), may hold values from 0 to 255
- inst_orient: int32 [128, 256], P('row', 'col'), may hold values from 0 to 3
- owner_map: int32 [256], replicated, may hold values from 0 to 255, each once
- tile_free: float32 [8192, 16384], P('row', 'col'), may hold values from -3 to 3
- target: float32 [8192, 16384], P('row', 'col'), may hold values from 0 to 1
- kernel_spectra: float32 [2, 128, 8, 128], replicated, may hold values from -6 to 6
- socs_weights: float32 [8], replicated, may hold values from 0.05 to 1
Outputs:
- resist: float32 [8192, 16384], P('row', 'col')
- new_mask: float32 [8192, 16384], P('row', 'col')
- masters_out: float32 [256, 4096], P('col')
The draws below stay inside these ranges and needn't reach their ends.
Inputs may be any that keep to these rules, and one draw needn't show every extreme that they name: `inst_orient`: bit 0 reverses a cell's rows, bit 1 its columns. `owner_map`: each storage row is used by exactly one master; storage row r lies on index r // 16 of col.
All inputs are finite; a program needn't handle non-finite values.
Results may differ from the reference program's by a relative error of at most 0.0092.
Values may be sent and summed in bfloat16 or wider, within the bound.
No kernel may reach another device: no remote copies, remote signals or barrier semaphores. Data moves between devices by JAX's collectives and lax.ppermute only.
A program may use at most 128 MiB of HBM per device.

```python
import math
import jax
import jax.numpy as jnp
import numpy as np
from jax import lax

TILE = 512
TPD = 2
HALO = 64
CELL = 64
BAND = 128
NK = 8
ITERS = 1
PAD = 640
NM = 256
ROWS = 8192
COLS = 16384
GRID_R = 128
GRID_C = 256
N_ROW = 8
N_COL = 16


def place_ends(values, own_key, least, high):
    dims = values.shape
    spot = [jax.random.randint(jax.random.fold_in(own_key, axis), (), 0, dims[axis]) for axis in range(len(dims))]
    values = values.at[tuple(spot)].set(least)
    longest = dims.index(max(dims))
    spot[longest] = (spot[longest] + 1) % dims[longest]
    return values.at[tuple(spot)].set(high)


def block_scale(rng, extent, shards, low, largest):
    def one(position, shards_of):
        draws = jax.random.uniform(jax.random.fold_in(jax.random.fold_in(rng, 6), position), (shards_of,), jnp.float32, low / len(shards), largest / len(shards))
        return jnp.repeat(jnp.exp(draws), extent[position] // shards_of).reshape((-1,) + (1,) * (len(extent) - position - 1))

    gain = one(*shards[0])
    for cut in shards[1:]:
        gain = gain * one(*cut)
    return gain


def rank_bounds(count, skew):
    portions = [(1 << 20) // math.isqrt(standing ** skew) + 1 for standing in range(1, count + 1)]
    deviation = 1 + sum(portions) // (1 << 30)
    return np.cumsum(np.array([max(1, weight // deviation) for weight in portions]))


def ranked(own_key, shape, count, slope):
    listing = rank_bounds(count, slope)
    lot = jax.random.randint(jax.random.fold_in(own_key, 1), shape, 0, int(listing[count - 1]))
    standing = jnp.searchsorted(jnp.asarray(listing, jnp.int32), lot, side="right")
    return jax.random.permutation(jax.random.fold_in(own_key, 2), count)[standing].astype(jnp.int32)


def bell_draw(stream_key, extent, deviation, reach, shards=(), kind=jnp.bfloat16):
    gain = block_scale(stream_key, extent, shards, -0.22, 0.18) if shards else 1.0
    entries = jax.random.normal(stream_key, extent, jnp.float32) * deviation * gain
    return jnp.minimum(jnp.maximum(entries, -reach), reach).astype(kind)


def setup_inputs(seed: int = 0) -> dict:
    key_of = jax.random.split(jax.random.key(seed), 9)
    return {
        "masters": bell_draw(key_of[0], (NM, CELL * CELL), 1.0, 6.0, ((0, 16),), jnp.float32),
        "inst_master": place_ends(ranked(key_of[1], (GRID_R, GRID_C), NM, 2), jax.random.fold_in(key_of[1], 3), 0, NM - 1).astype(jnp.int32),
        "inst_orient": place_ends(jax.random.randint(key_of[2], (GRID_R, GRID_C), 0, 4), jax.random.fold_in(key_of[2], 1), 0, 3).astype(jnp.int32),
        "owner_map": jax.random.permutation(key_of[3], NM).astype(jnp.int32),
        "tile_free": bell_draw(key_of[4], (ROWS, COLS), 0.5, 3.0, ((0, 8), (1, 16)), jnp.float32),
        "target": jnp.clip(1.0 * jax.random.uniform(key_of[5], (ROWS, COLS), jnp.float32) ** block_scale(key_of[5], (ROWS, COLS), ((0, 8), (1, 16)), -0.2, 0.2), 0.0, 1.0),
        "kernel_spectra": bell_draw(key_of[6], (2, BAND, NK, BAND), 1.0, 6.0, (), jnp.float32),
        "socs_weights": jnp.clip(jnp.exp(jax.random.uniform(key_of[7], (NK,), jnp.float32, math.log(0.05), math.log(1.0))), 0.05, 1.0),
    }


step_free = 1.0
step_master = 0.05
resist_gain = 2.0
resist_level = 1.8


def dot_plain(left, right):
    return jnp.dot(left, right, preferred_element_type=jnp.float32)


def dot_right_t(left, right):
    return lax.dot_general(left, right, (((1,), (1,)), ((), ())), preferred_element_type=jnp.float32)


def dot_left_t(left, right):
    return lax.dot_general(left, right, (((0,), (0,)), ((), ())), preferred_element_type=jnp.float32)


def tables(pad_side, band_side):
    freqs = jnp.arange(band_side, dtype=jnp.int32) - band_side // 2
    pixels = jnp.arange(pad_side, dtype=jnp.int32)
    phases = (freqs[:, None] * pixels[None, :]) % pad_side
    angles = phases.astype(jnp.float32) * (2.0 * math.pi / pad_side)
    return jnp.cos(angles).astype(jnp.bfloat16), jnp.sin(angles).astype(jnp.bfloat16)


def tile_step(padded, target, spectra, weights, halo_side):
    pad_side = padded.shape[0]
    band_side = spectra.shape[1]
    kernels = spectra.shape[2]
    tile_side = pad_side - 2 * halo_side
    cos_full, sin_full = tables(pad_side, band_side)
    cos_in = cos_full[:, halo_side:halo_side + tile_side]
    sin_in = sin_full[:, halo_side:halo_side + tile_side]
    forw_re = dot_plain(cos_full, padded).astype(jnp.bfloat16)
    forw_im = (-dot_plain(sin_full, padded)).astype(jnp.bfloat16)
    spec_re = (dot_right_t(forw_re, cos_full) - dot_right_t(forw_im, sin_full)) / pad_side
    spec_im = (-dot_right_t(forw_re, sin_full) - dot_right_t(forw_im, cos_full)) / pad_side
    kern_re = spectra[0]
    kern_im = spectra[1]
    amp_re = (kern_re * spec_re[:, None, :] - kern_im * spec_im[:, None, :]).astype(jnp.bfloat16)
    amp_im = (kern_re * spec_im[:, None, :] + kern_im * spec_re[:, None, :]).astype(jnp.bfloat16)
    amp_re = amp_re.reshape(band_side, kernels * band_side)
    amp_im = amp_im.reshape(band_side, kernels * band_side)
    half_re = (dot_left_t(cos_in, amp_re) - dot_left_t(sin_in, amp_im)).astype(jnp.bfloat16)
    half_im = (dot_left_t(cos_in, amp_im) + dot_left_t(sin_in, amp_re)).astype(jnp.bfloat16)
    half_re = half_re.reshape(tile_side * kernels, band_side)
    half_im = half_im.reshape(tile_side * kernels, band_side)
    field_re = (dot_plain(half_re, cos_in) - dot_plain(half_im, sin_in)) / band_side
    field_im = (dot_plain(half_re, sin_in) + dot_plain(half_im, cos_in)) / band_side
    field_re = field_re.reshape(tile_side, kernels, tile_side)
    field_im = field_im.reshape(tile_side, kernels, tile_side)
    scaled = weights[None, :, None]
    intensity = jnp.sum(scaled * (field_re * field_re + field_im * field_im), axis=1)
    resist = jax.nn.sigmoid(resist_gain * (intensity - resist_level))
    slopes = 2.0 * (resist - target) * resist_gain * resist * (1.0 - resist)
    back_re = (2.0 / band_side * scaled * slopes[:, None, :] * field_re).astype(jnp.bfloat16)
    back_im = (2.0 / band_side * scaled * slopes[:, None, :] * field_im).astype(jnp.bfloat16)
    back_re = back_re.reshape(tile_side * kernels, tile_side)
    back_im = back_im.reshape(tile_side * kernels, tile_side)
    bhalf_re = (dot_right_t(back_re, cos_in) + dot_right_t(back_im, sin_in)).astype(jnp.bfloat16)
    bhalf_im = (dot_right_t(back_im, cos_in) - dot_right_t(back_re, sin_in)).astype(jnp.bfloat16)
    bhalf_re = bhalf_re.reshape(tile_side, kernels * band_side)
    bhalf_im = bhalf_im.reshape(tile_side, kernels * band_side)
    bamp_re = (dot_plain(cos_in, bhalf_re) + dot_plain(sin_in, bhalf_im)).reshape(band_side, kernels, band_side)
    bamp_im = (dot_plain(cos_in, bhalf_im) - dot_plain(sin_in, bhalf_re)).reshape(band_side, kernels, band_side)
    bspec_re = (jnp.sum(kern_re * bamp_re + kern_im * bamp_im, axis=1) / pad_side).astype(jnp.bfloat16)
    bspec_im = (jnp.sum(kern_re * bamp_im - kern_im * bamp_re, axis=1) / pad_side).astype(jnp.bfloat16)
    bforw_re = (dot_plain(bspec_re, cos_in) - dot_plain(bspec_im, sin_in)).astype(jnp.bfloat16)
    bforw_im = (-dot_plain(bspec_re, sin_in) - dot_plain(bspec_im, cos_in)).astype(jnp.bfloat16)
    gradient = dot_left_t(cos_in, bforw_re) - dot_left_t(sin_in, bforw_im)
    return resist, gradient


def orient_cells(cells, orient):
    flip_first = (orient % 2) == 1
    flip_second = (orient // 2) == 1
    cells = jnp.where(flip_first[..., None, None], cells[..., ::-1, :], cells)
    cells = jnp.where(flip_second[..., None, None], cells[..., :, ::-1], cells)
    return cells


def assemble(master_rows, slots, orient, cell_side):
    grid_rows, grid_cols = slots.shape
    cells = jnp.take(master_rows, slots.reshape(-1), axis=0)
    cells = cells.reshape(grid_rows, grid_cols, cell_side, cell_side)
    cells = orient_cells(cells, orient)
    return cells.transpose(0, 2, 1, 3).reshape(grid_rows * cell_side, grid_cols * cell_side)


def cells_of(image, orient, cell_side):
    grid_rows, grid_cols = orient.shape
    cells = image.reshape(grid_rows, cell_side, grid_cols, cell_side).transpose(0, 2, 1, 3)
    cells = orient_cells(cells, orient)
    return cells.reshape(grid_rows * grid_cols, cell_side * cell_side)


def smooth(master_rows, cell_side):
    grids = master_rows.reshape(-1, cell_side, cell_side)
    framed = jnp.pad(grids, ((0, 0), (1, 1), (1, 1)))
    beside_all = framed[:, 2:, 1:-1] + framed[:, :-2, 1:-1] + framed[:, 1:-1, 2:] + framed[:, 1:-1, :-2]
    return (0.5 * grids + 0.125 * beside_all).reshape(master_rows.shape)


def stitch(tiles, tile_rows, tile_cols):
    return tiles.reshape(tile_rows, tile_cols, TILE, TILE).transpose(0, 2, 1, 3).reshape(tile_rows * TILE, tile_cols * TILE)


def reference(masters, inst_master, inst_orient, owner_map, tile_free, target, kernel_spectra, socs_weights):
    slots = jnp.take(owner_map, inst_master)
    master_rows = masters
    free_field = tile_free
    resist = jnp.zeros_like(tile_free)
    tile_rows = N_ROW * TPD
    tile_cols = N_COL * TPD
    for sweep_index in range(ITERS):
        shading = jnp.tanh(assemble(master_rows, slots, inst_orient, CELL) + free_field)
        framed = jnp.pad(shading.astype(jnp.bfloat16), HALO)

        def one_tile(tile_index):
            row_at = tile_index // tile_cols
            col_at = tile_index % tile_cols
            window = lax.dynamic_slice(framed, (row_at * TILE, col_at * TILE), (PAD, PAD))
            goal_tile = lax.dynamic_slice(target, (row_at * TILE, col_at * TILE), (TILE, TILE))
            return tile_step(window, goal_tile, kernel_spectra, socs_weights, HALO)

        resist_tiles, grad_tiles = lax.map(one_tile, jnp.arange(tile_rows * tile_cols, dtype=jnp.int32))
        resist = stitch(resist_tiles, tile_rows, tile_cols)
        grad_param = stitch(grad_tiles, tile_rows, tile_cols) * (1.0 - shading * shading)
        free_field = free_field - step_free * grad_param
        cell_grads = cells_of(grad_param, inst_orient, CELL)
        master_grad = jax.ops.segment_sum(cell_grads, slots.reshape(-1), num_segments=NM)
        master_rows = smooth(master_rows - step_master * master_grad, CELL)
    new_mask = jnp.tanh(assemble(master_rows, slots, inst_orient, CELL) + free_field)
    return resist, new_mask, master_rows
```

```python
import functools

import jax
import jax.numpy as jnp
import numpy as np
from jax import lax
from jax.experimental import pallas as pl
from jax.experimental.pallas import tpu as pltpu
from jax.sharding import PartitionSpec as P

TILE, HALO, CELL, BAND, NK, PAD = 512, 64, 64, 128, 8, 640
GRID = 256
SIDE = 1024
BOTH = ("row", "col")
F32, BF16 = jnp.float32, jnp.bfloat16


def waves(positions, period):
    freqs = np.arange(BAND) - BAND // 2
    angles = 2.0 * np.pi * ((freqs[:, None] * positions[None, :]) % period) / period
    return np.cos(angles), np.sin(angles)


def mean_gain(cos, sin):
    rounded = [t.astype(jnp.bfloat16).astype(np.float64) for t in (cos, sin)]
    return (rounded[0] * cos + rounded[1] * sin).mean(1)


@functools.cache
def constant_tables():
    cos_c, sin_c = waves(np.arange(GRID), GRID)
    cos_p, sin_p = waves(np.arange(PAD), PAD)
    cos_i, sin_i = cos_p[:, HALO : HALO + TILE], sin_p[:, HALO : HALO + TILE]
    by_pixel = np.concatenate([cos_p.T, sin_p.T], 1)
    first = np.zeros((2, 768, 256))
    first[0, 0:576] = by_pixel[64:640]
    first[0, 640:704] = by_pixel[0:64]
    first[1, 64:640] = by_pixel[0:576]
    first[1, 704:768] = by_pixel[576:640]
    second = np.concatenate([cos_p, sin_p], 0)
    up_u = np.block([[cos_c.T, -sin_c.T], [sin_c.T, cos_c.T]])
    up_v = np.block([[cos_c, sin_c], [-sin_c, cos_c]])
    places = (HALO + np.arange(TILE)) / PAD
    orders = np.arange(1, BAND)
    shift = places[:, None] - np.arange(GRID)[None, :] / GRID
    fine = (1.0 + 2.0 * np.cos(2 * np.pi * shift[..., None] * orders).sum(-1)) / GRID
    out_v = np.block([[cos_i, -sin_i], [-sin_i, -cos_i]])
    out_u = np.concatenate([cos_i.T, -sin_i.T], 1)
    high = fine.astype(jnp.bfloat16)
    low = (fine - high.astype(np.float64)).astype(jnp.bfloat16)
    cast = lambda a: np.ascontiguousarray(a).astype(jnp.bfloat16)
    gain = mean_gain(cos_i, sin_i) / mean_gain(cos_c, sin_c)
    return [
        np.outer(gain, gain).astype(np.float32), cast(first), cast(second), cast(up_u), cast(up_u.T), cast(up_v), cast(up_v.T),
        high, low, cast(fine.T), cast(low.T), cast(out_v), cast(out_u),
    ]


def dot(a, b):
    return jnp.dot(a, b, preferred_element_type=F32)


def index_vectors(orient):
    lane = lax.broadcasted_iota(jnp.int32, (8, 128), 1)
    sub = lax.broadcasted_iota(jnp.int32, (8, 128), 0)
    flip_rows = lax.rem(orient, 2) == 1
    flip_cols = orient >= 2
    lanes = jnp.where(flip_cols, jnp.where(lane < 64, 63 - lane, 191 - lane), lane)
    subs = jnp.where(flip_rows, 7 - sub, sub)
    return flip_rows, lanes, subs


def oriented(groups, orient):
    flip_rows, lanes, subs = index_vectors(orient)
    turned = []
    for g in groups:
        g = jnp.take_along_axis(g, lanes, axis=1)
        turned.append(jnp.take_along_axis(g, subs, axis=0))
    return [
        jnp.where(flip_rows, pltpu.roll(turned[3 - i], 64, 1), turned[i]) for i in range(4)
    ]


def pair_image(cells_ref, loc_a, turn_a, loc_b, turn_b):
    lane = lax.broadcasted_iota(jnp.int32, (8, 128), 1)
    a = oriented([cells_ref[loc_a, 8 * i : 8 * i + 8, :] for i in range(4)], turn_a)
    b = oriented([cells_ref[loc_b, 8 * i : 8 * i + 8, :] for i in range(4)], turn_b)
    top = [jnp.where(lane < 64, a[i], pltpu.roll(b[i], 64, 1)) for i in range(4)]
    low = [jnp.where(lane < 64, pltpu.roll(a[i], 64, 1), b[i]) for i in range(4)]
    return jnp.concatenate(top + low, axis=0)


def fill_cells(parts, cells_ref):
    for n, part in enumerate(parts):
        cells_ref[pl.ds(32 * n, 32)] = part[...].astype(F32)


def main_kernel(*refs):
    codes, weights = refs[0:2]
    parts = refs[2:10]
    free, top, bottom, before, after, target, spectra = refs[10:17]
    (gain, first, second, up_u, up_ut, up_v, up_vt, fine, fine_lo, fine_t, fine_tlo, out_v, out_u) = refs[17:30]
    resist_out, free_out, own_out, other_out = refs[30:34]
    cells, mask, shading, fields, amps, halves, sums = refs[34:41]

    def code(a, b):
        return codes[a * 18 + b], codes[324 + a * 18 + b]

    fill_cells(parts, cells)

    def interior(a, _):
        rows = pl.ds(pl.multiple_of(a * 64, 64), 64)
        rows_m = pl.ds(pl.multiple_of(a * 64 + 64, 64), 64)
        for p in range(8):
            cols = slice(p * 128, p * 128 + 128)
            image = pair_image(cells, *code(a + 1, 2 * p + 1), *code(a + 1, 2 * p + 2))
            value = jnp.tanh(image + free[rows, cols])
            shading[rows, cols] = value
            mask[rows_m, cols] = value.astype(BF16)
        return 0

    lax.fori_loop(0, 16, interior, 0)

    for a, strip, flag in ((0, top, 648), (17, bottom, 649)):
        for p in range(8):
            cols = slice(p * 128, p * 128 + 128)
            image = pair_image(cells, *code(a, 2 * p + 1), *code(a, 2 * p + 2))
            value = jnp.tanh(image + strip[0:64, cols].astype(F32))
            value = jnp.where(codes[flag] > 0, value, 0.0)
            mask[a * 64 : a * 64 + 64, cols] = value.astype(BF16)

    def edge_cols(n, _):
        for u in range(3):
            edge_cell(n * 3 + u)
        return 0

    def edge_cell(a):
        rows = pl.ds(pl.multiple_of(a * 64, 64), 64)
        image = pair_image(cells, *code(a, 0), *code(a, 17))
        strips = jnp.concatenate([before[rows, :], after[rows, :]], axis=1)
        value = jnp.tanh(image + strips.astype(F32))
        lane = lax.broadcasted_iota(jnp.int32, (64, 128), 1)
        at_row = jnp.where(a == 0, codes[648], jnp.where(a == 17, codes[649], 1))
        keep = jnp.where(lane < 64, codes[650], codes[651]) * at_row
        mask[rows, 1024:1152] = jnp.where(keep > 0, value, 0.0).astype(BF16)

    lax.fori_loop(0, 6, edge_cols, 0)

    def tile(t, _):
        i, j = t // 2, t % 2
        rows_w = pl.ds(pl.multiple_of(i * TILE, 128), PAD)
        window = jnp.concatenate(
            [mask[rows_w, pl.ds(pl.multiple_of(j * 384, 128), 640)], mask[rows_w, 1024:1152]], axis=1
        )
        forw = dot(window, first[j]).astype(BF16)
        spec = dot(second[...], forw)
        scale = gain[...] * (1.0 / PAD)
        spec_re = (spec[:128, :128] + spec[128:, 128:]) * scale
        spec_im = (spec[128:, :128] - spec[:128, 128:]) * scale
        for k in range(NK):
            at = slice(k * 128, k * 128 + 128)
            k_re, k_im = spectra[0, :, at], spectra[1, :, at]
            amps[0:128, at] = (k_re * spec_re - k_im * spec_im).astype(BF16)
            amps[128:256, at] = (k_re * spec_im + k_im * spec_re).astype(BF16)
        halves[...] = dot(up_u[...], amps[...]).astype(BF16)
        intensity = jnp.zeros((GRID, GRID), F32)
        for k in range(NK):
            at = slice(k * 128, k * 128 + 128)
            left = jnp.concatenate([halves[0:256, at], halves[256:512, at]], axis=1)
            field = dot(left, up_v[...]) * (1.0 / BAND)
            fields[k] = field
            re, im = field[:, :256], field[:, 256:]
            intensity = intensity + weights[k] * (re * re + im * im)
        coarse = intensity.astype(BF16)
        half_fine = dot(fine[...], coarse) + dot(fine_lo[...], coarse)
        half_fine = half_fine.astype(BF16)
        image = dot(half_fine, fine_t[...]) + dot(half_fine, fine_tlo[...])
        rows_t = pl.ds(pl.multiple_of(i * TILE, TILE), TILE)
        cols_t = pl.ds(pl.multiple_of(j * TILE, TILE), TILE)
        resist = jax.nn.sigmoid(2.0 * (image - 1.8))
        resist_out[rows_t, cols_t] = resist
        slopes = (4.0 * (resist - target[rows_t, cols_t]) * resist * (1.0 - resist)).astype(BF16)
        back = dot(fine_t[...], dot(slopes, fine[...]).astype(BF16))
        for k in range(NK):
            at = slice(k * 128, k * 128 + 128)
            scaled = back * (weights[k] * (2.0 / BAND))
            both = jnp.concatenate(
                [(scaled * fields[k, :, :256]).astype(BF16), (scaled * fields[k, :, 256:]).astype(BF16)], axis=1
            )
            low = dot(both, up_vt[...]).astype(BF16)
            halves[0:256, at] = low[:, :128]
            halves[256:512, at] = low[:, 128:]
        bspec_re = jnp.zeros((128, 128), F32)
        bspec_im = jnp.zeros((128, 128), F32)
        bamp = dot(up_ut[...], halves[...])
        for k in range(NK):
            at = slice(k * 128, k * 128 + 128)
            k_re, k_im = spectra[0, :, at], spectra[1, :, at]
            re, im = bamp[:128, at], bamp[128:, at]
            bspec_re = bspec_re + (k_re * re + k_im * im)
            bspec_im = bspec_im + (k_re * im - k_im * re)
        bspec = jnp.concatenate([bspec_re * scale, bspec_im * scale], axis=1)
        bforw = dot(bspec.astype(BF16), out_v[...]).astype(BF16)
        stacked = jnp.concatenate([bforw[:, :TILE], bforw[:, TILE:]], axis=0)
        gradient = dot(out_u[...], stacked)
        shade = shading[rows_t, cols_t]
        grad = gradient * (1.0 - shade * shade)
        shading[rows_t, cols_t] = grad
        free_out[rows_t, cols_t] = free[rows_t, cols_t] - grad
        return 0

    lax.fori_loop(0, 4, tile, 0)

    def clear(n, _):
        sums[pl.ds(n * 8, 8)] = jnp.zeros((8, 32, 128), F32)
        return 0

    lax.fori_loop(0, 32, clear, 0)
    lane = lax.broadcasted_iota(jnp.int32, (8, 128), 1)

    def collect(a, _):
        rows = pl.multiple_of(a * 64, 64)
        for batch in range(4):
            found = []
            for p in (2 * batch, 2 * batch + 1):
                cols = slice(p * 128, p * 128 + 128)
                upper = [shading[pl.ds(rows + 8 * i, 8), cols] for i in range(4)]
                lower = [shading[pl.ds(rows + 32 + 8 * i, 8), cols] for i in range(4)]
                left = [jnp.where(lane < 64, upper[i], pltpu.roll(lower[i], 64, 1)) for i in range(4)]
                right = [jnp.where(lane < 64, pltpu.roll(upper[i], 64, 1), lower[i]) for i in range(4)]
                for b, groups in ((2 * p + 1, left), (2 * p + 2, right)):
                    loc, turn = code(a + 1, b)
                    found.append((loc, oriented(groups, turn)))
            for loc, out in found:
                for i in range(4):
                    sums[loc, 8 * i : 8 * i + 8, :] = sums[loc, 8 * i : 8 * i + 8, :] + out[i]
        return 0

    lax.fori_loop(0, 16, collect, 0)
    own_out[...] = sums[0:128].astype(BF16)
    other_out[...] = sums[128:256].astype(BF16)


def final_kernel(*refs):
    codes = refs[0]
    parts = refs[1:9]
    free, out, cells = refs[9:12]
    step = pl.program_id(0)

    @pl.when(step == 0)
    def _():
        fill_cells(parts, cells)

    def interior(r, _):
        rows = pl.ds(pl.multiple_of(r * 64, 64), 64)
        for p in range(8):
            cols = slice(p * 128, p * 128 + 128)
            at = (step * 4 + r + 1) * 18 + 2 * p
            image = pair_image(cells, codes[at + 1], codes[325 + at], codes[at + 2], codes[326 + at])
            out[rows, cols] = jnp.tanh(image + free[rows, cols])
        return 0

    lax.fori_loop(0, 4, interior, 0)


def flat(x, c, y, z):
    return ((x % 4) * 2 + c) * 16 + (y % 4) * 4 + z % 4


CHIPS = [(x, y, z) for x in range(4) for y in range(4) for z in range(4)]


def shift_first(d):
    return [(flat(x, 0, y, z), flat(x, 0, y, z + d)) for x, y, z in CHIPS] + [
        (flat(x, 1, y, z), flat(x, 1, y + d, z)) for x, y, z in CHIPS
    ]


def shift_second(d):
    return [(flat(x, 0, y, z), flat(x, 0, y + d, z)) for x, y, z in CHIPS] + [
        (flat(x, 1, y, z), flat(x, 1, y, z + d)) for x, y, z in CHIPS
    ]


def shift_x(d):
    return [(flat(x, c, y, z), flat(x + d, c, y, z)) for x, y, z in CHIPS for c in range(2)]


SWAP = [(flat(x, c, y, z), flat(x, 1 - c, y, z)) for x, y, z in CHIPS for c in range(2)]


def send(value, pairs):
    return lax.ppermute(value, BOTH, pairs)


def gathered(piece):
    got = {d: send(piece, shift_first(d)) for d in (2, 1, 3)}
    group = jnp.concatenate([piece, got[1], got[2], got[3]], axis=0)
    far = {d: send(group, shift_second(d)) for d in (2, 1, 3)}
    mine = [group, far[1], far[2], far[3]]
    return mine + [send(part, SWAP) for part in mine]


def scattered_sum(own, other):
    total = (own.astype(F32) + send(other, SWAP).astype(F32)).astype(BF16).reshape(4, 32, 32, 128)
    got = [send(total[d], shift_second(-d)) for d in (2, 1, 3)]
    total = sum((g.astype(F32) for g in got), total[0].astype(F32)).astype(BF16).reshape(4, 8, 32, 128)
    got = [send(total[d], shift_first(-d)) for d in (2, 1, 3)]
    total = sum((g.astype(F32) for g in got), total[0].astype(F32)).astype(BF16)
    got = [send(total, shift_x(d)) for d in (2, 1, 3)]
    return sum((g.astype(F32) for g in got), total.astype(F32))


def to_wire(rows):
    cells = rows.reshape(-1, CELL, CELL)
    return jnp.concatenate([cells[:, :32, :], cells[:, 32:, :]], axis=2)


def from_wire(wire):
    return jnp.concatenate([wire[:, :, :64], wire[:, :, 64:]], axis=1)


def smooth(grids):
    framed = jnp.pad(grids, ((0, 0), (1, 1), (1, 1)))
    beside = framed[:, 2:, 1:-1] + framed[:, :-2, 1:-1] + framed[:, 1:-1, 2:] + framed[:, 1:-1, :-2]
    return 0.5 * grids + 0.125 * beside


def steps(axis):
    n = lax.axis_size(axis)
    up = [(i, i + 1) for i in range(n - 1)]
    return up, [(b, a) for a, b in up]


def per_device(masters, inst_master, inst_orient, owner_map, tile_free, target, spectra, weights):
    row, col = lax.axis_index("row"), lax.axis_index("col")
    core, y, z = row % 2, col // 4, col % 4
    own_cells = lax.dynamic_slice_in_dim(masters, core * 8, 8, 0)
    parts = gathered(to_wire(own_cells.astype(BF16)))

    def codes_of(a):
        return jnp.pad(a.astype(BF16), ((0, 0), (0, SIDE - a.shape[1])))

    def strip(at, line):
        pad = jnp.concatenate([codes_of(inst_master[line : line + 1]), codes_of(inst_orient[line : line + 1])], 0)
        return jnp.concatenate([tile_free[at : at + 64].astype(BF16), jnp.pad(pad, ((0, 14), (0, 0)))], 0)

    up, down = steps("row")
    above = lax.ppermute(strip(SIDE - 64, 15), "row", up)
    below = lax.ppermute(strip(0, 0), "row", down)

    def ints(a):
        return a.astype(F32).astype(jnp.int32)

    tall_master = jnp.concatenate([ints(above[64:65, :16]), inst_master, ints(below[64:65, :16])], 0)
    tall_orient = jnp.concatenate([ints(above[65:66, :16]), inst_orient, ints(below[65:66, :16])], 0)

    def side(at, line):
        pixels = jnp.concatenate(
            [above[:64, at : at + 64], tile_free[:, at : at + 64].astype(BF16), below[:64, at : at + 64]], 0
        )
        lines = jnp.stack([tall_master[:, line], tall_orient[:, line]], 1).astype(BF16)
        return jnp.concatenate([pixels, jnp.pad(lines, ((0, 14), (0, 62)))], 0)

    up, down = steps("col")
    before = lax.ppermute(side(SIDE - 64, 15), "col", up)
    after = lax.ppermute(side(0, 0), "col", down)
    all_master = jnp.concatenate([ints(before[1152:1170, 0:1]), tall_master, ints(after[1152:1170, 0:1])], 1)
    all_orient = jnp.concatenate([ints(before[1152:1170, 1:2]), tall_orient, ints(after[1152:1170, 1:2])], 1)

    matches = all_master[..., None] == jnp.arange(owner_map.shape[0], dtype=jnp.int32)
    slots = jnp.sum(jnp.where(matches, owner_map, 0), axis=-1)
    at_y, at_z, half, entry = slots // 64, (slots // 16) % 4, (slots // 8) % 2, slots % 8
    dy, dz = (y - at_y) % 4, (z - at_z) % 4
    far, near = jnp.where(half == 0, dy, dz), jnp.where(half == 0, dz, dy)
    locs = (jnp.where(half == core, 0, 1) * 16 + far * 4 + near) * 8 + entry
    inside = jnp.stack([row > 0, row < 7, col > 0, col < 15]).astype(jnp.int32)
    codes = jnp.concatenate([locs.reshape(-1), all_orient.reshape(-1), inside])

    vmem, smem = pl.BlockSpec(memory_space=pltpu.VMEM), pl.BlockSpec(memory_space=pltpu.SMEM)
    wide = jax.ShapeDtypeStruct((SIDE, SIDE), F32)
    sums_shape = jax.ShapeDtypeStruct((128, 32, 128), BF16)
    resist, free_new, own, other = pl.pallas_call(
        main_kernel,
        out_shape=(wide, wide, sums_shape, sums_shape),
        in_specs=[smem] * 2 + [vmem] * 28,
        out_specs=(vmem,) * 4,
        scratch_shapes=[
            pltpu.VMEM((256, 32, 128), F32),
            pltpu.VMEM((1152, 1152), BF16),
            pltpu.VMEM((SIDE, SIDE), F32),
            pltpu.VMEM((NK, GRID, 2 * GRID), F32),
            pltpu.VMEM((256, 1024), BF16),
            pltpu.VMEM((512, 1024), BF16),
            pltpu.VMEM((256, 32, 128), F32),
        ],
        compiler_params=pltpu.CompilerParams(vmem_limit_bytes=60 * 1024 * 1024),
        name="image_and_gradient",
    )(
        codes, weights, *parts, tile_free, above, below, before, after, target,
        spectra.reshape(2, BAND, NK * BAND), *constant_tables(),
    )

    summed = scattered_sum(own, other)
    fresh = smooth(own_cells.reshape(8, CELL, CELL) - 0.05 * from_wire(summed))
    fresh_wire = jnp.concatenate([fresh[:, :32, :], fresh[:, 32:, :]], axis=2).astype(BF16)
    parts = gathered(fresh_wire)
    new_mask = pl.pallas_call(
        final_kernel,
        out_shape=wide,
        grid=(4,),
        in_specs=[smem] + [vmem] * 8 + [pl.BlockSpec((256, SIDE), lambda s: (s, 0))],
        out_specs=pl.BlockSpec((256, SIDE), lambda s: (s, 0)),
        scratch_shapes=[pltpu.VMEM((256, 32, 128), F32)],
        compiler_params=pltpu.CompilerParams(vmem_limit_bytes=40 * 1024 * 1024),
        name="final_mask",
    )(codes, *parts, free_new)
    mine = from_wire(parts[0][:8]).reshape(8, CELL * CELL).astype(F32)
    others = from_wire(parts[4][:8]).reshape(8, CELL * CELL).astype(F32)
    masters_out = jnp.where(core == 0, jnp.concatenate([mine, others], 0), jnp.concatenate([others, mine], 0))
    return resist, new_mask, masters_out


def solution(mesh):
    placed = (P("col", None), P(*BOTH), P(*BOTH), P(), P(*BOTH), P(*BOTH), P(), P())
    return jax.shard_map(
        per_device,
        mesh=mesh,
        in_specs=placed,
        out_specs=(P(*BOTH), P(*BOTH), P("col", None)),
        check_vma=False,
    )
```

```python
import functools

import jax
import jax.numpy as jnp
import numpy as np
from jax import lax
from jax.experimental import pallas as pl
from jax.experimental.pallas import tpu as pltpu
from jax.sharding import PartitionSpec as P

TILE, HALO, CELL, BAND, NK, PAD = 512, 64, 64, 128, 8, 640
GRID = 256
SIDE = 1024
BOTH = ("row", "col")
F32, BF16 = jnp.float32, jnp.bfloat16


def waves(positions, period):
    freqs = np.arange(BAND) - BAND // 2
    angles = 2.0 * np.pi * ((freqs[:, None] * positions[None, :]) % period) / period
    return np.cos(angles), np.sin(angles)


def mean_gain(cos, sin):
    rounded = [t.astype(jnp.bfloat16).astype(np.float64) for t in (cos, sin)]
    return (rounded[0] * cos + rounded[1] * sin).mean(1)


@functools.cache
def constant_tables():
    cos_c, sin_c = waves(np.arange(GRID), GRID)
    cos_p, sin_p = waves(np.arange(PAD), PAD)
    cos_i, sin_i = cos_p[:, HALO : HALO + TILE], sin_p[:, HALO : HALO + TILE]
    by_pixel = np.concatenate([cos_p.T, sin_p.T], 1)
    first = np.zeros((2, 768, 256))
    first[0, 0:576] = by_pixel[64:640]
    first[0, 640:704] = by_pixel[0:64]
    first[1, 64:640] = by_pixel[0:576]
    first[1, 704:768] = by_pixel[576:640]
    second = np.concatenate([cos_p, sin_p], 0)
    up_u = np.block([[cos_c.T, -sin_c.T], [sin_c.T, cos_c.T]])
    up_v = np.block([[cos_c, sin_c], [-sin_c, cos_c]])
    places = (HALO + np.arange(TILE)) / PAD
    orders = np.arange(1, BAND)
    shift = places[:, None] - np.arange(GRID)[None, :] / GRID
    fine = (1.0 + 2.0 * np.cos(2 * np.pi * shift[..., None] * orders).sum(-1)) / GRID
    out_v = np.block([[cos_i, -sin_i], [-sin_i, -cos_i]])
    out_u = np.concatenate([cos_i.T, -sin_i.T], 1)
    high = fine.astype(jnp.bfloat16)
    low = (fine - high.astype(np.float64)).astype(jnp.bfloat16)
    cast = lambda a: np.ascontiguousarray(a).astype(jnp.bfloat16)
    gain = mean_gain(cos_i, sin_i) / mean_gain(cos_c, sin_c)
    return [
        np.outer(gain, gain).astype(np.float32), cast(first), cast(second), cast(up_u), cast(up_u.T), cast(up_v), cast(up_v.T),
        high, low, cast(fine.T), cast(low.T), cast(out_v), cast(out_u),
    ]


def dot(a, b):
    return jnp.dot(a, b, preferred_element_type=F32)


def half_lanes():
    return lax.broadcasted_iota(jnp.int32, (8, 128), 1) < 64


def turned(groups, turn_a, turn_b):
    lane = lax.broadcasted_iota(jnp.int32, (8, 128), 1)
    sub = lax.broadcasted_iota(jnp.int32, (8, 128), 0)
    left = half_lanes()
    flip_cols = jnp.where(left, turn_a, turn_b) >= 2
    lanes = jnp.where(flip_cols, jnp.where(left, 63, 191) - lane, lane)
    flip_rows = jnp.where(left, lax.rem(turn_a, 2), lax.rem(turn_b, 2)) == 1
    subs = jnp.where(flip_rows, 7 - sub, sub)
    return [
        jnp.take_along_axis(jnp.take_along_axis(g, subs, axis=0), lanes, axis=1) for g in groups
    ]


def places(loc, turn, right):
    flip = lax.rem(turn, 2)
    upper = (1 - flip) if right else flip
    rows = [pl.ds(pl.multiple_of(8 * i + flip * (8 * (3 - 2 * i)), 8), 8) for i in range(4)]
    return loc + 256 * upper, loc + 256 * (1 - upper), rows


def pair_image(cells, loc_a, turn_a, loc_b, turn_b):
    left = half_lanes()
    top_a, low_a, rows_a = places(loc_a, turn_a, False)
    top_b, low_b, rows_b = places(loc_b, turn_b, True)
    groups = [
        jnp.where(left, cells[a, rows_a[i], :], cells[b, rows_b[i], :])
        for a, b in ((top_a, top_b), (low_a, low_b))
        for i in range(4)
    ]
    return jnp.concatenate(turned(groups, turn_a, turn_b), axis=0)


def fill_cells(parts, cells):
    for n, part in enumerate(parts):
        value = part[...].astype(F32)
        cells[pl.ds(32 * n, 32)] = value
        cells[pl.ds(256 + 32 * n, 32)] = pltpu.roll(value.reshape(1024, 128), 64, 1).reshape(32, 32, 128)


def main_kernel(*refs):
    codes, weights = refs[0:2]
    parts = refs[2:10]
    near_strip, far_strip, before, after = refs[10:14]
    free_in, target_in = refs[14:16]
    table_in = refs[16:30]
    resist_out, free_out, own_out, other_out = refs[30:34]
    cells, mask, shading, fields, amps, halves, sums, free, target = refs[34:43]
    tables = refs[43:57]
    free_sems, table_sems, target_sem, resist_sems, out_sems = refs[57:62]
    (spectra, gain, first, second, up_u, up_ut, up_v, up_vt, fine, fine_lo, fine_t, fine_tlo, out_v, out_u) = tables

    loads = [
        pltpu.make_async_copy(free_in.at[pl.ds(256 * n, 256)], free.at[pl.ds(256 * n, 256)], free_sems.at[n])
        for n in range(4)
    ]
    for load in loads:
        load.start()
    table_loads = [pltpu.make_async_copy(a, b, table_sems.at[n]) for n, (a, b) in enumerate(zip(table_in, tables))]
    for load in table_loads:
        load.start()
    target_load = pltpu.make_async_copy(target_in, target, target_sem.at[0])
    target_load.start()

    def code(a, b):
        return codes[a * 18 + b], codes[324 + a * 18 + b]

    fill_cells(parts, cells)
    core = codes[652]
    for a, flag, own_core in ((0, 648, 1), (17, 649, 0)):
        for p in range(8):
            cols = slice(p * 128, p * 128 + 128)
            image = pair_image(cells, *code(a, 2 * p + 1), *code(a, 2 * p + 2))
            strip = jnp.where(core == own_core, near_strip[0:64, cols].astype(F32), far_strip[0:64, cols].astype(F32))
            value = jnp.where(codes[flag] > 0, jnp.tanh(image + strip), 0.0)
            mask[a * 64 : a * 64 + 64, cols] = value.astype(BF16)

    def edge_cell(a):
        rows = pl.ds(pl.multiple_of(a * 64, 64), 64)
        image = pair_image(cells, *code(a, 0), *code(a, 17))
        strips = jnp.concatenate([before[rows, :], after[rows, :]], axis=1)
        value = jnp.tanh(image + strips.astype(F32))
        lane = lax.broadcasted_iota(jnp.int32, (64, 128), 1)
        at_row = jnp.where(a == 0, codes[648], jnp.where(a == 17, codes[649], 1))
        keep = jnp.where(lane < 64, codes[650], codes[651]) * at_row
        mask[rows, 1024:1152] = jnp.where(keep > 0, value, 0.0).astype(BF16)

    def edge_cols(n, _):
        for u in range(6):
            edge_cell(n * 6 + u)
        return 0

    lax.fori_loop(0, 3, edge_cols, 0)

    def interior(a, _):
        rows = pl.ds(pl.multiple_of(a * 64, 64), 64)
        rows_m = pl.ds(pl.multiple_of(a * 64 + 64, 64), 64)
        for p in range(8):
            cols = slice(p * 128, p * 128 + 128)
            image = pair_image(cells, *code(a + 1, 2 * p + 1), *code(a + 1, 2 * p + 2))
            value = jnp.tanh(image + free[rows, cols])
            shading[rows, cols] = value
            mask[rows_m, cols] = value.astype(BF16)
        return 0

    for n in range(4):
        loads[n].wait()
        lax.fori_loop(4 * n, 4 * n + 4, interior, 0)
    for load in table_loads:
        load.wait()
    target_load.wait()

    def tile(t, _):
        i, j = t // 2, t % 2
        rows_w = pl.ds(pl.multiple_of(i * TILE, 128), PAD)
        window = jnp.concatenate(
            [mask[rows_w, pl.ds(pl.multiple_of(j * 384, 128), 640)], mask[rows_w, 1024:1152]], axis=1
        )
        forw = dot(window, first[j]).astype(BF16)
        spec = dot(second[...], forw)
        scale = gain[...] * (1.0 / PAD)
        spec_re = (spec[:128, :128] + spec[128:, 128:]) * scale
        spec_im = (spec[128:, :128] - spec[:128, 128:]) * scale
        for k in range(NK):
            at = slice(k * 128, k * 128 + 128)
            k_re, k_im = spectra[0, :, at], spectra[1, :, at]
            amps[0:128, at] = (k_re * spec_re - k_im * spec_im).astype(BF16)
            amps[128:256, at] = (k_re * spec_im + k_im * spec_re).astype(BF16)
        halves[...] = dot(up_u[...], amps[...]).astype(BF16)
        intensity = jnp.zeros((GRID, GRID), F32)
        for k in range(NK):
            at = slice(k * 128, k * 128 + 128)
            left = jnp.concatenate([halves[0:256, at], halves[256:512, at]], axis=1)
            field = dot(left, up_v[...]) * (1.0 / BAND)
            fields[k] = field
            re, im = field[:, :256], field[:, 256:]
            intensity = intensity + weights[k] * (re * re + im * im)
        coarse = intensity.astype(BF16)
        half_fine = dot(fine[...], coarse) + dot(fine_lo[...], coarse)
        half_fine = half_fine.astype(BF16)
        image = dot(half_fine, fine_t[...]) + dot(half_fine, fine_tlo[...])
        rows_t = pl.ds(pl.multiple_of(i * TILE, TILE), TILE)
        cols_t = pl.ds(pl.multiple_of(j * TILE, TILE), TILE)
        resist = jax.nn.sigmoid(2.0 * (image - 1.8))
        slopes = (4.0 * (resist - target[rows_t, cols_t]) * resist * (1.0 - resist)).astype(BF16)
        target[rows_t, cols_t] = resist
        pltpu.make_async_copy(
            target.at[rows_t, cols_t], resist_out.at[rows_t, cols_t], resist_sems.at[t]
        ).start()
        back = dot(fine_t[...], dot(slopes, fine[...]).astype(BF16))
        for k in range(NK):
            at = slice(k * 128, k * 128 + 128)
            scaled = back * (weights[k] * (2.0 / BAND))
            both = jnp.concatenate(
                [(scaled * fields[k, :, :256]).astype(BF16), (scaled * fields[k, :, 256:]).astype(BF16)], axis=1
            )
            low = dot(both, up_vt[...]).astype(BF16)
            halves[0:256, at] = low[:, :128]
            halves[256:512, at] = low[:, 128:]
        bspec_re = jnp.zeros((128, 128), F32)
        bspec_im = jnp.zeros((128, 128), F32)
        bamp = dot(up_ut[...], halves[...])
        for k in range(NK):
            at = slice(k * 128, k * 128 + 128)
            k_re, k_im = spectra[0, :, at], spectra[1, :, at]
            re, im = bamp[:128, at], bamp[128:, at]
            bspec_re = bspec_re + (k_re * re + k_im * im)
            bspec_im = bspec_im + (k_re * im - k_im * re)
        bspec = jnp.concatenate([bspec_re * scale, bspec_im * scale], axis=1)
        bforw = dot(bspec.astype(BF16), out_v[...]).astype(BF16)
        stacked = jnp.concatenate([bforw[:, :TILE], bforw[:, TILE:]], axis=0)
        gradient = dot(out_u[...], stacked)
        shade = shading[rows_t, cols_t]
        grad = gradient * (1.0 - shade * shade)
        shading[rows_t, cols_t] = grad
        free[rows_t, cols_t] = free[rows_t, cols_t] - grad
        pltpu.make_async_copy(free.at[rows_t, cols_t], free_out.at[rows_t, cols_t], out_sems.at[t]).start()
        return 0

    lax.fori_loop(0, 4, tile, 0)

    def clear(n, _):
        sums[pl.ds(n * 8, 8)] = jnp.zeros((8, 32, 128), F32)
        return 0

    lax.fori_loop(0, 64, clear, 0)

    def collect(a, _):
        rows = pl.multiple_of(a * 64, 64)
        left = half_lanes()
        for p in range(8):
            cols = slice(p * 128, p * 128 + 128)
            loc_a, turn_a = code(a + 1, 2 * p + 1)
            loc_b, turn_b = code(a + 1, 2 * p + 2)
            groups = turned([shading[pl.ds(rows + 8 * i, 8), cols] for i in range(8)], turn_a, turn_b)
            for loc, turn, right, keep in ((loc_a, turn_a, False, left), (loc_b, turn_b, True, ~left)):
                top, low, at = places(loc, turn, right)
                for i in range(4):
                    sums[top, at[i], :] = sums[top, at[i], :] + jnp.where(keep, groups[i], 0.0)
                    sums[low, at[i], :] = sums[low, at[i], :] + jnp.where(keep, groups[4 + i], 0.0)
        return 0

    lax.fori_loop(0, 16, collect, 0)
    for out, base in ((own_out, 0), (other_out, 128)):

        def join(n, _):
            at = pl.ds(base + n * 8, 8)
            rolled = pltpu.roll(sums[pl.ds(256 + base + n * 8, 8)].reshape(256, 128), 64, 1)
            out[pl.ds(n * 8, 8)] = (sums[at].reshape(256, 128) + rolled).reshape(8, 32, 128).astype(BF16)
            return 0

        lax.fori_loop(0, 16, join, 0)

    for t in range(4):
        at = (pl.ds(t // 2 * TILE, TILE), pl.ds(t % 2 * TILE, TILE))
        pltpu.make_async_copy(target.at[at], resist_out.at[at], resist_sems.at[t]).wait()
        pltpu.make_async_copy(free.at[at], free_out.at[at], out_sems.at[t]).wait()


def final_kernel(*refs):
    codes = refs[0]
    parts = refs[1:9]
    free, out, cells = refs[9:12]
    step = pl.program_id(0)

    @pl.when(step == 0)
    def _():
        fill_cells(parts, cells)

    def interior(r, _):
        rows = pl.ds(pl.multiple_of(r * 64, 64), 64)
        for p in range(8):
            cols = slice(p * 128, p * 128 + 128)
            at = (step * 2 + r + 1) * 18 + 2 * p
            image = pair_image(cells, codes[at + 1], codes[325 + at], codes[at + 2], codes[326 + at])
            out[rows, cols] = jnp.tanh(image + free[rows, cols])
        return 0

    lax.fori_loop(0, 2, interior, 0)


def flat(x, c, y, z):
    return ((x % 4) * 2 + c) * 16 + (y % 4) * 4 + z % 4


CHIPS = [(x, y, z) for x in range(4) for y in range(4) for z in range(4)]


def shift_first(d):
    return [(flat(x, 0, y, z), flat(x, 0, y, z + d)) for x, y, z in CHIPS] + [
        (flat(x, 1, y, z), flat(x, 1, y + d, z)) for x, y, z in CHIPS
    ]


def shift_second(d):
    return [(flat(x, 0, y, z), flat(x, 0, y + d, z)) for x, y, z in CHIPS] + [
        (flat(x, 1, y, z), flat(x, 1, y, z + d)) for x, y, z in CHIPS
    ]


def shift_x(d):
    return [(flat(x, c, y, z), flat(x + d, c, y, z)) for x, y, z in CHIPS for c in range(2)]


SWAP = [(flat(x, c, y, z), flat(x, 1 - c, y, z)) for x, y, z in CHIPS for c in range(2)]


OVER = [(flat(x, 0, y, z), flat(x - 1, 1, y, z)) for x, y, z in CHIPS if x > 0] + [
    (flat(x, 1, y, z), flat(x + 1, 0, y, z)) for x, y, z in CHIPS if x < 3
]


def send(value, pairs):
    return lax.ppermute(value, BOTH, pairs)


def gathered_near(piece):
    got = {d: send(piece, shift_first(d)) for d in (2, 1, 3)}
    return jnp.concatenate([piece, got[1], got[2], got[3]], axis=0)


def gathered_far(group):
    far = {d: send(group, shift_second(d)) for d in (2, 1, 3)}
    mine = [group, far[1], far[2], far[3]]
    return mine + [send(part, SWAP) for part in mine]


def scattered_sum(own, other):
    total = (own.astype(F32) + send(other, SWAP).astype(F32)).astype(BF16).reshape(4, 32, 32, 128)
    got = [send(total[d], shift_second(-d)) for d in (2, 1, 3)]
    total = sum((g.astype(F32) for g in got), total[0].astype(F32)).astype(BF16).reshape(4, 8, 32, 128)
    got = [send(total[d], shift_first(-d)) for d in (2, 1, 3)]
    total = sum((g.astype(F32) for g in got), total[0].astype(F32)).astype(BF16)
    got = [send(total, shift_x(d)) for d in (2, 1, 3)]
    return sum((g.astype(F32) for g in got), total.astype(F32))


def to_wire(rows):
    cells = rows.reshape(-1, CELL, CELL)
    return jnp.concatenate([cells[:, :32, :], cells[:, 32:, :]], axis=2)


def from_wire(wire):
    return jnp.concatenate([wire[:, :, :64], wire[:, :, 64:]], axis=1)


def smooth(grids):
    framed = jnp.pad(grids, ((0, 0), (1, 1), (1, 1)))
    beside = framed[:, 2:, 1:-1] + framed[:, :-2, 1:-1] + framed[:, 1:-1, 2:] + framed[:, 1:-1, :-2]
    return 0.5 * grids + 0.125 * beside


def steps(axis):
    n = lax.axis_size(axis)
    up = [(i, i + 1) for i in range(n - 1)]
    return up, [(b, a) for a, b in up]


def per_device(masters, inst_master, inst_orient, owner_map, tile_free, target, spectra, weights):
    row, col = lax.axis_index("row"), lax.axis_index("col")
    core, y, z = row % 2, col // 4, col % 4
    own_cells = lax.dynamic_slice_in_dim(masters, core * 8, 8, 0)
    group = gathered_near(to_wire(own_cells.astype(BF16)))

    def codes_of(a):
        return jnp.pad(a.astype(BF16), ((0, 0), (0, SIDE - a.shape[1])))

    def strip(at, line):
        pad = jnp.concatenate([codes_of(inst_master[line : line + 1]), codes_of(inst_orient[line : line + 1])], 0)
        return jnp.concatenate([tile_free[at : at + 64].astype(BF16), jnp.pad(pad, ((0, 14), (0, 0)))], 0)

    top, bottom = strip(0, 0), strip(SIDE - 64, 15)
    for_near, for_far = jnp.where(core == 0, bottom, top), jnp.where(core == 0, top, bottom)
    group, for_near, for_far = lax.optimization_barrier((group, for_near, for_far))
    parts = gathered_far(group)
    near_strip, far_strip = send(for_near, SWAP), send(for_far, OVER)

    def ints(a):
        return a.astype(F32).astype(jnp.int32)

    def above_below(at):
        near, far = near_strip[at], far_strip[at]
        return jnp.where(core == 0, far, near), jnp.where(core == 0, near, far)

    above, below = above_below((slice(64, 66), slice(0, 16)))
    tall_master = jnp.concatenate([ints(above[0:1]), inst_master, ints(below[0:1])], 0)
    tall_orient = jnp.concatenate([ints(above[1:2]), inst_orient, ints(below[1:2])], 0)

    def side(at, line):
        over, under = above_below((slice(0, 64), slice(at, at + 64)))
        pixels = jnp.concatenate([over, tile_free[:, at : at + 64].astype(BF16), under], 0)
        lines = jnp.stack([tall_master[:, line], tall_orient[:, line]], 1).astype(BF16)
        return jnp.concatenate([pixels, jnp.pad(lines, ((0, 14), (0, 62)))], 0)

    up, down = steps("col")
    before = lax.ppermute(side(SIDE - 64, 15), "col", up)
    after = lax.ppermute(side(0, 0), "col", down)
    all_master = jnp.concatenate([ints(before[1152:1170, 0:1]), tall_master, ints(after[1152:1170, 0:1])], 1)
    all_orient = jnp.concatenate([ints(before[1152:1170, 1:2]), tall_orient, ints(after[1152:1170, 1:2])], 1)

    matches = all_master[..., None] == jnp.arange(owner_map.shape[0], dtype=jnp.int32)
    slots = jnp.sum(jnp.where(matches, owner_map, 0), axis=-1)
    at_y, at_z, half, entry = slots // 64, (slots // 16) % 4, (slots // 8) % 2, slots % 8
    dy, dz = (y - at_y) % 4, (z - at_z) % 4
    far, near = jnp.where(half == 0, dy, dz), jnp.where(half == 0, dz, dy)
    locs = (jnp.where(half == core, 0, 1) * 16 + far * 4 + near) * 8 + entry
    inside = jnp.stack([row > 0, row < 7, col > 0, col < 15]).astype(jnp.int32)
    codes = jnp.concatenate([locs.reshape(-1), all_orient.reshape(-1), inside, core.reshape(1).astype(jnp.int32)])

    vmem, smem = pl.BlockSpec(memory_space=pltpu.VMEM), pl.BlockSpec(memory_space=pltpu.SMEM)
    anywhere = pl.BlockSpec(memory_space=pl.ANY)
    wide = jax.ShapeDtypeStruct((SIDE, SIDE), F32)
    sums_shape = jax.ShapeDtypeStruct((128, 32, 128), BF16)
    tables = [spectra.reshape(2, BAND, NK * BAND), *constant_tables()]
    resist, free_new, own, other = pl.pallas_call(
        main_kernel,
        out_shape=(wide, wide, sums_shape, sums_shape),
        in_specs=[smem] * 2 + [vmem] * 12 + [anywhere] * (2 + len(tables)),
        out_specs=(anywhere, anywhere, vmem, vmem),
        scratch_shapes=[
            pltpu.VMEM((512, 32, 128), F32),
            pltpu.VMEM((1152, 1152), BF16),
            pltpu.VMEM((SIDE, SIDE), F32),
            pltpu.VMEM((NK, GRID, 2 * GRID), F32),
            pltpu.VMEM((256, 1024), BF16),
            pltpu.VMEM((512, 1024), BF16),
            pltpu.VMEM((512, 32, 128), F32),
            pltpu.VMEM((SIDE, SIDE), F32),
            pltpu.VMEM((SIDE, SIDE), F32),
            *(pltpu.VMEM(t.shape, t.dtype) for t in tables),
            pltpu.SemaphoreType.DMA((4,)),
            pltpu.SemaphoreType.DMA((len(tables),)),
            pltpu.SemaphoreType.DMA((1,)),
            pltpu.SemaphoreType.DMA((4,)),
            pltpu.SemaphoreType.DMA((4,)),
        ],
        compiler_params=pltpu.CompilerParams(vmem_limit_bytes=60 * 1024 * 1024),
        name="image_and_gradient",
    )(codes, weights, *parts, near_strip, far_strip, before, after, tile_free, target, *tables)

    summed = scattered_sum(own, other)
    fresh = smooth(own_cells.reshape(8, CELL, CELL) - 0.05 * from_wire(summed))
    fresh_wire = jnp.concatenate([fresh[:, :32, :], fresh[:, 32:, :]], axis=2).astype(BF16)
    parts = gathered_far(gathered_near(fresh_wire))
    new_mask = pl.pallas_call(
        final_kernel,
        out_shape=wide,
        grid=(8,),
        in_specs=[smem] + [vmem] * 8 + [pl.BlockSpec((128, SIDE), lambda s: (s, 0))],
        out_specs=pl.BlockSpec((128, SIDE), lambda s: (s, 0)),
        scratch_shapes=[pltpu.VMEM((512, 32, 128), F32)],
        compiler_params=pltpu.CompilerParams(vmem_limit_bytes=58 * 1024 * 1024),
        name="final_mask",
    )(codes, *parts, free_new)
    mine = from_wire(parts[0][:8]).reshape(8, CELL * CELL).astype(F32)
    others = from_wire(parts[4][:8]).reshape(8, CELL * CELL).astype(F32)
    masters_out = jnp.where(core == 0, jnp.concatenate([mine, others], 0), jnp.concatenate([others, mine], 0))
    return resist, new_mask, masters_out


def solution(mesh):
    placed = (P("col", None), P(*BOTH), P(*BOTH), P(), P(*BOTH), P(*BOTH), P(), P())
    return jax.shard_map(
        per_device,
        mesh=mesh,
        in_specs=placed,
        out_specs=(P(*BOTH), P(*BOTH), P("col", None)),
        check_vma=False,
    )
```

```python
import functools

import jax
import jax.numpy as jnp
import numpy as np
from jax import lax
from jax.experimental import pallas as pl
from jax.experimental.pallas import tpu as pltpu
from jax.sharding import PartitionSpec as P

TILE, HALO, CELL, BAND, NK, PAD = 512, 64, 64, 128, 8, 640
GRID = 256
SIDE = 1024
BOTH = ("row", "col")
F32, BF16 = jnp.float32, jnp.bfloat16


def waves(positions, period):
    freqs = np.arange(BAND) - BAND // 2
    angles = 2.0 * np.pi * ((freqs[:, None] * positions[None, :]) % period) / period
    return np.cos(angles), np.sin(angles)


def mean_gain(cos, sin):
    rounded = [t.astype(jnp.bfloat16).astype(np.float64) for t in (cos, sin)]
    return (rounded[0] * cos + rounded[1] * sin).mean(1)


@functools.cache
def constant_tables():
    cos_c, sin_c = waves(np.arange(GRID), GRID)
    cos_p, sin_p = waves(np.arange(PAD), PAD)
    cos_i, sin_i = cos_p[:, HALO : HALO + TILE], sin_p[:, HALO : HALO + TILE]
    by_pixel = np.concatenate([cos_p.T, sin_p.T], 1)
    first = np.zeros((2, 768, 256))
    first[0, 0:576] = by_pixel[64:640]
    first[0, 640:704] = by_pixel[0:64]
    first[1, 64:640] = by_pixel[0:576]
    first[1, 704:768] = by_pixel[576:640]
    second = np.concatenate([cos_p, sin_p], 0)
    up_u = np.block([[cos_c.T, -sin_c.T], [sin_c.T, cos_c.T]])
    up_v = np.block([[cos_c, sin_c], [-sin_c, cos_c]])
    places = (HALO + np.arange(TILE)) / PAD
    orders = np.arange(1, BAND)
    shift = places[:, None] - np.arange(GRID)[None, :] / GRID
    fine = (1.0 + 2.0 * np.cos(2 * np.pi * shift[..., None] * orders).sum(-1)) / GRID
    out_v = np.block([[cos_i, -sin_i], [-sin_i, -cos_i]])
    out_u = np.concatenate([cos_i.T, -sin_i.T], 1)
    high = fine.astype(jnp.bfloat16)
    low = (fine - high.astype(np.float64)).astype(jnp.bfloat16)
    cast = lambda a: np.ascontiguousarray(a).astype(jnp.bfloat16)
    gain = mean_gain(cos_i, sin_i) / mean_gain(cos_c, sin_c)
    return [
        np.outer(gain, gain).astype(np.float32), cast(first), cast(second), cast(up_u), cast(up_u.T), cast(up_v), cast(up_v.T),
        high, low, cast(fine.T), cast(low.T), cast(out_v), cast(out_u),
    ]


def dot(a, b):
    return jnp.dot(a, b, preferred_element_type=F32)


def half_lanes():
    return lax.broadcasted_iota(jnp.int32, (8, 128), 1) < 64


def turned(groups, turn_a, turn_b):
    lane = lax.broadcasted_iota(jnp.int32, (8, 128), 1)
    sub = lax.broadcasted_iota(jnp.int32, (8, 128), 0)
    left = half_lanes()
    flip_cols = jnp.where(left, turn_a, turn_b) >= 2
    lanes = jnp.where(flip_cols, jnp.where(left, 63, 191) - lane, lane)
    flip_rows = jnp.where(left, lax.rem(turn_a, 2), lax.rem(turn_b, 2)) == 1
    subs = jnp.where(flip_rows, 7 - sub, sub)
    return [
        jnp.take_along_axis(jnp.take_along_axis(g, subs, axis=0), lanes, axis=1) for g in groups
    ]


def places(loc, turn, right):
    flip = lax.rem(turn, 2)
    upper = (1 - flip) if right else flip
    rows = [pl.ds(pl.multiple_of(8 * i + flip * (8 * (3 - 2 * i)), 8), 8) for i in range(4)]
    return loc + 256 * upper, loc + 256 * (1 - upper), rows


def pair_image(cells, loc_a, turn_a, loc_b, turn_b):
    left = half_lanes()
    top_a, low_a, rows_a = places(loc_a, turn_a, False)
    top_b, low_b, rows_b = places(loc_b, turn_b, True)
    groups = [
        jnp.where(left, cells[a, rows_a[i], :], cells[b, rows_b[i], :])
        for a, b in ((top_a, top_b), (low_a, low_b))
        for i in range(4)
    ]
    return jnp.concatenate(turned(groups, turn_a, turn_b), axis=0)


def fill_cells(parts, cells, loads):
    for n, part in enumerate(parts):
        loads[n].wait()
        value = part[...].astype(F32)
        cells[pl.ds(32 * n, 32)] = value
        cells[pl.ds(256 + 32 * n, 32)] = pltpu.roll(value.reshape(1024, 128), 64, 1).reshape(32, 32, 128)


def main_kernel(*refs):
    codes, weights = refs[0:2]
    part_in = refs[2:10]
    near_strip, far_strip, before, after = refs[10:14]
    free_in, target_in = refs[14:16]
    table_in = refs[16:30]
    resist_out, free_out, own_out, other_out = refs[30:34]
    cells, mask, shading, fields, amps, halves, sums, free, target = refs[34:43]
    tables = refs[43:57]
    parts = refs[57:65]
    free_sems, table_sems, target_sem, resist_sems, out_sems, part_sems = refs[65:71]
    (spectra, gain, first, second, up_u, up_ut, up_v, up_vt, fine, fine_lo, fine_t, fine_tlo, out_v, out_u) = tables

    part_loads = [pltpu.make_async_copy(a, b, part_sems.at[n]) for n, (a, b) in enumerate(zip(part_in, parts))]
    for load in part_loads:
        load.start()
    loads = [
        pltpu.make_async_copy(free_in.at[pl.ds(256 * n, 256)], free.at[pl.ds(256 * n, 256)], free_sems.at[n])
        for n in range(4)
    ]
    for load in loads:
        load.start()
    table_loads = [pltpu.make_async_copy(a, b, table_sems.at[n]) for n, (a, b) in enumerate(zip(table_in, tables))]
    for load in table_loads:
        load.start()
    target_load = pltpu.make_async_copy(target_in, target, target_sem.at[0])
    target_load.start()

    def code(a, b):
        return codes[a * 18 + b], codes[324 + a * 18 + b]

    fill_cells(parts, cells, part_loads)
    core = codes[652]
    for a, flag, own_core in ((0, 648, 1), (17, 649, 0)):
        for p in range(8):
            cols = slice(p * 128, p * 128 + 128)
            image = pair_image(cells, *code(a, 2 * p + 1), *code(a, 2 * p + 2))
            strip = jnp.where(core == own_core, near_strip[0:64, cols].astype(F32), far_strip[0:64, cols].astype(F32))
            value = jnp.where(codes[flag] > 0, jnp.tanh(image + strip), 0.0)
            mask[a * 64 : a * 64 + 64, cols] = value.astype(BF16)

    def edge_cell(a):
        rows = pl.ds(pl.multiple_of(a * 64, 64), 64)
        image = pair_image(cells, *code(a, 0), *code(a, 17))
        strips = jnp.concatenate([before[rows, :], after[rows, :]], axis=1)
        value = jnp.tanh(image + strips.astype(F32))
        lane = lax.broadcasted_iota(jnp.int32, (64, 128), 1)
        at_row = jnp.where(a == 0, codes[648], jnp.where(a == 17, codes[649], 1))
        keep = jnp.where(lane < 64, codes[650], codes[651]) * at_row
        mask[rows, 1024:1152] = jnp.where(keep > 0, value, 0.0).astype(BF16)

    def edge_cols(n, _):
        for u in range(6):
            edge_cell(n * 6 + u)
        return 0

    lax.fori_loop(0, 3, edge_cols, 0)

    def interior(a, _):
        rows = pl.ds(pl.multiple_of(a * 64, 64), 64)
        rows_m = pl.ds(pl.multiple_of(a * 64 + 64, 64), 64)
        for p in range(8):
            cols = slice(p * 128, p * 128 + 128)
            image = pair_image(cells, *code(a + 1, 2 * p + 1), *code(a + 1, 2 * p + 2))
            value = jnp.tanh(image + free[rows, cols])
            shading[rows, cols] = value
            mask[rows_m, cols] = value.astype(BF16)
        return 0

    for n in range(4):
        loads[n].wait()
        lax.fori_loop(4 * n, 4 * n + 4, interior, 0)
    for load in table_loads:
        load.wait()
    target_load.wait()

    def tile(t, _):
        i, j = t // 2, t % 2
        rows_w = pl.ds(pl.multiple_of(i * TILE, 128), PAD)
        window = jnp.concatenate(
            [mask[rows_w, pl.ds(pl.multiple_of(j * 384, 128), 640)], mask[rows_w, 1024:1152]], axis=1
        )
        forw = dot(window, first[j]).astype(BF16)
        spec = dot(second[...], forw)
        scale = gain[...] * (1.0 / PAD)
        spec_re = (spec[:128, :128] + spec[128:, 128:]) * scale
        spec_im = (spec[128:, :128] - spec[:128, 128:]) * scale
        for k in range(NK):
            at = slice(k * 128, k * 128 + 128)
            k_re, k_im = spectra[0, :, at], spectra[1, :, at]
            amps[0:128, at] = (k_re * spec_re - k_im * spec_im).astype(BF16)
            amps[128:256, at] = (k_re * spec_im + k_im * spec_re).astype(BF16)
        halves[...] = dot(up_u[...], amps[...]).astype(BF16)
        intensity = jnp.zeros((GRID, GRID), F32)
        for k in range(NK):
            at = slice(k * 128, k * 128 + 128)
            left = jnp.concatenate([halves[0:256, at], halves[256:512, at]], axis=1)
            field = dot(left, up_v[...]) * (1.0 / BAND)
            fields[k] = field
            re, im = field[:, :256], field[:, 256:]
            intensity = intensity + weights[k] * (re * re + im * im)
        coarse = intensity.astype(BF16)
        half_fine = dot(fine[...], coarse) + dot(fine_lo[...], coarse)
        half_fine = half_fine.astype(BF16)
        image = dot(half_fine, fine_t[...]) + dot(half_fine, fine_tlo[...])
        rows_t = pl.ds(pl.multiple_of(i * TILE, TILE), TILE)
        cols_t = pl.ds(pl.multiple_of(j * TILE, TILE), TILE)
        resist = jax.nn.sigmoid(2.0 * (image - 1.8))
        slopes = (4.0 * (resist - target[rows_t, cols_t]) * resist * (1.0 - resist)).astype(BF16)
        target[rows_t, cols_t] = resist
        pltpu.make_async_copy(
            target.at[rows_t, cols_t], resist_out.at[rows_t, cols_t], resist_sems.at[t]
        ).start()
        back = dot(fine_t[...], dot(slopes, fine[...]).astype(BF16))
        for k in range(NK):
            at = slice(k * 128, k * 128 + 128)
            scaled = back * (weights[k] * (2.0 / BAND))
            both = jnp.concatenate(
                [(scaled * fields[k, :, :256]).astype(BF16), (scaled * fields[k, :, 256:]).astype(BF16)], axis=1
            )
            low = dot(both, up_vt[...]).astype(BF16)
            halves[0:256, at] = low[:, :128]
            halves[256:512, at] = low[:, 128:]
        bspec_re = jnp.zeros((128, 128), F32)
        bspec_im = jnp.zeros((128, 128), F32)
        bamp = dot(up_ut[...], halves[...])
        for k in range(NK):
            at = slice(k * 128, k * 128 + 128)
            k_re, k_im = spectra[0, :, at], spectra[1, :, at]
            re, im = bamp[:128, at], bamp[128:, at]
            bspec_re = bspec_re + (k_re * re + k_im * im)
            bspec_im = bspec_im + (k_re * im - k_im * re)
        bspec = jnp.concatenate([bspec_re * scale, bspec_im * scale], axis=1)
        bforw = dot(bspec.astype(BF16), out_v[...]).astype(BF16)
        stacked = jnp.concatenate([bforw[:, :TILE], bforw[:, TILE:]], axis=0)
        gradient = dot(out_u[...], stacked)
        shade = shading[rows_t, cols_t]
        grad = gradient * (1.0 - shade * shade)
        shading[rows_t, cols_t] = grad
        free[rows_t, cols_t] = free[rows_t, cols_t] - grad
        pltpu.make_async_copy(free.at[rows_t, cols_t], free_out.at[rows_t, cols_t], out_sems.at[t]).start()
        return 0

    lax.fori_loop(0, 4, tile, 0)

    def clear(n, _):
        sums[pl.ds(n * 8, 8)] = jnp.zeros((8, 32, 128), F32)
        return 0

    lax.fori_loop(0, 64, clear, 0)

    def collect(a, _):
        rows = pl.multiple_of(a * 64, 64)
        left = half_lanes()
        for p in range(8):
            cols = slice(p * 128, p * 128 + 128)
            loc_a, turn_a = code(a + 1, 2 * p + 1)
            loc_b, turn_b = code(a + 1, 2 * p + 2)
            groups = turned([shading[pl.ds(rows + 8 * i, 8), cols] for i in range(8)], turn_a, turn_b)
            for loc, turn, right, keep in ((loc_a, turn_a, False, left), (loc_b, turn_b, True, ~left)):
                top, low, at = places(loc, turn, right)
                spots = [(top, at[i]) for i in range(4)] + [(low, at[i]) for i in range(4)]
                totals = [sums[n, r, :] + jnp.where(keep, g, 0.0) for (n, r), g in zip(spots, groups)]
                for (n, r), total in zip(spots, totals):
                    sums[n, r, :] = total
        return 0

    lax.fori_loop(0, 16, collect, 0)
    for out, base in ((own_out, 0), (other_out, 128)):

        def join(n, _):
            at = pl.ds(base + n * 8, 8)
            rolled = pltpu.roll(sums[pl.ds(256 + base + n * 8, 8)].reshape(256, 128), 64, 1)
            out[pl.ds(n * 8, 8)] = (sums[at].reshape(256, 128) + rolled).reshape(8, 32, 128).astype(BF16)
            return 0

        lax.fori_loop(0, 16, join, 0)

    for t in range(4):
        at = (pl.ds(t // 2 * TILE, TILE), pl.ds(t % 2 * TILE, TILE))
        pltpu.make_async_copy(target.at[at], resist_out.at[at], resist_sems.at[t]).wait()
        pltpu.make_async_copy(free.at[at], free_out.at[at], out_sems.at[t]).wait()


def final_kernel(*refs):
    codes = refs[0]
    part_in, (free_in, out), cells, free = refs[1:9], refs[9:11], refs[11], refs[12]
    parts, (part_sems, free_sems, out_sems) = refs[13:21], refs[21:24]
    part_loads = [pltpu.make_async_copy(a, b, part_sems.at[n]) for n, (a, b) in enumerate(zip(part_in, parts))]
    strips = [pl.ds(128 * n, 128) for n in range(8)]
    loads = [pltpu.make_async_copy(free_in.at[r], free.at[r], free_sems.at[n]) for n, r in enumerate(strips)]
    stores = [pltpu.make_async_copy(free.at[r], out.at[r], out_sems.at[n]) for n, r in enumerate(strips)]
    for load in part_loads + loads:
        load.start()
    fill_cells(parts, cells, part_loads)

    def interior(a, _):
        rows = pl.ds(pl.multiple_of(a * 64, 64), 64)
        for p in range(8):
            cols = slice(p * 128, p * 128 + 128)
            at = (a + 1) * 18 + 2 * p
            image = pair_image(cells, codes[at + 1], codes[325 + at], codes[at + 2], codes[326 + at])
            free[rows, cols] = jnp.tanh(image + free[rows, cols])
        return 0

    for n in range(8):
        loads[n].wait()
        lax.fori_loop(2 * n, 2 * n + 2, interior, 0)
        stores[n].start()
    for store in stores:
        store.wait()


def flat(x, c, y, z):
    return ((x % 4) * 2 + c) * 16 + (y % 4) * 4 + z % 4


CHIPS = [(x, y, z) for x in range(4) for y in range(4) for z in range(4)]


def shift_first(d):
    return [(flat(x, 0, y, z), flat(x, 0, y, z + d)) for x, y, z in CHIPS] + [
        (flat(x, 1, y, z), flat(x, 1, y + d, z)) for x, y, z in CHIPS
    ]


def shift_second(d):
    return [(flat(x, 0, y, z), flat(x, 0, y + d, z)) for x, y, z in CHIPS] + [
        (flat(x, 1, y, z), flat(x, 1, y, z + d)) for x, y, z in CHIPS
    ]


def shift_x(d):
    return [(flat(x, c, y, z), flat(x + d, c, y, z)) for x, y, z in CHIPS for c in range(2)]


SWAP = [(flat(x, c, y, z), flat(x, 1 - c, y, z)) for x, y, z in CHIPS for c in range(2)]


OVER = [(flat(x, 0, y, z), flat(x - 1, 1, y, z)) for x, y, z in CHIPS if x > 0] + [
    (flat(x, 1, y, z), flat(x + 1, 0, y, z)) for x, y, z in CHIPS if x < 3
]


def send(value, pairs):
    return lax.ppermute(value, BOTH, pairs)


def gathered_near(piece):
    got = {d: send(piece, shift_first(d)) for d in (2, 1, 3)}
    return jnp.concatenate([piece, got[1], got[2], got[3]], axis=0)


def gathered_far(group):
    far = {d: send(group, shift_second(d)) for d in (2, 1, 3)}
    mine = [group, far[1], far[2], far[3]]
    return mine + [send(part, SWAP) for part in mine]


def scattered_sum(own, other):
    total = (own.astype(F32) + send(other, SWAP).astype(F32)).astype(BF16).reshape(4, 32, 32, 128)
    got = [send(total[d], shift_second(-d)) for d in (2, 1, 3)]
    total = sum((g.astype(F32) for g in got), total[0].astype(F32)).astype(BF16).reshape(4, 8, 32, 128)
    got = [send(total[d], shift_first(-d)) for d in (2, 1, 3)]
    total = sum((g.astype(F32) for g in got), total[0].astype(F32)).astype(BF16)
    got = [send(total, shift_x(d)) for d in (2, 1, 3)]
    return sum((g.astype(F32) for g in got), total.astype(F32))


def to_wire(rows):
    cells = rows.reshape(-1, CELL, CELL)
    return jnp.concatenate([cells[:, :32, :], cells[:, 32:, :]], axis=2)


def from_wire(wire):
    return jnp.concatenate([wire[:, :, :64], wire[:, :, 64:]], axis=1)


def smooth(grids):
    framed = jnp.pad(grids, ((0, 0), (1, 1), (1, 1)))
    beside = framed[:, 2:, 1:-1] + framed[:, :-2, 1:-1] + framed[:, 1:-1, 2:] + framed[:, 1:-1, :-2]
    return 0.5 * grids + 0.125 * beside


def steps(axis):
    n = lax.axis_size(axis)
    up = [(i, i + 1) for i in range(n - 1)]
    return up, [(b, a) for a, b in up]


def per_device(masters, inst_master, inst_orient, owner_map, tile_free, target, spectra, weights):
    row, col = lax.axis_index("row"), lax.axis_index("col")
    core, y, z = row % 2, col // 4, col % 4
    own_cells = lax.dynamic_slice_in_dim(masters, core * 8, 8, 0)
    group = gathered_near(to_wire(own_cells.astype(BF16)))

    def codes_of(a):
        return jnp.pad(a.astype(BF16), ((0, 0), (0, SIDE - a.shape[1])))

    def strip(at, line):
        pad = jnp.concatenate([codes_of(inst_master[line : line + 1]), codes_of(inst_orient[line : line + 1])], 0)
        return jnp.concatenate([edges[at].astype(BF16), jnp.pad(pad, ((0, 14), (0, 0)))], 0)

    edges = lax.optimization_barrier(
        (tile_free[:64], tile_free[SIDE - 64 :], tile_free[:, :64], tile_free[:, SIDE - 64 :])
    )
    top, bottom = strip(0, 0), strip(1, 15)
    for_near, for_far = jnp.where(core == 0, bottom, top), jnp.where(core == 0, top, bottom)
    near_strip, far_strip = send(for_near, SWAP), send(for_far, OVER)
    parts = gathered_far(group)
    _, near_strip, far_strip = lax.optimization_barrier((group, near_strip, far_strip))

    def ints(a):
        return a.astype(F32).astype(jnp.int32)

    def above_below(at):
        near, far = near_strip[at], far_strip[at]
        return jnp.where(core == 0, far, near), jnp.where(core == 0, near, far)

    above, below = above_below((slice(64, 66), slice(0, 16)))
    tall_master = jnp.concatenate([ints(above[0:1]), inst_master, ints(below[0:1])], 0)
    tall_orient = jnp.concatenate([ints(above[1:2]), inst_orient, ints(below[1:2])], 0)

    def side(at, line):
        over, under = above_below((slice(0, 64), slice(at, at + 64)))
        pixels = jnp.concatenate([over, edges[2 if at == 0 else 3].astype(BF16), under], 0)
        lines = jnp.stack([tall_master[:, line], tall_orient[:, line]], 1).astype(BF16)
        return jnp.concatenate([pixels, jnp.pad(lines, ((0, 14), (0, 62)))], 0)

    up, down = steps("col")
    before = lax.ppermute(side(SIDE - 64, 15), "col", up)
    after = lax.ppermute(side(0, 0), "col", down)
    all_master = jnp.concatenate([ints(before[1152:1170, 0:1]), tall_master, ints(after[1152:1170, 0:1])], 1)
    all_orient = jnp.concatenate([ints(before[1152:1170, 1:2]), tall_orient, ints(after[1152:1170, 1:2])], 1)

    matches = all_master[..., None] == jnp.arange(owner_map.shape[0], dtype=jnp.int32)
    slots = jnp.sum(jnp.where(matches, owner_map, 0), axis=-1)
    at_y, at_z, half, entry = slots // 64, (slots // 16) % 4, (slots // 8) % 2, slots % 8
    dy, dz = (y - at_y) % 4, (z - at_z) % 4
    far, near = jnp.where(half == 0, dy, dz), jnp.where(half == 0, dz, dy)
    locs = (jnp.where(half == core, 0, 1) * 16 + far * 4 + near) * 8 + entry
    inside = jnp.stack([row > 0, row < 7, col > 0, col < 15]).astype(jnp.int32)
    codes = jnp.concatenate([locs.reshape(-1), all_orient.reshape(-1), inside, core.reshape(1).astype(jnp.int32)])

    vmem, smem = pl.BlockSpec(memory_space=pltpu.VMEM), pl.BlockSpec(memory_space=pltpu.SMEM)
    anywhere = pl.BlockSpec(memory_space=pl.ANY)
    wide = jax.ShapeDtypeStruct((SIDE, SIDE), F32)
    sums_shape = jax.ShapeDtypeStruct((128, 32, 128), BF16)
    tables = [spectra.reshape(2, BAND, NK * BAND), *constant_tables()]
    resist, free_new, own, other = pl.pallas_call(
        main_kernel,
        out_shape=(wide, wide, sums_shape, sums_shape),
        in_specs=[smem] * 2 + [anywhere] * 8 + [vmem] * 4 + [anywhere] * (2 + len(tables)),
        out_specs=(anywhere, anywhere, vmem, vmem),
        scratch_shapes=[
            pltpu.VMEM((512, 32, 128), F32),
            pltpu.VMEM((1152, 1152), BF16),
            pltpu.VMEM((SIDE, SIDE), F32),
            pltpu.VMEM((NK, GRID, 2 * GRID), F32),
            pltpu.VMEM((256, 1024), BF16),
            pltpu.VMEM((512, 1024), BF16),
            pltpu.VMEM((512, 32, 128), F32),
            pltpu.VMEM((SIDE, SIDE), F32),
            pltpu.VMEM((SIDE, SIDE), F32),
            *(pltpu.VMEM(t.shape, t.dtype) for t in tables),
            *[pltpu.VMEM((32, 32, 128), BF16)] * 8,
            pltpu.SemaphoreType.DMA((4,)),
            pltpu.SemaphoreType.DMA((len(tables),)),
            pltpu.SemaphoreType.DMA((1,)),
            pltpu.SemaphoreType.DMA((4,)),
            pltpu.SemaphoreType.DMA((4,)),
            pltpu.SemaphoreType.DMA((8,)),
        ],
        compiler_params=pltpu.CompilerParams(vmem_limit_bytes=52 * 1024 * 1024),
        name="image_and_gradient",
    )(codes, weights, *parts, near_strip, far_strip, before, after, tile_free, target, *tables)

    summed = scattered_sum(own, other)
    fresh = smooth(own_cells.reshape(8, CELL, CELL) - 0.05 * from_wire(summed))
    fresh_wire = jnp.concatenate([fresh[:, :32, :], fresh[:, 32:, :]], axis=2).astype(BF16)
    parts = gathered_far(gathered_near(fresh_wire))
    new_mask = pl.pallas_call(
        final_kernel,
        out_shape=wide,
        in_specs=[smem] + [anywhere] * 9,
        out_specs=anywhere,
        scratch_shapes=[
            pltpu.VMEM((512, 32, 128), F32),
            pltpu.VMEM((SIDE, SIDE), F32),
            *[pltpu.VMEM((32, 32, 128), BF16)] * 8,
            *[pltpu.SemaphoreType.DMA((8,))] * 3,
        ],
        compiler_params=pltpu.CompilerParams(vmem_limit_bytes=52 * 1024 * 1024),
        name="final_mask",
    )(codes, *parts, free_new)
    mine = from_wire(parts[0][:8]).reshape(8, CELL * CELL).astype(F32)
    others = from_wire(parts[4][:8]).reshape(8, CELL * CELL).astype(F32)
    masters_out = jnp.where(core == 0, jnp.concatenate([mine, others], 0), jnp.concatenate([others, mine], 0))
    return resist, new_mask, masters_out


def solution(mesh):
    placed = (P("col", None), P(*BOTH), P(*BOTH), P(), P(*BOTH), P(*BOTH), P(), P())
    return jax.shard_map(
        per_device,
        mesh=mesh,
        in_specs=placed,
        out_specs=(P(*BOTH), P(*BOTH), P("col", None)),
        check_vma=False,
    )
```

```python
import functools

import jax
import jax.numpy as jnp
import numpy as np
from jax import lax
from jax.experimental import pallas as pl
from jax.experimental.pallas import tpu as pltpu
from jax.sharding import PartitionSpec as P

TILE, HALO, CELL, BAND, NK, PAD = 512, 64, 64, 128, 8, 640
GRID = 256
SIDE = 1024
BOTH = ("row", "col")
F32, BF16 = jnp.float32, jnp.bfloat16


def waves(positions, period):
    freqs = np.arange(BAND) - BAND // 2
    angles = 2.0 * np.pi * ((freqs[:, None] * positions[None, :]) % period) / period
    return np.cos(angles), np.sin(angles)


def mean_gain(cos, sin):
    rounded = [t.astype(jnp.bfloat16).astype(np.float64) for t in (cos, sin)]
    return (rounded[0] * cos + rounded[1] * sin).mean(1)


@functools.cache
def constant_tables():
    cos_c, sin_c = waves(np.arange(GRID), GRID)
    cos_p, sin_p = waves(np.arange(PAD), PAD)
    cos_i, sin_i = cos_p[:, HALO : HALO + TILE], sin_p[:, HALO : HALO + TILE]
    by_pixel = np.concatenate([cos_p.T, sin_p.T], 1)
    first = np.zeros((2, 768, 256))
    first[0, 0:576] = by_pixel[64:640]
    first[0, 640:704] = by_pixel[0:64]
    first[1, 64:640] = by_pixel[0:576]
    first[1, 704:768] = by_pixel[576:640]
    second = np.concatenate([cos_p, sin_p], 0)
    up_u = np.block([[cos_c.T, -sin_c.T], [sin_c.T, cos_c.T]])
    up_v = np.block([[cos_c, sin_c], [-sin_c, cos_c]])
    places = (HALO + np.arange(TILE)) / PAD
    orders = np.arange(1, BAND)
    shift = places[:, None] - np.arange(GRID)[None, :] / GRID
    fine = (1.0 + 2.0 * np.cos(2 * np.pi * shift[..., None] * orders).sum(-1)) / GRID
    out_v = np.block([[cos_i, -sin_i], [-sin_i, -cos_i]])
    out_u = np.concatenate([cos_i.T, -sin_i.T], 1)
    high = fine.astype(jnp.bfloat16)
    low = (fine - high.astype(np.float64)).astype(jnp.bfloat16)
    cast = lambda a: np.ascontiguousarray(a).astype(jnp.bfloat16)
    gain = mean_gain(cos_i, sin_i) / mean_gain(cos_c, sin_c)
    return [
        np.outer(gain, gain).astype(np.float32), cast(first), cast(second), cast(up_u), cast(up_u.T), cast(up_v), cast(up_v.T),
        high, low, cast(fine.T), cast(low.T), cast(out_v), cast(out_u),
    ]


def dot(a, b):
    return jnp.dot(a, b, preferred_element_type=F32)


def half_lanes():
    return lax.broadcasted_iota(jnp.int32, (8, 128), 1) < 64


def turned(groups, turn_a, turn_b):
    lane = lax.broadcasted_iota(jnp.int32, (8, 128), 1)
    sub = lax.broadcasted_iota(jnp.int32, (8, 128), 0)
    left = half_lanes()
    flip_cols = jnp.where(left, turn_a, turn_b) >= 2
    lanes = jnp.where(flip_cols, jnp.where(left, 63, 191) - lane, lane)
    flip_rows = jnp.where(left, lax.rem(turn_a, 2), lax.rem(turn_b, 2)) == 1
    subs = jnp.where(flip_rows, 7 - sub, sub)
    return [
        jnp.take_along_axis(jnp.take_along_axis(g, subs, axis=0), lanes, axis=1) for g in groups
    ]


def places(loc, turn, right):
    flip = lax.rem(turn, 2)
    upper = (1 - flip) if right else flip
    rows = [pl.ds(pl.multiple_of(8 * i + flip * (8 * (3 - 2 * i)), 8), 8) for i in range(4)]
    return loc + 256 * upper, loc + 256 * (1 - upper), rows


def pair_image(cells, loc_a, turn_a, loc_b, turn_b):
    left = half_lanes()
    top_a, low_a, rows_a = places(loc_a, turn_a, False)
    top_b, low_b, rows_b = places(loc_b, turn_b, True)
    groups = [
        jnp.where(left, cells[a, rows_a[i], :], cells[b, rows_b[i], :])
        for a, b in ((top_a, top_b), (low_a, low_b))
        for i in range(4)
    ]
    return jnp.concatenate(turned(groups, turn_a, turn_b), axis=0)


def fill_cells(parts, cells, loads):
    for n, part in enumerate(parts):
        loads[n].wait()
        value = part[...].astype(F32)
        cells[pl.ds(32 * n, 32)] = value
        cells[pl.ds(256 + 32 * n, 32)] = pltpu.roll(value.reshape(1024, 128), 64, 1).reshape(32, 32, 128)


def main_kernel(*refs):
    codes, weights = refs[0:2]
    part_in = refs[2:10]
    near_strip, far_strip, before, after = refs[10:14]
    free_in, target_in = refs[14:16]
    table_in = refs[16:30]
    resist_out, free_out, own_out, other_out = refs[30:34]
    cells, mask, shading, fields, amps, halves, sums, free, target = refs[34:43]
    tables = refs[43:57]
    parts = refs[57:65]
    free_sems, table_sems, target_sem, resist_sems, out_sems, part_sems = refs[65:71]
    (spectra, gain, first, second, up_u, up_ut, up_v, up_vt, fine, fine_lo, fine_t, fine_tlo, out_v, out_u) = tables

    part_loads = [pltpu.make_async_copy(a, b, part_sems.at[n]) for n, (a, b) in enumerate(zip(part_in, parts))]
    for load in part_loads:
        load.start()
    loads = [
        pltpu.make_async_copy(free_in.at[pl.ds(256 * n, 256)], free.at[pl.ds(256 * n, 256)], free_sems.at[n])
        for n in range(4)
    ]
    for load in loads:
        load.start()
    table_loads = [pltpu.make_async_copy(a, b, table_sems.at[n]) for n, (a, b) in enumerate(zip(table_in, tables))]
    for load in table_loads:
        load.start()
    target_load = pltpu.make_async_copy(target_in, target, target_sem.at[0])
    target_load.start()

    def code(a, b):
        return codes[a * 18 + b], codes[324 + a * 18 + b]

    fill_cells(parts, cells, part_loads)
    core = codes[652]
    def edge_strip(lanes, own_core):
        return jnp.where(core == own_core, near_strip[0:64, lanes].astype(F32), far_strip[0:64, lanes].astype(F32))

    lane_w = lax.broadcasted_iota(jnp.int32, (64, 128), 1)
    inside_cols = jnp.where(lane_w < 64, codes[650], codes[651]) > 0
    for a, flag, own_core in ((0, 648, 1), (17, 649, 0)):
        for p in range(9):
            cols = slice(p * 128, p * 128 + 128)
            ends = (2 * p + 1, 2 * p + 2) if p < 8 else (0, 17)
            image = pair_image(cells, *code(a, ends[0]), *code(a, ends[1]))
            value = jnp.where(codes[flag] > 0, jnp.tanh(image + edge_strip(cols, own_core)), 0.0)
            if p == 8:
                value = jnp.where(inside_cols, value, 0.0)
            mask[a * 64 : a * 64 + 64, cols] = value.astype(BF16)

    def edge_cols(r, _):
        rows = pl.ds(pl.multiple_of(r * 64, 64), 64)
        left, right = before[rows, :].astype(F32), after[rows, :].astype(F32)
        strips = (
            jnp.where(lane_w < 64, left, pltpu.roll(right, 64, 1)),
            jnp.where(lane_w < 64, pltpu.roll(left, 64, 1), right),
        )
        for n in range(2):
            a = r + 8 * n + 1
            image = pair_image(cells, *code(a, 0), *code(a, 17))
            value = jnp.where(inside_cols, jnp.tanh(image + strips[n]), 0.0)
            mask[pl.ds(pl.multiple_of(a * 64, 64), 64), 1024:1152] = value.astype(BF16)
        return 0

    lax.fori_loop(0, 8, edge_cols, 0, unroll=2)

    def interior(a, _):
        rows = pl.ds(pl.multiple_of(a * 64, 64), 64)
        rows_m = pl.ds(pl.multiple_of(a * 64 + 64, 64), 64)
        for p in range(8):
            cols = slice(p * 128, p * 128 + 128)
            image = pair_image(cells, *code(a + 1, 2 * p + 1), *code(a + 1, 2 * p + 2))
            value = jnp.tanh(image + free[rows, cols])
            shading[rows, cols] = value
            mask[rows_m, cols] = value.astype(BF16)
        return 0

    for n in range(4):
        loads[n].wait()
        lax.fori_loop(4 * n, 4 * n + 4, interior, 0)
    for load in table_loads:
        load.wait()
    target_load.wait()

    def tile(t, _):
        i, j = t // 2, t % 2
        rows_w = pl.ds(pl.multiple_of(i * TILE, 128), PAD)
        window = jnp.concatenate(
            [mask[rows_w, pl.ds(pl.multiple_of(j * 384, 128), 640)], mask[rows_w, 1024:1152]], axis=1
        )
        forw = dot(window, first[j]).astype(BF16)
        spec = dot(second[...], forw)
        scale = gain[...] * (1.0 / PAD)
        spec_re = (spec[:128, :128] + spec[128:, 128:]) * scale
        spec_im = (spec[128:, :128] - spec[:128, 128:]) * scale
        for k in range(NK):
            at = slice(k * 128, k * 128 + 128)
            k_re, k_im = spectra[0, :, at], spectra[1, :, at]
            amps[0:128, at] = (k_re * spec_re - k_im * spec_im).astype(BF16)
            amps[128:256, at] = (k_re * spec_im + k_im * spec_re).astype(BF16)
        halves[...] = dot(up_u[...], amps[...]).astype(BF16)
        intensity = jnp.zeros((GRID, GRID), F32)
        for k in range(NK):
            at = slice(k * 128, k * 128 + 128)
            left = jnp.concatenate([halves[0:256, at], halves[256:512, at]], axis=1)
            field = dot(left, up_v[...]) * (1.0 / BAND)
            fields[k] = field
            re, im = field[:, :256], field[:, 256:]
            intensity = intensity + weights[k] * (re * re + im * im)
        coarse = intensity.astype(BF16)
        half_fine = dot(fine[...], coarse) + dot(fine_lo[...], coarse)
        half_fine = half_fine.astype(BF16)
        image = dot(half_fine, fine_t[...]) + dot(half_fine, fine_tlo[...])
        rows_t = pl.ds(pl.multiple_of(i * TILE, TILE), TILE)
        cols_t = pl.ds(pl.multiple_of(j * TILE, TILE), TILE)
        resist = jax.nn.sigmoid(2.0 * (image - 1.8))
        slopes = (4.0 * (resist - target[rows_t, cols_t]) * resist * (1.0 - resist)).astype(BF16)
        target[rows_t, cols_t] = resist
        pltpu.make_async_copy(
            target.at[rows_t, cols_t], resist_out.at[rows_t, cols_t], resist_sems.at[t]
        ).start()
        back = dot(fine_t[...], dot(slopes, fine[...]).astype(BF16))
        for k in range(NK):
            at = slice(k * 128, k * 128 + 128)
            scaled = back * (weights[k] * (2.0 / BAND))
            both = jnp.concatenate(
                [(scaled * fields[k, :, :256]).astype(BF16), (scaled * fields[k, :, 256:]).astype(BF16)], axis=1
            )
            low = dot(both, up_vt[...]).astype(BF16)
            halves[0:256, at] = low[:, :128]
            halves[256:512, at] = low[:, 128:]
        bspec_re = jnp.zeros((128, 128), F32)
        bspec_im = jnp.zeros((128, 128), F32)
        bamp = dot(up_ut[...], halves[...])
        for k in range(NK):
            at = slice(k * 128, k * 128 + 128)
            k_re, k_im = spectra[0, :, at], spectra[1, :, at]
            re, im = bamp[:128, at], bamp[128:, at]
            bspec_re = bspec_re + (k_re * re + k_im * im)
            bspec_im = bspec_im + (k_re * im - k_im * re)
        bspec = jnp.concatenate([bspec_re * scale, bspec_im * scale], axis=1)
        bforw = dot(bspec.astype(BF16), out_v[...]).astype(BF16)
        stacked = jnp.concatenate([bforw[:, :TILE], bforw[:, TILE:]], axis=0)
        gradient = dot(out_u[...], stacked)
        shade = shading[rows_t, cols_t]
        grad = gradient * (1.0 - shade * shade)
        shading[rows_t, cols_t] = grad
        free[rows_t, cols_t] = free[rows_t, cols_t] - grad
        pltpu.make_async_copy(free.at[rows_t, cols_t], free_out.at[rows_t, cols_t], out_sems.at[t]).start()
        return 0

    lax.fori_loop(0, 4, tile, 0)

    def clear(n, _):
        sums[pl.ds(n * 8, 8)] = jnp.zeros((8, 32, 128), F32)
        return 0

    lax.fori_loop(0, 64, clear, 0)

    def collect(a, _):
        rows = pl.multiple_of(a * 64, 64)
        left = half_lanes()
        for p in range(8):
            cols = slice(p * 128, p * 128 + 128)
            loc_a, turn_a = code(a + 1, 2 * p + 1)
            loc_b, turn_b = code(a + 1, 2 * p + 2)
            groups = turned([shading[pl.ds(rows + 8 * i, 8), cols] for i in range(8)], turn_a, turn_b)
            for loc, turn, right, keep in ((loc_a, turn_a, False, left), (loc_b, turn_b, True, ~left)):
                top, low, at = places(loc, turn, right)
                spots = [(top, at[i]) for i in range(4)] + [(low, at[i]) for i in range(4)]
                totals = [sums[n, r, :] + jnp.where(keep, g, 0.0) for (n, r), g in zip(spots, groups)]
                for (n, r), total in zip(spots, totals):
                    sums[n, r, :] = total
        return 0

    lax.fori_loop(0, 16, collect, 0)
    for out, base in ((own_out, 0), (other_out, 128)):

        def join(n, _):
            at = pl.ds(base + n * 8, 8)
            rolled = pltpu.roll(sums[pl.ds(256 + base + n * 8, 8)].reshape(256, 128), 64, 1)
            out[pl.ds(n * 8, 8)] = (sums[at].reshape(256, 128) + rolled).reshape(8, 32, 128).astype(BF16)
            return 0

        lax.fori_loop(0, 16, join, 0)

    for t in range(4):
        at = (pl.ds(t // 2 * TILE, TILE), pl.ds(t % 2 * TILE, TILE))
        pltpu.make_async_copy(target.at[at], resist_out.at[at], resist_sems.at[t]).wait()
        pltpu.make_async_copy(free.at[at], free_out.at[at], out_sems.at[t]).wait()


def final_kernel(*refs):
    codes = refs[0]
    part_in, (free_in, out), cells, free = refs[1:9], refs[9:11], refs[11], refs[12]
    parts, (part_sems, free_sems, out_sems) = refs[13:21], refs[21:24]
    part_loads = [pltpu.make_async_copy(a, b, part_sems.at[n]) for n, (a, b) in enumerate(zip(part_in, parts))]
    strips = [pl.ds(128 * n, 128) for n in range(8)]
    loads = [pltpu.make_async_copy(free_in.at[r], free.at[r], free_sems.at[n]) for n, r in enumerate(strips)]
    stores = [pltpu.make_async_copy(free.at[r], out.at[r], out_sems.at[n]) for n, r in enumerate(strips)]
    for load in part_loads + loads:
        load.start()
    fill_cells(parts, cells, part_loads)

    def interior(a, _):
        rows = pl.ds(pl.multiple_of(a * 64, 64), 64)
        for p in range(8):
            cols = slice(p * 128, p * 128 + 128)
            at = (a + 1) * 18 + 2 * p
            image = pair_image(cells, codes[at + 1], codes[325 + at], codes[at + 2], codes[326 + at])
            free[rows, cols] = jnp.tanh(image + free[rows, cols])
        return 0

    for n in range(8):
        loads[n].wait()
        lax.fori_loop(2 * n, 2 * n + 2, interior, 0)
        stores[n].start()
    for store in stores:
        store.wait()


def flat(x, c, y, z):
    return ((x % 4) * 2 + c) * 16 + (y % 4) * 4 + z % 4


CHIPS = [(x, y, z) for x in range(4) for y in range(4) for z in range(4)]


def mirrored(n, masks):
    return [
        (flat(x, c, y, z), flat(x, c, y ^ (masks[c] * (n % 2)), z ^ (masks[c] * (n // 2))))
        for x, y, z in CHIPS
        for c in range(2)
    ]


def near(n):
    return mirrored(n, (3, 1))


def far(n):
    return mirrored(n, (1, 3))


def shift_x(d):
    return [(flat(x, c, y, z), flat(x + d, c, y, z)) for x, y, z in CHIPS for c in range(2)]


SWAP = [(flat(x, c, y, z), flat(x, 1 - c, y, z)) for x, y, z in CHIPS for c in range(2)]


OVER = [(flat(x, 0, y, z), flat(x - 1, 1, y, z)) for x, y, z in CHIPS if x > 0] + [
    (flat(x, 1, y, z), flat(x + 1, 0, y, z)) for x, y, z in CHIPS if x < 3
]


def send(value, pairs):
    return lax.ppermute(value, BOTH, pairs)


def gathered_near(piece):
    got = [send(piece, near(n)) for n in (3, 1, 2)]
    return jnp.concatenate([piece, got[1], got[2], got[0]], axis=0)


def gathered_far(group):
    got = [send(group, far(n)) for n in (3, 1, 2)]
    mine = [group, got[1], got[2], got[0]]
    return mine + [send(part, SWAP) for part in mine]


def scattered_sum(own, other):
    total = (own.astype(F32) + send(other, SWAP).astype(F32)).astype(BF16).reshape(4, 32, 32, 128)
    got = [send(total[n], far(n)) for n in (3, 1, 2)]
    total = sum((g.astype(F32) for g in got), total[0].astype(F32)).astype(BF16).reshape(4, 8, 32, 128)
    got = [send(total[n], near(n)) for n in (3, 1, 2)]
    total = sum((g.astype(F32) for g in got), total[0].astype(F32)).astype(BF16)
    got = [send(total, shift_x(d)) for d in (2, 1, 3)]
    return sum((g.astype(F32) for g in got), total.astype(F32))


def to_wire(rows):
    cells = rows.reshape(-1, CELL, CELL)
    return jnp.concatenate([cells[:, :32, :], cells[:, 32:, :]], axis=2)


def from_wire(wire):
    return jnp.concatenate([wire[:, :, :64], wire[:, :, 64:]], axis=1)


def smooth(grids):
    framed = jnp.pad(grids, ((0, 0), (1, 1), (1, 1)))
    beside = framed[:, 2:, 1:-1] + framed[:, :-2, 1:-1] + framed[:, 1:-1, 2:] + framed[:, 1:-1, :-2]
    return 0.5 * grids + 0.125 * beside


def steps(axis):
    n = lax.axis_size(axis)
    up = [(i, i + 1) for i in range(n - 1)]
    return up, [(b, a) for a, b in up]


def per_device(masters, inst_master, inst_orient, owner_map, tile_free, target, spectra, weights):
    row, col = lax.axis_index("row"), lax.axis_index("col")
    core, y, z = row % 2, col // 4, col % 4
    own_cells = lax.dynamic_slice_in_dim(masters, core * 8, 8, 0)
    group = gathered_near(to_wire(own_cells.astype(BF16)))

    edges = lax.optimization_barrier(
        (tile_free[:64], tile_free[SIDE - 64 :], tile_free[:, :64], tile_free[:, SIDE - 64 :])
    )
    insts = jnp.stack([inst_master, inst_orient])

    def side(pixels, line):
        packed = jnp.concatenate([pixels[:512], pixels[512:]], 1).astype(BF16)
        lines = jnp.pad(insts[:, :, line].astype(BF16), ((0, 14), (0, 112)))
        return jnp.concatenate([packed, lines], 0)

    up, down = steps("col")
    before = lax.ppermute(side(edges[3], 15), "col", up)
    after = lax.ppermute(side(edges[2], 0), "col", down)

    def ints(a):
        return a.astype(F32).astype(jnp.int32)

    wide_insts = jnp.concatenate(
        [ints(before[512:514, :16])[:, :, None], insts, ints(after[512:514, :16])[:, :, None]], 2
    )

    def strip(pixels, rows, lanes, line):
        full = jnp.concatenate([pixels.astype(BF16), before[rows, lanes], after[rows, lanes]], 1)
        lines = jnp.pad(wide_insts[:, line, :].astype(BF16), ((0, 14), (0, SIDE + 128 - 18)))
        return jnp.concatenate([full, lines], 0)

    top = strip(edges[0], slice(0, 64), slice(0, 64), 0)
    bottom = strip(edges[1], slice(448, 512), slice(64, 128), 15)
    near_strip = send(jnp.where(core == 0, bottom, top), SWAP)
    far_strip = send(jnp.where(core == 0, top, bottom), OVER)
    parts = gathered_far(group)

    from_near, from_far = ints(near_strip[64:66, :18]), ints(far_strip[64:66, :18])
    above, below = jnp.where(core == 0, from_far, from_near), jnp.where(core == 0, from_near, from_far)
    all_insts = jnp.concatenate([above[:, None, :], wide_insts, below[:, None, :]], 1)
    all_master, all_orient = all_insts[0], all_insts[1]

    matches = all_master[..., None] == jnp.arange(owner_map.shape[0], dtype=jnp.int32)
    slots = jnp.sum(jnp.where(matches, owner_map, 0), axis=-1)
    dy, dz = y ^ (slots // 64), z ^ ((slots // 16) % 4)
    half, entry = (slots // 8) % 2, slots % 8
    high = (dy // 2) + 2 * (dz // 2)
    mixed = (dy // 2 ^ dy % 2) + 2 * (dz // 2 ^ dz % 2)
    outer, inner = jnp.where(half == 0, mixed, high), jnp.where(half == 0, high, mixed)
    locs = (jnp.where(half == core, 0, 1) * 16 + outer * 4 + inner) * 8 + entry
    inside = jnp.stack([row > 0, row < 7, col > 0, col < 15]).astype(jnp.int32)
    codes = jnp.concatenate([locs.reshape(-1), all_orient.reshape(-1), inside, core.reshape(1).astype(jnp.int32)])

    vmem, smem = pl.BlockSpec(memory_space=pltpu.VMEM), pl.BlockSpec(memory_space=pltpu.SMEM)
    anywhere = pl.BlockSpec(memory_space=pl.ANY)
    wide = jax.ShapeDtypeStruct((SIDE, SIDE), F32)
    sums_shape = jax.ShapeDtypeStruct((128, 32, 128), BF16)
    tables = [spectra.reshape(2, BAND, NK * BAND), *constant_tables()]
    resist, free_new, own, other = pl.pallas_call(
        main_kernel,
        out_shape=(wide, wide, sums_shape, sums_shape),
        in_specs=[smem] * 2 + [anywhere] * 8 + [vmem] * 4 + [anywhere] * (2 + len(tables)),
        out_specs=(anywhere, anywhere, vmem, vmem),
        scratch_shapes=[
            pltpu.VMEM((512, 32, 128), F32),
            pltpu.VMEM((1152, 1152), BF16),
            pltpu.VMEM((SIDE, SIDE), F32),
            pltpu.VMEM((NK, GRID, 2 * GRID), F32),
            pltpu.VMEM((256, 1024), BF16),
            pltpu.VMEM((512, 1024), BF16),
            pltpu.VMEM((512, 32, 128), F32),
            pltpu.VMEM((SIDE, SIDE), F32),
            pltpu.VMEM((SIDE, SIDE), F32),
            *(pltpu.VMEM(t.shape, t.dtype) for t in tables),
            *[pltpu.VMEM((32, 32, 128), BF16)] * 8,
            pltpu.SemaphoreType.DMA((4,)),
            pltpu.SemaphoreType.DMA((len(tables),)),
            pltpu.SemaphoreType.DMA((1,)),
            pltpu.SemaphoreType.DMA((4,)),
            pltpu.SemaphoreType.DMA((4,)),
            pltpu.SemaphoreType.DMA((8,)),
        ],
        compiler_params=pltpu.CompilerParams(vmem_limit_bytes=52 * 1024 * 1024),
        name="image_and_gradient",
    )(codes, weights, *parts, near_strip, far_strip, before, after, tile_free, target, *tables)

    summed = scattered_sum(own, other)
    fresh = smooth(own_cells.reshape(8, CELL, CELL) - 0.05 * from_wire(summed))
    fresh_wire = jnp.concatenate([fresh[:, :32, :], fresh[:, 32:, :]], axis=2).astype(BF16)
    parts = gathered_far(gathered_near(fresh_wire))
    new_mask = pl.pallas_call(
        final_kernel,
        out_shape=wide,
        in_specs=[smem] + [anywhere] * 9,
        out_specs=anywhere,
        scratch_shapes=[
            pltpu.VMEM((512, 32, 128), F32),
            pltpu.VMEM((SIDE, SIDE), F32),
            *[pltpu.VMEM((32, 32, 128), BF16)] * 8,
            *[pltpu.SemaphoreType.DMA((8,))] * 3,
        ],
        compiler_params=pltpu.CompilerParams(vmem_limit_bytes=52 * 1024 * 1024),
        name="final_mask",
    )(codes, *parts, free_new)
    mine = from_wire(parts[0][:8]).reshape(8, CELL * CELL).astype(F32)
    others = from_wire(parts[4][:8]).reshape(8, CELL * CELL).astype(F32)
    masters_out = jnp.where(core == 0, jnp.concatenate([mine, others], 0), jnp.concatenate([others, mine], 0))
    return resist, new_mask, masters_out


def solution(mesh):
    placed = (P("col", None), P(*BOTH), P(*BOTH), P(), P(*BOTH), P(*BOTH), P(), P())
    return jax.shard_map(
        per_device,
        mesh=mesh,
        in_specs=placed,
        out_specs=(P(*BOTH), P(*BOTH), P("col", None)),
        check_vma=False,
    )
```

```python
import functools

import jax
import jax.numpy as jnp
import numpy as np
from jax import lax
from jax.experimental import pallas as pl
from jax.experimental.pallas import tpu as pltpu
from jax.sharding import PartitionSpec as P

TILE, HALO, CELL, BAND, NK, PAD = 512, 64, 64, 128, 8, 640
GRID = 256
SIDE = 1024
BOTH = ("row", "col")
F32, BF16 = jnp.float32, jnp.bfloat16


def waves(positions, period):
    freqs = np.arange(BAND) - BAND // 2
    angles = 2.0 * np.pi * ((freqs[:, None] * positions[None, :]) % period) / period
    return np.cos(angles), np.sin(angles)


def mean_gain(cos, sin):
    rounded = [t.astype(jnp.bfloat16).astype(np.float64) for t in (cos, sin)]
    return (rounded[0] * cos + rounded[1] * sin).mean(1)


@functools.cache
def constant_tables():
    cos_c, sin_c = waves(np.arange(GRID), GRID)
    cos_p, sin_p = waves(np.arange(PAD), PAD)
    cos_i, sin_i = cos_p[:, HALO : HALO + TILE], sin_p[:, HALO : HALO + TILE]
    by_pixel = np.concatenate([cos_p.T, sin_p.T], 1)
    first = np.zeros((2, 768, 256))
    first[0, 0:576] = by_pixel[64:640]
    first[0, 640:704] = by_pixel[0:64]
    first[1, 64:640] = by_pixel[0:576]
    first[1, 704:768] = by_pixel[576:640]
    second = np.concatenate([cos_p, sin_p], 0)
    up_u = np.block([[cos_c.T, -sin_c.T], [sin_c.T, cos_c.T]])
    up_v = np.block([[cos_c, sin_c], [-sin_c, cos_c]])
    places = (HALO + np.arange(TILE)) / PAD
    orders = np.arange(1, BAND)
    shift = places[:, None] - np.arange(GRID)[None, :] / GRID
    fine = (1.0 + 2.0 * np.cos(2 * np.pi * shift[..., None] * orders).sum(-1)) / GRID
    out_v = np.block([[cos_i, -sin_i], [-sin_i, -cos_i]])
    out_u = np.concatenate([cos_i.T, -sin_i.T], 1)
    high = fine.astype(jnp.bfloat16)
    low = (fine - high.astype(np.float64)).astype(jnp.bfloat16)
    cast = lambda a: np.ascontiguousarray(a).astype(jnp.bfloat16)
    gain = mean_gain(cos_i, sin_i) / mean_gain(cos_c, sin_c)
    return [
        np.outer(gain, gain).astype(np.float32), cast(first), cast(second), cast(up_u), cast(up_u.T), cast(up_v), cast(up_v.T),
        high, low, cast(fine.T), cast(low.T), cast(out_v), cast(out_u),
    ]


def dot(a, b):
    return jnp.dot(a, b, preferred_element_type=F32)


def half_lanes():
    return lax.broadcasted_iota(jnp.int32, (8, 128), 1) < 64


def turned(groups, turn_a, turn_b):
    lane = lax.broadcasted_iota(jnp.int32, (8, 128), 1)
    sub = lax.broadcasted_iota(jnp.int32, (8, 128), 0)
    left = half_lanes()
    flip_cols = jnp.where(left, turn_a, turn_b) >= 2
    lanes = jnp.where(flip_cols, jnp.where(left, 63, 191) - lane, lane)
    flip_rows = jnp.where(left, lax.rem(turn_a, 2), lax.rem(turn_b, 2)) == 1
    subs = jnp.where(flip_rows, 7 - sub, sub)
    return [
        jnp.take_along_axis(jnp.take_along_axis(g, subs, axis=0), lanes, axis=1) for g in groups
    ]


def places(loc, turn, right):
    flip = lax.rem(turn, 2)
    upper = (1 - flip) if right else flip
    rows = [pl.ds(pl.multiple_of(8 * i + flip * (8 * (3 - 2 * i)), 8), 8) for i in range(4)]
    return loc + 256 * upper, loc + 256 * (1 - upper), rows


def pair_image(cells, loc_a, turn_a, loc_b, turn_b):
    left = half_lanes()
    top_a, low_a, rows_a = places(loc_a, turn_a, False)
    top_b, low_b, rows_b = places(loc_b, turn_b, True)
    groups = [
        jnp.where(left, cells[a, rows_a[i], :], cells[b, rows_b[i], :])
        for a, b in ((top_a, top_b), (low_a, low_b))
        for i in range(4)
    ]
    return jnp.concatenate(turned(groups, turn_a, turn_b), axis=0)


def fill_cells(parts, cells, loads):
    for n, part in enumerate(parts):
        loads[n].wait()
        value = part[...].astype(F32)
        cells[pl.ds(32 * n, 32)] = value
        cells[pl.ds(256 + 32 * n, 32)] = pltpu.roll(value.reshape(1024, 128), 64, 1).reshape(32, 32, 128)


def main_kernel(*refs):
    codes, weights = refs[0:2]
    part_in = refs[2:10]
    near_strip, far_strip, before, after = refs[10:14]
    free_in, target_in = refs[14:16]
    table_in = refs[16:30]
    resist_out, free_out = refs[30:32]
    sum_outs = refs[32:40]
    cells, mask, shading, fields, amps, halves, sums, free, target = refs[40:49]
    tables = refs[49:63]
    parts = refs[63:71]
    free_sems, table_sems, target_sem, resist_sems, out_sems, part_sems = refs[71:77]
    (spectra, gain, first, second, up_u, up_ut, up_v, up_vt, fine, fine_lo, fine_t, fine_tlo, out_v, out_u) = tables

    part_loads = [pltpu.make_async_copy(a, b, part_sems.at[n]) for n, (a, b) in enumerate(zip(part_in, parts))]
    for load in part_loads:
        load.start()
    loads = [
        pltpu.make_async_copy(free_in.at[pl.ds(256 * n, 256)], free.at[pl.ds(256 * n, 256)], free_sems.at[n])
        for n in range(4)
    ]
    for load in loads:
        load.start()
    table_loads = [pltpu.make_async_copy(a, b, table_sems.at[n]) for n, (a, b) in enumerate(zip(table_in, tables))]
    for load in table_loads:
        load.start()
    target_load = pltpu.make_async_copy(target_in, target, target_sem.at[0])
    target_load.start()

    def code(a, b):
        return codes[a * 18 + b], codes[324 + a * 18 + b]

    fill_cells(parts, cells, part_loads)
    core = codes[652]
    def edge_strip(lanes, own_core):
        return jnp.where(core == own_core, near_strip[0:64, lanes].astype(F32), far_strip[0:64, lanes].astype(F32))

    lane_w = lax.broadcasted_iota(jnp.int32, (64, 128), 1)
    inside_cols = jnp.where(lane_w < 64, codes[650], codes[651]) > 0
    for a, flag, own_core in ((0, 648, 1), (17, 649, 0)):
        for p in range(9):
            cols = slice(p * 128, p * 128 + 128)
            ends = (2 * p + 1, 2 * p + 2) if p < 8 else (0, 17)
            image = pair_image(cells, *code(a, ends[0]), *code(a, ends[1]))
            value = jnp.where(codes[flag] > 0, jnp.tanh(image + edge_strip(cols, own_core)), 0.0)
            if p == 8:
                value = jnp.where(inside_cols, value, 0.0)
            mask[a * 64 : a * 64 + 64, cols] = value.astype(BF16)

    def edge_cols(r, _):
        rows = pl.ds(pl.multiple_of(r * 64, 64), 64)
        left, right = before[rows, :].astype(F32), after[rows, :].astype(F32)
        strips = (
            jnp.where(lane_w < 64, left, pltpu.roll(right, 64, 1)),
            jnp.where(lane_w < 64, pltpu.roll(left, 64, 1), right),
        )
        for n in range(2):
            a = r + 8 * n + 1
            image = pair_image(cells, *code(a, 0), *code(a, 17))
            value = jnp.where(inside_cols, jnp.tanh(image + strips[n]), 0.0)
            mask[pl.ds(pl.multiple_of(a * 64, 64), 64), 1024:1152] = value.astype(BF16)
        return 0

    lax.fori_loop(0, 8, edge_cols, 0, unroll=2)

    def interior(a, _):
        rows = pl.ds(pl.multiple_of(a * 64, 64), 64)
        rows_m = pl.ds(pl.multiple_of(a * 64 + 64, 64), 64)
        for p in range(8):
            cols = slice(p * 128, p * 128 + 128)
            image = pair_image(cells, *code(a + 1, 2 * p + 1), *code(a + 1, 2 * p + 2))
            value = jnp.tanh(image + free[rows, cols])
            shading[rows, cols] = value
            mask[rows_m, cols] = value.astype(BF16)
        return 0

    for n in range(4):
        loads[n].wait()
        lax.fori_loop(4 * n, 4 * n + 4, interior, 0)
    for load in table_loads:
        load.wait()
    target_load.wait()

    def tile(t, _):
        i, j = t // 2, t % 2
        rows_w = pl.ds(pl.multiple_of(i * TILE, 128), PAD)
        window = jnp.concatenate(
            [mask[rows_w, pl.ds(pl.multiple_of(j * 384, 128), 640)], mask[rows_w, 1024:1152]], axis=1
        )
        forw = dot(window, first[j]).astype(BF16)
        spec = dot(second[...], forw)
        scale = gain[...] * (1.0 / PAD)
        spec_re = (spec[:128, :128] + spec[128:, 128:]) * scale
        spec_im = (spec[128:, :128] - spec[:128, 128:]) * scale
        for k in range(NK):
            at = slice(k * 128, k * 128 + 128)
            k_re, k_im = spectra[0, :, at], spectra[1, :, at]
            amps[0:128, at] = (k_re * spec_re - k_im * spec_im).astype(BF16)
            amps[128:256, at] = (k_re * spec_im + k_im * spec_re).astype(BF16)
        half = dot(up_u[...], amps[...]).astype(BF16)
        left = jnp.concatenate(
            [jnp.concatenate([half[0:256, k * 128 : k * 128 + 128], half[256:512, k * 128 : k * 128 + 128]], axis=1) for k in range(NK)],
            axis=0,
        )
        fields[...] = dot(left, up_v[...]).reshape(NK, GRID, 2 * GRID)
        intensity = jnp.zeros((GRID, GRID), F32)
        for k in range(NK):
            at = slice(k * 128, k * 128 + 128)
            re, im = fields[k, :, :256], fields[k, :, 256:]
            intensity = intensity + weights[k] * (re * re + im * im)
        coarse = (intensity * (1.0 / BAND**2)).astype(BF16)
        half_fine = dot(fine[...], coarse) + dot(fine_lo[...], coarse)
        half_fine = half_fine.astype(BF16)
        image = dot(half_fine, fine_t[...]) + dot(half_fine, fine_tlo[...])
        rows_t = pl.ds(pl.multiple_of(i * TILE, TILE), TILE)
        cols_t = pl.ds(pl.multiple_of(j * TILE, TILE), TILE)
        resist = jax.nn.sigmoid(2.0 * (image - 1.8))
        slopes = (4.0 * (resist - target[rows_t, cols_t]) * resist * (1.0 - resist)).astype(BF16)
        target[rows_t, cols_t] = resist
        pltpu.make_async_copy(
            target.at[rows_t, cols_t], resist_out.at[rows_t, cols_t], resist_sems.at[t]
        ).start()
        back = dot(fine_t[...], dot(slopes, fine[...]).astype(BF16))
        for k in range(NK):
            at = slice(k * 128, k * 128 + 128)
            scaled = back * (weights[k] * (2.0 / BAND**2))
            both = jnp.concatenate(
                [(scaled * fields[k, :, :256]).astype(BF16), (scaled * fields[k, :, 256:]).astype(BF16)], axis=1
            )
            low = dot(both, up_vt[...]).astype(BF16)
            halves[0:256, at] = low[:, :128]
            halves[256:512, at] = low[:, 128:]
        bspec_re = jnp.zeros((128, 128), F32)
        bspec_im = jnp.zeros((128, 128), F32)
        bamp = dot(up_ut[...], halves[...])
        for k in range(NK):
            at = slice(k * 128, k * 128 + 128)
            k_re, k_im = spectra[0, :, at], spectra[1, :, at]
            re, im = bamp[:128, at], bamp[128:, at]
            bspec_re = bspec_re + (k_re * re + k_im * im)
            bspec_im = bspec_im + (k_re * im - k_im * re)
        bspec = jnp.concatenate([bspec_re * scale, bspec_im * scale], axis=1)
        bforw = dot(bspec.astype(BF16), out_v[...]).astype(BF16)
        stacked = jnp.concatenate([bforw[:, :TILE], bforw[:, TILE:]], axis=0)
        gradient = dot(out_u[...], stacked)
        shade = shading[rows_t, cols_t]
        grad = gradient * (1.0 - shade * shade)
        shading[rows_t, cols_t] = grad
        free[rows_t, cols_t] = free[rows_t, cols_t] - grad
        pltpu.make_async_copy(free.at[rows_t, cols_t], free_out.at[rows_t, cols_t], out_sems.at[t]).start()
        return 0

    lax.fori_loop(0, 4, tile, 0)

    def clear(n, _):
        sums[pl.ds(n * 8, 8)] = jnp.zeros((8, 32, 128), F32)
        return 0

    lax.fori_loop(0, 64, clear, 0)

    def collect(a, _):
        rows = pl.multiple_of(a * 64, 64)
        left = half_lanes()
        for p in range(8):
            cols = slice(p * 128, p * 128 + 128)
            loc_a, turn_a = code(a + 1, 2 * p + 1)
            loc_b, turn_b = code(a + 1, 2 * p + 2)
            groups = turned([shading[pl.ds(rows + 8 * i, 8), cols] for i in range(8)], turn_a, turn_b)
            for loc, turn, right, keep in ((loc_a, turn_a, False, left), (loc_b, turn_b, True, ~left)):
                top, low, at = places(loc, turn, right)
                spots = [(top, at[i]) for i in range(4)] + [(low, at[i]) for i in range(4)]
                totals = [sums[n, r, :] + jnp.where(keep, g, 0.0) for (n, r), g in zip(spots, groups)]
                for (n, r), total in zip(spots, totals):
                    sums[n, r, :] = total
        return 0

    lax.fori_loop(0, 16, collect, 0)
    for part, out in enumerate(sum_outs):

        def join(n, _):
            at = part * 32 + n * 8
            rolled = pltpu.roll(sums[pl.ds(256 + at, 8)].reshape(256, 128), 64, 1)
            out[pl.ds(n * 8, 8)] = (sums[pl.ds(at, 8)].reshape(256, 128) + rolled).reshape(8, 32, 128).astype(BF16)
            return 0

        lax.fori_loop(0, 4, join, 0)

    for t in range(4):
        at = (pl.ds(t // 2 * TILE, TILE), pl.ds(t % 2 * TILE, TILE))
        pltpu.make_async_copy(target.at[at], resist_out.at[at], resist_sems.at[t]).wait()
        pltpu.make_async_copy(free.at[at], free_out.at[at], out_sems.at[t]).wait()


def final_kernel(*refs):
    codes = refs[0]
    part_in, (free_in, out), cells, free = refs[1:9], refs[9:11], refs[11], refs[12]
    parts, (part_sems, free_sems, out_sems) = refs[13:21], refs[21:24]
    part_loads = [pltpu.make_async_copy(a, b, part_sems.at[n]) for n, (a, b) in enumerate(zip(part_in, parts))]
    strips = [pl.ds(128 * n, 128) for n in range(8)]
    loads = [pltpu.make_async_copy(free_in.at[r], free.at[r], free_sems.at[n]) for n, r in enumerate(strips)]
    stores = [pltpu.make_async_copy(free.at[r], out.at[r], out_sems.at[n]) for n, r in enumerate(strips)]
    for load in part_loads + loads:
        load.start()
    fill_cells(parts, cells, part_loads)

    def interior(a, _):
        rows = pl.ds(pl.multiple_of(a * 64, 64), 64)
        for p in range(8):
            cols = slice(p * 128, p * 128 + 128)
            at = (a + 1) * 18 + 2 * p
            image = pair_image(cells, codes[at + 1], codes[325 + at], codes[at + 2], codes[326 + at])
            free[rows, cols] = jnp.tanh(image + free[rows, cols])
        return 0

    for n in range(8):
        loads[n].wait()
        lax.fori_loop(2 * n, 2 * n + 2, interior, 0)
        stores[n].start()
    for store in stores:
        store.wait()


def flat(x, c, y, z):
    return ((x % 4) * 2 + c) * 16 + (y % 4) * 4 + z % 4


CHIPS = [(x, y, z) for x in range(4) for y in range(4) for z in range(4)]


def mirrored(n, masks):
    return [
        (flat(x, c, y, z), flat(x, c, y ^ (masks[c] * (n % 2)), z ^ (masks[c] * (n // 2))))
        for x, y, z in CHIPS
        for c in range(2)
    ]


def near(n):
    return mirrored(n, (3, 1))


def far(n):
    return mirrored(n, (1, 3))


def shift_x(d):
    return [(flat(x, c, y, z), flat(x + d, c, y, z)) for x, y, z in CHIPS for c in range(2)]


SWAP = [(flat(x, c, y, z), flat(x, 1 - c, y, z)) for x, y, z in CHIPS for c in range(2)]


OVER = [(flat(x, 0, y, z), flat(x - 1, 1, y, z)) for x, y, z in CHIPS if x > 0] + [
    (flat(x, 1, y, z), flat(x + 1, 0, y, z)) for x, y, z in CHIPS if x < 3
]


def send(value, pairs):
    return lax.ppermute(value, BOTH, pairs)


def gathered_near(piece):
    got = [send(piece, near(n)) for n in (3, 1, 2)]
    return jnp.concatenate([piece, got[1], got[2], got[0]], axis=0)


def gathered_far(group):
    got = [send(group, far(n)) for n in (3, 1, 2)]
    mine = [group, got[1], got[2], got[0]]
    return mine + [send(part, SWAP) for part in mine]


def scattered_sum(own, other):
    swapped = {n: send(other[n], SWAP) for n in (3, 1, 2, 0)}
    total = {n: (own[n].astype(F32) + swapped[n].astype(F32)).astype(BF16) for n in (3, 1, 2, 0)}
    got = [send(total[n], far(n)) for n in (3, 1, 2)]
    total = sum((g.astype(F32) for g in got), total[0].astype(F32)).astype(BF16).reshape(4, 8, 32, 128)
    got = [send(total[n], near(n)) for n in (3, 1, 2)]
    total = sum((g.astype(F32) for g in got), total[0].astype(F32)).astype(BF16)
    got = [send(total, shift_x(d)) for d in (2, 1, 3)]
    return sum((g.astype(F32) for g in got), total.astype(F32))


def to_wire(rows):
    cells = rows.reshape(-1, CELL, CELL)
    return jnp.concatenate([cells[:, :32, :], cells[:, 32:, :]], axis=2)


def from_wire(wire):
    return jnp.concatenate([wire[:, :, :64], wire[:, :, 64:]], axis=1)


def smooth(grids):
    framed = jnp.pad(grids, ((0, 0), (1, 1), (1, 1)))
    beside = framed[:, 2:, 1:-1] + framed[:, :-2, 1:-1] + framed[:, 1:-1, 2:] + framed[:, 1:-1, :-2]
    return 0.5 * grids + 0.125 * beside


def steps(axis):
    n = lax.axis_size(axis)
    up = [(i, i + 1) for i in range(n - 1)]
    return up, [(b, a) for a, b in up]


def per_device(masters, inst_master, inst_orient, owner_map, tile_free, target, spectra, weights):
    row, col = lax.axis_index("row"), lax.axis_index("col")
    core, y, z = row % 2, col // 4, col % 4
    own_cells = lax.dynamic_slice_in_dim(masters, core * 8, 8, 0)
    piece, tile_free_late = lax.optimization_barrier((to_wire(own_cells.astype(BF16)), tile_free))
    group = gathered_near(piece)

    edges = lax.optimization_barrier(
        (
            tile_free_late[:64],
            tile_free_late[SIDE - 64 :],
            tile_free_late[:, :64],
            tile_free_late[:, SIDE - 64 :],
        )
    )
    insts = jnp.stack([inst_master, inst_orient])

    def side(pixels, line):
        packed = jnp.concatenate([pixels[:512], pixels[512:]], 1).astype(BF16)
        lines = jnp.pad(insts[:, :, line].astype(BF16), ((0, 14), (0, 112)))
        return jnp.concatenate([packed, lines], 0)

    up, down = steps("col")
    before = lax.ppermute(side(edges[3], 15), "col", up)
    after = lax.ppermute(side(edges[2], 0), "col", down)

    def ints(a):
        return a.astype(F32).astype(jnp.int32)

    wide_insts = jnp.concatenate(
        [ints(before[512:514, :16])[:, :, None], insts, ints(after[512:514, :16])[:, :, None]], 2
    )

    def strip(pixels, rows, lanes, line):
        full = jnp.concatenate([pixels.astype(BF16), before[rows, lanes], after[rows, lanes]], 1)
        lines = jnp.pad(wide_insts[:, line, :].astype(BF16), ((0, 14), (0, SIDE + 128 - 18)))
        return jnp.concatenate([full, lines], 0)

    top = strip(edges[0], slice(0, 64), slice(0, 64), 0)
    bottom = strip(edges[1], slice(448, 512), slice(64, 128), 15)
    near_strip = send(jnp.where(core == 0, bottom, top), SWAP)
    far_strip = send(jnp.where(core == 0, top, bottom), OVER)
    parts = gathered_far(group)

    from_near, from_far = ints(near_strip[64:66, :18]), ints(far_strip[64:66, :18])
    above, below = jnp.where(core == 0, from_far, from_near), jnp.where(core == 0, from_near, from_far)
    all_insts = jnp.concatenate([above[:, None, :], wide_insts, below[:, None, :]], 1)
    all_master, all_orient = all_insts[0], all_insts[1]

    matches = all_master[..., None] == jnp.arange(owner_map.shape[0], dtype=jnp.int32)
    slots = jnp.sum(jnp.where(matches, owner_map, 0), axis=-1)
    dy, dz = y ^ (slots // 64), z ^ ((slots // 16) % 4)
    half, entry = (slots // 8) % 2, slots % 8
    high = (dy // 2) + 2 * (dz // 2)
    mixed = (dy // 2 ^ dy % 2) + 2 * (dz // 2 ^ dz % 2)
    outer, inner = jnp.where(half == 0, mixed, high), jnp.where(half == 0, high, mixed)
    locs = (jnp.where(half == core, 0, 1) * 16 + outer * 4 + inner) * 8 + entry
    inside = jnp.stack([row > 0, row < 7, col > 0, col < 15]).astype(jnp.int32)
    codes = jnp.concatenate([locs.reshape(-1), all_orient.reshape(-1), inside, core.reshape(1).astype(jnp.int32)])

    vmem, smem = pl.BlockSpec(memory_space=pltpu.VMEM), pl.BlockSpec(memory_space=pltpu.SMEM)
    anywhere = pl.BlockSpec(memory_space=pl.ANY)
    wide = jax.ShapeDtypeStruct((SIDE, SIDE), F32)
    sums_shape = jax.ShapeDtypeStruct((32, 32, 128), BF16)
    tables = [spectra.reshape(2, BAND, NK * BAND), *constant_tables()]
    resist, free_new, *sums = pl.pallas_call(
        main_kernel,
        out_shape=(wide, wide, *[sums_shape] * 8),
        in_specs=[smem] * 2 + [anywhere] * 8 + [vmem] * 4 + [anywhere] * (2 + len(tables)),
        out_specs=(anywhere, anywhere, *[vmem] * 8),
        scratch_shapes=[
            pltpu.VMEM((512, 32, 128), F32),
            pltpu.VMEM((1152, 1152), BF16),
            pltpu.VMEM((SIDE, SIDE), F32),
            pltpu.VMEM((NK, GRID, 2 * GRID), F32),
            pltpu.VMEM((256, 1024), BF16),
            pltpu.VMEM((512, 1024), BF16),
            pltpu.VMEM((512, 32, 128), F32),
            pltpu.VMEM((SIDE, SIDE), F32),
            pltpu.VMEM((SIDE, SIDE), F32),
            *(pltpu.VMEM(t.shape, t.dtype) for t in tables),
            *[pltpu.VMEM((32, 32, 128), BF16)] * 8,
            pltpu.SemaphoreType.DMA((4,)),
            pltpu.SemaphoreType.DMA((len(tables),)),
            pltpu.SemaphoreType.DMA((1,)),
            pltpu.SemaphoreType.DMA((4,)),
            pltpu.SemaphoreType.DMA((4,)),
            pltpu.SemaphoreType.DMA((8,)),
        ],
        compiler_params=pltpu.CompilerParams(vmem_limit_bytes=52 * 1024 * 1024),
        name="image_and_gradient",
    )(codes, weights, *parts, near_strip, far_strip, before, after, tile_free, target, *tables)

    summed = scattered_sum(sums[:4], sums[4:])
    fresh = smooth(own_cells.reshape(8, CELL, CELL) - 0.05 * from_wire(summed))
    fresh_wire = jnp.concatenate([fresh[:, :32, :], fresh[:, 32:, :]], axis=2).astype(BF16)
    parts = gathered_far(gathered_near(fresh_wire))
    new_mask = pl.pallas_call(
        final_kernel,
        out_shape=wide,
        in_specs=[smem] + [anywhere] * 9,
        out_specs=anywhere,
        scratch_shapes=[
            pltpu.VMEM((512, 32, 128), F32),
            pltpu.VMEM((SIDE, SIDE), F32),
            *[pltpu.VMEM((32, 32, 128), BF16)] * 8,
            *[pltpu.SemaphoreType.DMA((8,))] * 3,
        ],
        compiler_params=pltpu.CompilerParams(vmem_limit_bytes=52 * 1024 * 1024),
        name="final_mask",
    )(codes, *parts, free_new)
    mine = from_wire(parts[0][:8]).reshape(8, CELL * CELL).astype(F32)
    others = from_wire(parts[4][:8]).reshape(8, CELL * CELL).astype(F32)
    masters_out = jnp.where(core == 0, jnp.concatenate([mine, others], 0), jnp.concatenate([others, mine], 0))
    return resist, new_mask, masters_out


def solution(mesh):
    placed = (P("col", None), P(*BOTH), P(*BOTH), P(), P(*BOTH), P(*BOTH), P(), P())
    return jax.shard_map(
        per_device,
        mesh=mesh,
        in_specs=placed,
        out_specs=(P(*BOTH), P(*BOTH), P("col", None)),
        check_vma=False,
    )
```

```python
import functools

import jax
import jax.numpy as jnp
import numpy as np
from jax import lax
from jax.experimental import pallas as pl
from jax.experimental.pallas import tpu as pltpu
from jax.sharding import PartitionSpec as P

TILE, HALO, CELL, BAND, NK, PAD = 512, 64, 64, 128, 8, 640
GRID = 256
SIDE = 1024
BOTH = ("row", "col")
F32, BF16 = jnp.float32, jnp.bfloat16


def waves(positions, period):
    freqs = np.arange(BAND) - BAND // 2
    angles = 2.0 * np.pi * ((freqs[:, None] * positions[None, :]) % period) / period
    return np.cos(angles), np.sin(angles)


def mean_gain(cos, sin):
    rounded = [t.astype(jnp.bfloat16).astype(np.float64) for t in (cos, sin)]
    return (rounded[0] * cos + rounded[1] * sin).mean(1)


@functools.cache
def constant_tables():
    cos_c, sin_c = waves(np.arange(GRID), GRID)
    cos_p, sin_p = waves(np.arange(PAD), PAD)
    cos_i, sin_i = cos_p[:, HALO : HALO + TILE], sin_p[:, HALO : HALO + TILE]
    by_pixel = np.concatenate([cos_p.T, sin_p.T], 1)
    first = np.zeros((2, 768, 256))
    first[0, 0:576] = by_pixel[64:640]
    first[0, 640:704] = by_pixel[0:64]
    first[1, 64:640] = by_pixel[0:576]
    first[1, 704:768] = by_pixel[576:640]
    second = np.concatenate([cos_p, sin_p], 0)
    up_u = np.block([[cos_c.T, -sin_c.T], [sin_c.T, cos_c.T]])
    up_v = np.block([[cos_c, sin_c], [-sin_c, cos_c]])
    places = (HALO + np.arange(TILE)) / PAD
    orders = np.arange(1, BAND)
    shift = places[:, None] - np.arange(GRID)[None, :] / GRID
    fine = (1.0 + 2.0 * np.cos(2 * np.pi * shift[..., None] * orders).sum(-1)) / GRID
    out_v = np.block([[cos_i, -sin_i], [-sin_i, -cos_i]])
    out_u = np.concatenate([cos_i.T, -sin_i.T], 1)
    high = fine.astype(jnp.bfloat16)
    low = (fine - high.astype(np.float64)).astype(jnp.bfloat16)
    cast = lambda a: np.ascontiguousarray(a).astype(jnp.bfloat16)
    gain = mean_gain(cos_i, sin_i) / mean_gain(cos_c, sin_c)
    return [
        np.outer(gain, gain).astype(np.float32), cast(first), cast(second), cast(up_u), cast(up_u.T), cast(up_v), cast(up_v.T),
        high, low, cast(fine.T), cast(low.T), cast(out_v), cast(out_u),
    ]


def dot(a, b):
    return jnp.dot(a, b, preferred_element_type=F32)


def half_lanes():
    return lax.broadcasted_iota(jnp.int32, (8, 128), 1) < 64


def turned(groups, turn_a, turn_b):
    lane = lax.broadcasted_iota(jnp.int32, (8, 128), 1)
    sub = lax.broadcasted_iota(jnp.int32, (8, 128), 0)
    left = half_lanes()
    flip_cols = jnp.where(left, turn_a, turn_b) >= 2
    lanes = jnp.where(flip_cols, jnp.where(left, 63, 191) - lane, lane)
    flip_rows = jnp.where(left, lax.rem(turn_a, 2), lax.rem(turn_b, 2)) == 1
    subs = jnp.where(flip_rows, 7 - sub, sub)
    return [
        jnp.take_along_axis(jnp.take_along_axis(g, subs, axis=0), lanes, axis=1) for g in groups
    ]


def places(loc, turn, right):
    flip = lax.rem(turn, 2)
    upper = (1 - flip) if right else flip
    rows = [pl.ds(pl.multiple_of(8 * i + flip * (8 * (3 - 2 * i)), 8), 8) for i in range(4)]
    return loc + 256 * upper, loc + 256 * (1 - upper), rows


def pair_image(cells, loc_a, turn_a, loc_b, turn_b):
    left = half_lanes()
    top_a, low_a, rows_a = places(loc_a, turn_a, False)
    top_b, low_b, rows_b = places(loc_b, turn_b, True)
    groups = [
        jnp.where(left, cells[a, rows_a[i], :], cells[b, rows_b[i], :])
        for a, b in ((top_a, top_b), (low_a, low_b))
        for i in range(4)
    ]
    return jnp.concatenate(turned(groups, turn_a, turn_b), axis=0)


def fill_cells(parts, cells, loads):
    for n, part in enumerate(parts):
        loads[n].wait()
        value = part[...].astype(F32)
        cells[pl.ds(32 * n, 32)] = value
        cells[pl.ds(256 + 32 * n, 32)] = pltpu.roll(value.reshape(1024, 128), 64, 1).reshape(32, 32, 128)


def main_kernel(*refs):
    codes, weights = refs[0:2]
    part_in = refs[2:10]
    near_strip, far_strip, before, after = refs[10:14]
    free_in, target_in = refs[14:16]
    table_in = refs[16:30]
    resist_out, free_out = refs[30:32]
    sum_outs = refs[32:40]
    cells, mask, shading, fields, amps, halves, sums, free, target = refs[40:49]
    tables = refs[49:63]
    parts = refs[63:71]
    free_sems, table_sems, target_sem, resist_sems, out_sems, part_sems = refs[71:77]
    (spectra, gain, first, second, up_u, up_ut, up_v, up_vt, fine, fine_lo, fine_t, fine_tlo, out_v, out_u) = tables

    part_loads = [pltpu.make_async_copy(a, b, part_sems.at[n]) for n, (a, b) in enumerate(zip(part_in, parts))]
    for load in part_loads:
        load.start()
    loads = [
        pltpu.make_async_copy(free_in.at[pl.ds(256 * n, 256)], free.at[pl.ds(256 * n, 256)], free_sems.at[n])
        for n in range(4)
    ]
    for load in loads:
        load.start()
    table_loads = [pltpu.make_async_copy(a, b, table_sems.at[n]) for n, (a, b) in enumerate(zip(table_in, tables))]
    for load in table_loads:
        load.start()
    target_load = pltpu.make_async_copy(target_in, target, target_sem.at[0])
    target_load.start()

    def code(a, b):
        return codes[a * 18 + b], codes[324 + a * 18 + b]

    fill_cells(parts, cells, part_loads)
    core = codes[652]
    def edge_strip(lanes, own_core):
        return jnp.where(core == own_core, near_strip[0:64, lanes].astype(F32), far_strip[0:64, lanes].astype(F32))

    lane_w = lax.broadcasted_iota(jnp.int32, (64, 128), 1)
    inside_cols = jnp.where(lane_w < 64, codes[650], codes[651]) > 0
    for a, flag, own_core in ((0, 648, 1), (17, 649, 0)):
        for p in range(9):
            cols = slice(p * 128, p * 128 + 128)
            ends = (2 * p + 1, 2 * p + 2) if p < 8 else (0, 17)
            image = pair_image(cells, *code(a, ends[0]), *code(a, ends[1]))
            value = jnp.where(codes[flag] > 0, jnp.tanh(image + edge_strip(cols, own_core)), 0.0)
            if p == 8:
                value = jnp.where(inside_cols, value, 0.0)
            mask[a * 64 : a * 64 + 64, cols] = value.astype(BF16)

    def edge_cols(r, _):
        rows = pl.ds(pl.multiple_of(r * 64, 64), 64)
        left, right = before[rows, :].astype(F32), after[rows, :].astype(F32)
        strips = (
            jnp.where(lane_w < 64, left, pltpu.roll(right, 64, 1)),
            jnp.where(lane_w < 64, pltpu.roll(left, 64, 1), right),
        )
        for n in range(2):
            a = r + 8 * n + 1
            image = pair_image(cells, *code(a, 0), *code(a, 17))
            value = jnp.where(inside_cols, jnp.tanh(image + strips[n]), 0.0)
            mask[pl.ds(pl.multiple_of(a * 64, 64), 64), 1024:1152] = value.astype(BF16)
        return 0

    lax.fori_loop(0, 8, edge_cols, 0, unroll=2)

    def interior(a, _):
        rows = pl.ds(pl.multiple_of(a * 64, 64), 64)
        rows_m = pl.ds(pl.multiple_of(a * 64 + 64, 64), 64)
        for p in range(8):
            cols = slice(p * 128, p * 128 + 128)
            image = pair_image(cells, *code(a + 1, 2 * p + 1), *code(a + 1, 2 * p + 2))
            value = jnp.tanh(image + free[rows, cols])
            shading[rows, cols] = value
            mask[rows_m, cols] = value.astype(BF16)
        return 0

    for n in range(4):
        loads[n].wait()
        lax.fori_loop(4 * n, 4 * n + 4, interior, 0)
    for load in table_loads:
        load.wait()
    target_load.wait()

    def tile(t, _):
        i, j = t // 2, t % 2
        rows_w = pl.ds(pl.multiple_of(i * TILE, 128), PAD)
        window = jnp.concatenate(
            [mask[rows_w, pl.ds(pl.multiple_of(j * 384, 128), 640)], mask[rows_w, 1024:1152]], axis=1
        )
        forw = dot(window, first[j]).astype(BF16)
        spec = dot(second[...], forw)
        scale = gain[...] * (1.0 / PAD)
        spec_re = (spec[:128, :128] + spec[128:, 128:]) * scale
        spec_im = (spec[128:, :128] - spec[:128, 128:]) * scale
        for k in range(NK):
            at = slice(k * 128, k * 128 + 128)
            k_re, k_im = spectra[0, :, at], spectra[1, :, at]
            amps[0:128, at] = (k_re * spec_re - k_im * spec_im).astype(BF16)
            amps[128:256, at] = (k_re * spec_im + k_im * spec_re).astype(BF16)
        half = dot(up_u[...], amps[...]).astype(BF16)
        left = jnp.concatenate(
            [jnp.concatenate([half[0:256, k * 128 : k * 128 + 128], half[256:512, k * 128 : k * 128 + 128]], axis=1) for k in range(NK)],
            axis=0,
        )
        fields[...] = dot(left, up_v[...]).reshape(NK, GRID, 2 * GRID)
        intensity = jnp.zeros((GRID, GRID), F32)
        for k in range(NK):
            at = slice(k * 128, k * 128 + 128)
            re, im = fields[k, :, :256], fields[k, :, 256:]
            intensity = intensity + weights[k] * (re * re + im * im)
        coarse = (intensity * (1.0 / BAND**2)).astype(BF16)
        half_fine = dot(fine[...], coarse) + dot(fine_lo[...], coarse)
        half_fine = half_fine.astype(BF16)
        image = dot(half_fine, fine_t[...]) + dot(half_fine, fine_tlo[...])
        rows_t = pl.ds(pl.multiple_of(i * TILE, TILE), TILE)
        cols_t = pl.ds(pl.multiple_of(j * TILE, TILE), TILE)
        resist = jax.nn.sigmoid(2.0 * (image - 1.8))
        slopes = (4.0 * (resist - target[rows_t, cols_t]) * resist * (1.0 - resist)).astype(BF16)
        target[rows_t, cols_t] = resist
        pltpu.make_async_copy(
            target.at[rows_t, cols_t], resist_out.at[rows_t, cols_t], resist_sems.at[t]
        ).start()
        back = dot(fine_t[...], dot(slopes, fine[...]).astype(BF16))
        both = []
        for k in range(NK):
            scaled = back * (weights[k] * (2.0 / BAND**2))
            both.append(
                jnp.concatenate(
                    [(scaled * fields[k, :, :256]).astype(BF16), (scaled * fields[k, :, 256:]).astype(BF16)], axis=1
                )
            )
        low = dot(jnp.concatenate(both, axis=0), up_vt[...]).astype(BF16)
        for k in range(NK):
            at = slice(k * 128, k * 128 + 128)
            halves[0:256, at] = low[k * 256 : k * 256 + 256, :128]
            halves[256:512, at] = low[k * 256 : k * 256 + 256, 128:]
        bspec_re = jnp.zeros((128, 128), F32)
        bspec_im = jnp.zeros((128, 128), F32)
        bamp = dot(up_ut[...], halves[...])
        for k in range(NK):
            at = slice(k * 128, k * 128 + 128)
            k_re, k_im = spectra[0, :, at], spectra[1, :, at]
            re, im = bamp[:128, at], bamp[128:, at]
            bspec_re = bspec_re + (k_re * re + k_im * im)
            bspec_im = bspec_im + (k_re * im - k_im * re)
        bspec = jnp.concatenate([bspec_re * scale, bspec_im * scale], axis=1)
        bforw = dot(bspec.astype(BF16), out_v[...]).astype(BF16)
        stacked = jnp.concatenate([bforw[:, :TILE], bforw[:, TILE:]], axis=0)
        gradient = dot(out_u[...], stacked)
        shade = shading[rows_t, cols_t]
        grad = gradient * (1.0 - shade * shade)
        shading[rows_t, cols_t] = grad
        free[rows_t, cols_t] = free[rows_t, cols_t] - grad
        pltpu.make_async_copy(free.at[rows_t, cols_t], free_out.at[rows_t, cols_t], out_sems.at[t]).start()
        return 0

    lax.fori_loop(0, 4, tile, 0)

    def clear(n, _):
        sums[pl.ds(n * 8, 8)] = jnp.zeros((8, 32, 128), F32)
        return 0

    lax.fori_loop(0, 64, clear, 0)

    def collect(a, _):
        rows = pl.multiple_of(a * 64, 64)
        left = half_lanes()
        for p in range(8):
            cols = slice(p * 128, p * 128 + 128)
            loc_a, turn_a = code(a + 1, 2 * p + 1)
            loc_b, turn_b = code(a + 1, 2 * p + 2)
            groups = turned([shading[pl.ds(rows + 8 * i, 8), cols] for i in range(8)], turn_a, turn_b)
            for loc, turn, right, keep in ((loc_a, turn_a, False, left), (loc_b, turn_b, True, ~left)):
                top, low, at = places(loc, turn, right)
                spots = [(top, at[i]) for i in range(4)] + [(low, at[i]) for i in range(4)]
                totals = [sums[n, r, :] + jnp.where(keep, g, 0.0) for (n, r), g in zip(spots, groups)]
                for (n, r), total in zip(spots, totals):
                    sums[n, r, :] = total
        return 0

    lax.fori_loop(0, 16, collect, 0)
    for part, out in enumerate(sum_outs):

        def join(n, _):
            at = part * 32 + n * 8
            rolled = pltpu.roll(sums[pl.ds(256 + at, 8)].reshape(256, 128), 64, 1)
            out[pl.ds(n * 8, 8)] = (sums[pl.ds(at, 8)].reshape(256, 128) + rolled).reshape(8, 32, 128).astype(BF16)
            return 0

        lax.fori_loop(0, 4, join, 0)

    for t in range(4):
        at = (pl.ds(t // 2 * TILE, TILE), pl.ds(t % 2 * TILE, TILE))
        pltpu.make_async_copy(target.at[at], resist_out.at[at], resist_sems.at[t]).wait()
        pltpu.make_async_copy(free.at[at], free_out.at[at], out_sems.at[t]).wait()


def final_kernel(*refs):
    codes = refs[0]
    part_in, (free_in, out), cells, free = refs[1:9], refs[9:11], refs[11], refs[12]
    parts, (part_sems, free_sems, out_sems) = refs[13:21], refs[21:24]
    part_loads = [pltpu.make_async_copy(a, b, part_sems.at[n]) for n, (a, b) in enumerate(zip(part_in, parts))]
    strips = [pl.ds(128 * n, 128) for n in range(8)]
    loads = [pltpu.make_async_copy(free_in.at[r], free.at[r], free_sems.at[n]) for n, r in enumerate(strips)]
    stores = [pltpu.make_async_copy(free.at[r], out.at[r], out_sems.at[n]) for n, r in enumerate(strips)]
    for load in part_loads + loads:
        load.start()
    fill_cells(parts, cells, part_loads)

    def interior(a, _):
        rows = pl.ds(pl.multiple_of(a * 64, 64), 64)
        for p in range(8):
            cols = slice(p * 128, p * 128 + 128)
            at = (a + 1) * 18 + 2 * p
            image = pair_image(cells, codes[at + 1], codes[325 + at], codes[at + 2], codes[326 + at])
            free[rows, cols] = jnp.tanh(image + free[rows, cols])
        return 0

    for n in range(8):
        loads[n].wait()
        lax.fori_loop(2 * n, 2 * n + 2, interior, 0)
        stores[n].start()
    for store in stores:
        store.wait()


def flat(x, c, y, z):
    return ((x % 4) * 2 + c) * 16 + (y % 4) * 4 + z % 4


CHIPS = [(x, y, z) for x in range(4) for y in range(4) for z in range(4)]


def mirrored(n, masks):
    return [
        (flat(x, c, y, z), flat(x, c, y ^ (masks[c] * (n % 2)), z ^ (masks[c] * (n // 2))))
        for x, y, z in CHIPS
        for c in range(2)
    ]


def near(n):
    return mirrored(n, (3, 1))


def far(n):
    return mirrored(n, (1, 3))


def shift_x(d):
    return [(flat(x, c, y, z), flat(x + d, c, y, z)) for x, y, z in CHIPS for c in range(2)]


SWAP = [(flat(x, c, y, z), flat(x, 1 - c, y, z)) for x, y, z in CHIPS for c in range(2)]


OVER = [(flat(x, 0, y, z), flat(x - 1, 1, y, z)) for x, y, z in CHIPS if x > 0] + [
    (flat(x, 1, y, z), flat(x + 1, 0, y, z)) for x, y, z in CHIPS if x < 3
]


def send(value, pairs):
    return lax.ppermute(value, BOTH, pairs)


def gathered_near(piece):
    got = [send(piece, near(n)) for n in (3, 1, 2)]
    return jnp.concatenate([piece, got[1], got[2], got[0]], axis=0)


def gathered_far(group):
    got = [send(group, far(n)) for n in (3, 1, 2)]
    mine = [group, got[1], got[2], got[0]]
    return mine + [send(part, SWAP) for part in mine]


def scattered_sum(own, other):
    swapped = {n: send(other[n], SWAP) for n in (3, 1, 2, 0)}
    total = {n: (own[n].astype(F32) + swapped[n].astype(F32)).astype(BF16) for n in (3, 1, 2, 0)}
    got = [send(total[n], far(n)) for n in (3, 1, 2)]
    total = sum((g.astype(F32) for g in got), total[0].astype(F32)).astype(BF16).reshape(4, 8, 32, 128)
    got = [send(total[n], near(n)) for n in (3, 1, 2)]
    total = sum((g.astype(F32) for g in got), total[0].astype(F32)).astype(BF16)
    got = [send(total, shift_x(d)) for d in (2, 1, 3)]
    return sum((g.astype(F32) for g in got), total.astype(F32))


def to_wire(rows):
    cells = rows.reshape(-1, CELL, CELL)
    return jnp.concatenate([cells[:, :32, :], cells[:, 32:, :]], axis=2)


def from_wire(wire):
    return jnp.concatenate([wire[:, :, :64], wire[:, :, 64:]], axis=1)


def smooth(grids):
    framed = jnp.pad(grids, ((0, 0), (1, 1), (1, 1)))
    beside = framed[:, 2:, 1:-1] + framed[:, :-2, 1:-1] + framed[:, 1:-1, 2:] + framed[:, 1:-1, :-2]
    return 0.5 * grids + 0.125 * beside


def steps(axis):
    n = lax.axis_size(axis)
    up = [(i, i + 1) for i in range(n - 1)]
    return up, [(b, a) for a, b in up]


def per_device(masters, inst_master, inst_orient, owner_map, tile_free, target, spectra, weights):
    row, col = lax.axis_index("row"), lax.axis_index("col")
    core, y, z = row % 2, col // 4, col % 4
    own_cells = lax.dynamic_slice_in_dim(masters, core * 8, 8, 0)
    piece, tile_free_late = lax.optimization_barrier((to_wire(own_cells.astype(BF16)), tile_free))
    group = gathered_near(piece)

    edges = lax.optimization_barrier(
        (
            tile_free_late[:64],
            tile_free_late[SIDE - 64 :],
            tile_free_late[:, :64],
            tile_free_late[:, SIDE - 64 :],
        )
    )
    insts = jnp.stack([inst_master, inst_orient])

    def side(pixels, line):
        packed = jnp.concatenate([pixels[:512], pixels[512:]], 1).astype(BF16)
        lines = jnp.pad(insts[:, :, line].astype(BF16), ((0, 14), (0, 112)))
        return jnp.concatenate([packed, lines], 0)

    up, down = steps("col")
    before = lax.ppermute(side(edges[3], 15), "col", up)
    after = lax.ppermute(side(edges[2], 0), "col", down)

    def ints(a):
        return a.astype(F32).astype(jnp.int32)

    wide_insts = jnp.concatenate(
        [ints(before[512:514, :16])[:, :, None], insts, ints(after[512:514, :16])[:, :, None]], 2
    )

    def strip(pixels, rows, lanes, line):
        full = jnp.concatenate([pixels.astype(BF16), before[rows, lanes], after[rows, lanes]], 1)
        lines = jnp.pad(wide_insts[:, line, :].astype(BF16), ((0, 14), (0, SIDE + 128 - 18)))
        return jnp.concatenate([full, lines], 0)

    top = strip(edges[0], slice(0, 64), slice(0, 64), 0)
    bottom = strip(edges[1], slice(448, 512), slice(64, 128), 15)
    for_near, for_far = jnp.where(core == 0, bottom, top), jnp.where(core == 0, top, bottom)
    parts = gathered_far(group)
    _, for_near, for_far = lax.optimization_barrier((parts[1], for_near, for_far))
    near_strip, far_strip = send(for_near, SWAP), send(for_far, OVER)

    from_near, from_far = ints(near_strip[64:66, :18]), ints(far_strip[64:66, :18])
    above, below = jnp.where(core == 0, from_far, from_near), jnp.where(core == 0, from_near, from_far)
    all_insts = jnp.concatenate([above[:, None, :], wide_insts, below[:, None, :]], 1)
    all_master, all_orient = all_insts[0], all_insts[1]

    matches = all_master[..., None] == jnp.arange(owner_map.shape[0], dtype=jnp.int32)
    slots = jnp.sum(jnp.where(matches, owner_map, 0), axis=-1)
    dy, dz = y ^ (slots // 64), z ^ ((slots // 16) % 4)
    half, entry = (slots // 8) % 2, slots % 8
    high = (dy // 2) + 2 * (dz // 2)
    mixed = (dy // 2 ^ dy % 2) + 2 * (dz // 2 ^ dz % 2)
    outer, inner = jnp.where(half == 0, mixed, high), jnp.where(half == 0, high, mixed)
    locs = (jnp.where(half == core, 0, 1) * 16 + outer * 4 + inner) * 8 + entry
    inside = jnp.stack([row > 0, row < 7, col > 0, col < 15]).astype(jnp.int32)
    codes = jnp.concatenate([locs.reshape(-1), all_orient.reshape(-1), inside, core.reshape(1).astype(jnp.int32)])

    vmem, smem = pl.BlockSpec(memory_space=pltpu.VMEM), pl.BlockSpec(memory_space=pltpu.SMEM)
    anywhere = pl.BlockSpec(memory_space=pl.ANY)
    wide = jax.ShapeDtypeStruct((SIDE, SIDE), F32)
    sums_shape = jax.ShapeDtypeStruct((32, 32, 128), BF16)
    tables = [spectra.reshape(2, BAND, NK * BAND), *constant_tables()]
    resist, free_new, *sums = pl.pallas_call(
        main_kernel,
        out_shape=(wide, wide, *[sums_shape] * 8),
        in_specs=[smem] * 2 + [anywhere] * 8 + [vmem] * 4 + [anywhere] * (2 + len(tables)),
        out_specs=(anywhere, anywhere, *[vmem] * 8),
        scratch_shapes=[
            pltpu.VMEM((512, 32, 128), F32),
            pltpu.VMEM((1152, 1152), BF16),
            pltpu.VMEM((SIDE, SIDE), F32),
            pltpu.VMEM((NK, GRID, 2 * GRID), F32),
            pltpu.VMEM((256, 1024), BF16),
            pltpu.VMEM((512, 1024), BF16),
            pltpu.VMEM((512, 32, 128), F32),
            pltpu.VMEM((SIDE, SIDE), F32),
            pltpu.VMEM((SIDE, SIDE), F32),
            *(pltpu.VMEM(t.shape, t.dtype) for t in tables),
            *[pltpu.VMEM((32, 32, 128), BF16)] * 8,
            pltpu.SemaphoreType.DMA((4,)),
            pltpu.SemaphoreType.DMA((len(tables),)),
            pltpu.SemaphoreType.DMA((1,)),
            pltpu.SemaphoreType.DMA((4,)),
            pltpu.SemaphoreType.DMA((4,)),
            pltpu.SemaphoreType.DMA((8,)),
        ],
        compiler_params=pltpu.CompilerParams(vmem_limit_bytes=52 * 1024 * 1024),
        name="image_and_gradient",
    )(codes, weights, *parts, near_strip, far_strip, before, after, tile_free, target, *tables)

    summed = scattered_sum(sums[:4], sums[4:])
    fresh = smooth(own_cells.reshape(8, CELL, CELL) - 0.05 * from_wire(summed))
    fresh_wire = jnp.concatenate([fresh[:, :32, :], fresh[:, 32:, :]], axis=2).astype(BF16)
    parts = gathered_far(gathered_near(fresh_wire))
    new_mask = pl.pallas_call(
        final_kernel,
        out_shape=wide,
        in_specs=[smem] + [anywhere] * 9,
        out_specs=anywhere,
        scratch_shapes=[
            pltpu.VMEM((512, 32, 128), F32),
            pltpu.VMEM((SIDE, SIDE), F32),
            *[pltpu.VMEM((32, 32, 128), BF16)] * 8,
            *[pltpu.SemaphoreType.DMA((8,))] * 3,
        ],
        compiler_params=pltpu.CompilerParams(vmem_limit_bytes=52 * 1024 * 1024),
        name="final_mask",
    )(codes, *parts, free_new)
    mine = from_wire(parts[0][:8]).reshape(8, CELL * CELL).astype(F32)
    others = from_wire(parts[4][:8]).reshape(8, CELL * CELL).astype(F32)
    masters_out = jnp.where(core == 0, jnp.concatenate([mine, others], 0), jnp.concatenate([others, mine], 0))
    return resist, new_mask, masters_out


def solution(mesh):
    placed = (P("col", None), P(*BOTH), P(*BOTH), P(), P(*BOTH), P(*BOTH), P(), P())
    return jax.shard_map(
        per_device,
        mesh=mesh,
        in_specs=placed,
        out_specs=(P(*BOTH), P(*BOTH), P("col", None)),
        check_vma=False,
    )
```

```python
import functools

import jax
import jax.numpy as jnp
import numpy as np
from jax import lax
from jax.experimental import pallas as pl
from jax.experimental.pallas import tpu as pltpu
from jax.sharding import PartitionSpec as P

TILE, HALO, CELL, BAND, NK, PAD = 512, 64, 64, 128, 8, 640
GRID = 256
SIDE = 1024
BOTH = ("row", "col")
F32, BF16 = jnp.float32, jnp.bfloat16


def waves(positions, period):
    freqs = np.arange(BAND) - BAND // 2
    angles = 2.0 * np.pi * ((freqs[:, None] * positions[None, :]) % period) / period
    return np.cos(angles), np.sin(angles)


def mean_gain(cos, sin):
    rounded = [t.astype(jnp.bfloat16).astype(np.float64) for t in (cos, sin)]
    return (rounded[0] * cos + rounded[1] * sin).mean(1)


@functools.cache
def constant_tables():
    cos_c, sin_c = waves(np.arange(GRID), GRID)
    cos_p, sin_p = waves(np.arange(PAD), PAD)
    cos_i, sin_i = cos_p[:, HALO : HALO + TILE], sin_p[:, HALO : HALO + TILE]
    by_pixel = np.concatenate([cos_p.T, sin_p.T], 1)
    first = np.zeros((2, 768, 256))
    first[0, 0:576] = by_pixel[64:640]
    first[0, 640:704] = by_pixel[0:64]
    first[1, 64:640] = by_pixel[0:576]
    first[1, 704:768] = by_pixel[576:640]
    second = np.concatenate([cos_p, sin_p], 0)
    up_u = np.block([[cos_c.T, -sin_c.T], [sin_c.T, cos_c.T]])
    up_v = np.block([[cos_c, sin_c], [-sin_c, cos_c]])
    places = (HALO + np.arange(TILE)) / PAD
    orders = np.arange(1, BAND)
    shift = places[:, None] - np.arange(GRID)[None, :] / GRID
    fine = (1.0 + 2.0 * np.cos(2 * np.pi * shift[..., None] * orders).sum(-1)) / GRID
    out_v = np.block([[cos_i, -sin_i], [-sin_i, -cos_i]])
    out_u = np.concatenate([cos_i.T, -sin_i.T], 1)
    high = fine.astype(jnp.bfloat16)
    low = (fine - high.astype(np.float64)).astype(jnp.bfloat16)
    cast = lambda a: np.ascontiguousarray(a).astype(jnp.bfloat16)
    gain = mean_gain(cos_i, sin_i) / mean_gain(cos_c, sin_c)
    return [
        np.outer(gain, gain).astype(np.float32), cast(first), cast(second), cast(up_u), cast(up_u.T), cast(up_v), cast(up_v.T),
        high, low, cast(fine.T), cast(low.T), cast(out_v), cast(out_u),
    ]


def dot(a, b):
    return jnp.dot(a, b, preferred_element_type=F32)


def half_lanes():
    return lax.broadcasted_iota(jnp.int32, (8, 128), 1) < 64


def turned(groups, turn_a, turn_b):
    lane = lax.broadcasted_iota(jnp.int32, (8, 128), 1)
    sub = lax.broadcasted_iota(jnp.int32, (8, 128), 0)
    left = half_lanes()
    flip_cols = jnp.where(left, turn_a, turn_b) >= 2
    lanes = jnp.where(flip_cols, jnp.where(left, 63, 191) - lane, lane)
    flip_rows = jnp.where(left, lax.rem(turn_a, 2), lax.rem(turn_b, 2)) == 1
    subs = jnp.where(flip_rows, 7 - sub, sub)
    return [
        jnp.take_along_axis(jnp.take_along_axis(g, subs, axis=0), lanes, axis=1) for g in groups
    ]


def places(loc, turn, right):
    flip = lax.rem(turn, 2)
    upper = (1 - flip) if right else flip
    rows = [pl.ds(pl.multiple_of(8 * i + flip * (8 * (3 - 2 * i)), 8), 8) for i in range(4)]
    return loc + 256 * upper, loc + 256 * (1 - upper), rows


def pair_image(cells, loc_a, turn_a, loc_b, turn_b):
    left = half_lanes()
    top_a, low_a, rows_a = places(loc_a, turn_a, False)
    top_b, low_b, rows_b = places(loc_b, turn_b, True)
    groups = [
        jnp.where(left, cells[a, rows_a[i], :], cells[b, rows_b[i], :])
        for a, b in ((top_a, top_b), (low_a, low_b))
        for i in range(4)
    ]
    return jnp.concatenate(turned(groups, turn_a, turn_b), axis=0)


def fill_cells(parts, cells, loads):
    for n, part in enumerate(parts):
        loads[n].wait()
        value = part[...].astype(F32)
        cells[pl.ds(32 * n, 32)] = value
        cells[pl.ds(256 + 32 * n, 32)] = pltpu.roll(value.reshape(1024, 128), 64, 1).reshape(32, 32, 128)


def main_kernel(*refs):
    codes, weights = refs[0:2]
    part_in = refs[2:10]
    near_strip, far_strip, before, after = refs[10:14]
    free_in, target_in = refs[14:16]
    table_in = refs[16:30]
    resist_out, free_out = refs[30:32]
    sum_outs = refs[32:40]
    cells, mask, shading, fields, amps, halves, sums, free, target = refs[40:49]
    tables = refs[49:63]
    parts = refs[63:71]
    free_sems, table_sems, target_sem, resist_sems, out_sems, part_sems = refs[71:77]
    (spectra, gain, first, second, up_u, up_ut, up_v, up_vt, fine, fine_lo, fine_t, fine_tlo, out_v, out_u) = tables

    part_loads = [pltpu.make_async_copy(a, b, part_sems.at[n]) for n, (a, b) in enumerate(zip(part_in, parts))]
    for load in part_loads:
        load.start()
    loads = [
        pltpu.make_async_copy(free_in.at[pl.ds(256 * n, 256)], free.at[pl.ds(256 * n, 256)], free_sems.at[n])
        for n in range(4)
    ]
    for load in loads:
        load.start()
    table_loads = [pltpu.make_async_copy(a, b, table_sems.at[n]) for n, (a, b) in enumerate(zip(table_in, tables))]
    for load in table_loads:
        load.start()
    target_load = pltpu.make_async_copy(target_in, target, target_sem.at[0])
    target_load.start()

    def code(a, b):
        return codes[a * 18 + b], codes[324 + a * 18 + b]

    fill_cells(parts, cells, part_loads)
    core = codes[652]
    def edge_strip(lanes, own_core):
        return jnp.where(core == own_core, near_strip[0:64, lanes].astype(F32), far_strip[0:64, lanes].astype(F32))

    lane_w = lax.broadcasted_iota(jnp.int32, (64, 128), 1)
    inside_cols = jnp.where(lane_w < 64, codes[650], codes[651]) > 0
    for a, flag, own_core in ((0, 648, 1), (17, 649, 0)):
        for p in range(9):
            cols = slice(p * 128, p * 128 + 128)
            ends = (2 * p + 1, 2 * p + 2) if p < 8 else (0, 17)
            image = pair_image(cells, *code(a, ends[0]), *code(a, ends[1]))
            value = jnp.where(codes[flag] > 0, jnp.tanh(image + edge_strip(cols, own_core)), 0.0)
            if p == 8:
                value = jnp.where(inside_cols, value, 0.0)
            mask[a * 64 : a * 64 + 64, cols] = value.astype(BF16)

    def edge_cols(r, _):
        rows = pl.ds(pl.multiple_of(r * 64, 64), 64)
        left, right = before[rows, :].astype(F32), after[rows, :].astype(F32)
        strips = (
            jnp.where(lane_w < 64, left, pltpu.roll(right, 64, 1)),
            jnp.where(lane_w < 64, pltpu.roll(left, 64, 1), right),
        )
        for n in range(2):
            a = r + 8 * n + 1
            image = pair_image(cells, *code(a, 0), *code(a, 17))
            value = jnp.where(inside_cols, jnp.tanh(image + strips[n]), 0.0)
            mask[pl.ds(pl.multiple_of(a * 64, 64), 64), 1024:1152] = value.astype(BF16)
        return 0

    lax.fori_loop(0, 8, edge_cols, 0, unroll=2)

    def interior(a, _):
        rows = pl.ds(pl.multiple_of(a * 64, 64), 64)
        rows_m = pl.ds(pl.multiple_of(a * 64 + 64, 64), 64)
        for p in range(8):
            cols = slice(p * 128, p * 128 + 128)
            image = pair_image(cells, *code(a + 1, 2 * p + 1), *code(a + 1, 2 * p + 2))
            value = jnp.tanh(image + free[rows, cols])
            shading[rows, cols] = value
            mask[rows_m, cols] = value.astype(BF16)
        return 0

    for n in range(4):
        loads[n].wait()
        lax.fori_loop(4 * n, 4 * n + 4, interior, 0)
    for load in table_loads:
        load.wait()
    target_load.wait()

    def tile(t, _):
        i, j = t // 2, t % 2
        rows_w = pl.ds(pl.multiple_of(i * TILE, 128), PAD)
        window = jnp.concatenate(
            [mask[rows_w, pl.ds(pl.multiple_of(j * 384, 128), 640)], mask[rows_w, 1024:1152]], axis=1
        )
        forw = dot(window, first[j]).astype(BF16)
        spec = dot(second[...], forw)
        scale = gain[...] * (1.0 / PAD)
        spec_re = (spec[:128, :128] + spec[128:, 128:]) * scale
        spec_im = (spec[128:, :128] - spec[:128, 128:]) * scale
        for k in range(NK):
            at = slice(k * 128, k * 128 + 128)
            k_re, k_im = spectra[0, :, at], spectra[1, :, at]
            amps[0:128, at] = (k_re * spec_re - k_im * spec_im).astype(BF16)
            amps[128:256, at] = (k_re * spec_im + k_im * spec_re).astype(BF16)
        half = dot(up_u[...], amps[...]).astype(BF16)
        left = jnp.concatenate(
            [jnp.concatenate([half[0:256, k * 128 : k * 128 + 128], half[256:512, k * 128 : k * 128 + 128]], axis=1) for k in range(NK)],
            axis=0,
        )
        fields[...] = dot(left, up_v[...]).reshape(NK, GRID, 2 * GRID)
        intensity = jnp.zeros((GRID, GRID), F32)
        for k in range(NK):
            at = slice(k * 128, k * 128 + 128)
            re, im = fields[k, :, :256], fields[k, :, 256:]
            intensity = intensity + weights[k] * (re * re + im * im)
        coarse = (intensity * (1.0 / BAND**2)).astype(BF16)
        half_fine = dot(fine[...], coarse) + dot(fine_lo[...], coarse)
        half_fine = half_fine.astype(BF16)
        image = dot(half_fine, fine_t[...]) + dot(half_fine, fine_tlo[...])
        rows_t = pl.ds(pl.multiple_of(i * TILE, TILE), TILE)
        cols_t = pl.ds(pl.multiple_of(j * TILE, TILE), TILE)
        resist = jax.nn.sigmoid(2.0 * (image - 1.8))
        slopes = (4.0 * (resist - target[rows_t, cols_t]) * resist * (1.0 - resist)).astype(BF16)
        target[rows_t, cols_t] = resist
        pltpu.make_async_copy(
            target.at[rows_t, cols_t], resist_out.at[rows_t, cols_t], resist_sems.at[t]
        ).start()
        back = dot(fine_t[...], dot(slopes, fine[...]).astype(BF16))
        for k in range(NK):
            at = slice(k * 128, k * 128 + 128)
            scaled = back * (weights[k] * (2.0 / BAND**2))
            both = jnp.concatenate(
                [(scaled * fields[k, :, :256]).astype(BF16), (scaled * fields[k, :, 256:]).astype(BF16)], axis=1
            )
            low = dot(both, up_vt[...]).astype(BF16)
            halves[0:256, at] = low[:, :128]
            halves[256:512, at] = low[:, 128:]
        bspec_re = jnp.zeros((128, 128), F32)
        bspec_im = jnp.zeros((128, 128), F32)
        bamp = dot(up_ut[...], halves[...])
        for k in range(NK):
            at = slice(k * 128, k * 128 + 128)
            k_re, k_im = spectra[0, :, at], spectra[1, :, at]
            re, im = bamp[:128, at], bamp[128:, at]
            bspec_re = bspec_re + (k_re * re + k_im * im)
            bspec_im = bspec_im + (k_re * im - k_im * re)
        bspec = jnp.concatenate([bspec_re * scale, bspec_im * scale], axis=1)
        bforw = dot(bspec.astype(BF16), out_v[...]).astype(BF16)
        stacked = jnp.concatenate([bforw[:, :TILE], bforw[:, TILE:]], axis=0)
        gradient = dot(out_u[...], stacked)
        shade = shading[rows_t, cols_t]
        grad = gradient * (1.0 - shade * shade)
        shading[rows_t, cols_t] = grad
        free[rows_t, cols_t] = free[rows_t, cols_t] - grad
        pltpu.make_async_copy(free.at[rows_t, cols_t], free_out.at[rows_t, cols_t], out_sems.at[t]).start()
        return 0

    lax.fori_loop(0, 4, tile, 0)

    def clear(n, _):
        sums[pl.ds(n * 8, 8)] = jnp.zeros((8, 32, 128), F32)
        return 0

    lax.fori_loop(0, 64, clear, 0)

    def collect(a, _):
        rows = pl.multiple_of(a * 64, 64)
        left = half_lanes()
        for p in range(8):
            cols = slice(p * 128, p * 128 + 128)
            loc_a, turn_a = code(a + 1, 2 * p + 1)
            loc_b, turn_b = code(a + 1, 2 * p + 2)
            groups = turned([shading[pl.ds(rows + 8 * i, 8), cols] for i in range(8)], turn_a, turn_b)
            for loc, turn, right, keep in ((loc_a, turn_a, False, left), (loc_b, turn_b, True, ~left)):
                top, low, at = places(loc, turn, right)
                spots = [(top, at[i]) for i in range(4)] + [(low, at[i]) for i in range(4)]
                totals = [sums[n, r, :] + jnp.where(keep, g, 0.0) for (n, r), g in zip(spots, groups)]
                for (n, r), total in zip(spots, totals):
                    sums[n, r, :] = total
        return 0

    lax.fori_loop(0, 16, collect, 0)
    for part, out in enumerate(sum_outs):

        def join(n, _):
            at = part * 32 + n * 8
            rolled = pltpu.roll(sums[pl.ds(256 + at, 8)].reshape(256, 128), 64, 1)
            out[pl.ds(n * 8, 8)] = (sums[pl.ds(at, 8)].reshape(256, 128) + rolled).reshape(8, 32, 128).astype(BF16)
            return 0

        lax.fori_loop(0, 4, join, 0)

    for t in range(4):
        at = (pl.ds(t // 2 * TILE, TILE), pl.ds(t % 2 * TILE, TILE))
        pltpu.make_async_copy(target.at[at], resist_out.at[at], resist_sems.at[t]).wait()
        pltpu.make_async_copy(free.at[at], free_out.at[at], out_sems.at[t]).wait()


def final_kernel(*refs):
    codes = refs[0]
    part_in, (free_in, out), cells, free = refs[1:9], refs[9:11], refs[11], refs[12]
    parts, (part_sems, free_sems, out_sems) = refs[13:21], refs[21:24]
    part_loads = [pltpu.make_async_copy(a, b, part_sems.at[n]) for n, (a, b) in enumerate(zip(part_in, parts))]
    strips = [pl.ds(128 * n, 128) for n in range(8)]
    loads = [pltpu.make_async_copy(free_in.at[r], free.at[r], free_sems.at[n]) for n, r in enumerate(strips)]
    stores = [pltpu.make_async_copy(free.at[r], out.at[r], out_sems.at[n]) for n, r in enumerate(strips)]
    for load in part_loads + loads:
        load.start()
    fill_cells(parts, cells, part_loads)

    def interior(a, _):
        rows = pl.ds(pl.multiple_of(a * 64, 64), 64)
        for p in range(8):
            cols = slice(p * 128, p * 128 + 128)
            at = (a + 1) * 18 + 2 * p
            image = pair_image(cells, codes[at + 1], codes[325 + at], codes[at + 2], codes[326 + at])
            free[rows, cols] = jnp.tanh(image + free[rows, cols])
        return 0

    for n in range(8):
        loads[n].wait()
        lax.fori_loop(2 * n, 2 * n + 2, interior, 0)
        stores[n].start()
    for store in stores:
        store.wait()


def flat(x, c, y, z):
    return ((x % 4) * 2 + c) * 16 + (y % 4) * 4 + z % 4


CHIPS = [(x, y, z) for x in range(4) for y in range(4) for z in range(4)]


def mirrored(n, masks):
    return [
        (flat(x, c, y, z), flat(x, c, y ^ (masks[c] * (n % 2)), z ^ (masks[c] * (n // 2))))
        for x, y, z in CHIPS
        for c in range(2)
    ]


def near(n):
    return mirrored(n, (3, 1))


def far(n):
    return mirrored(n, (1, 3))


def shift_x(d):
    return [(flat(x, c, y, z), flat(x + d, c, y, z)) for x, y, z in CHIPS for c in range(2)]


SWAP = [(flat(x, c, y, z), flat(x, 1 - c, y, z)) for x, y, z in CHIPS for c in range(2)]


OVER = [(flat(x, 0, y, z), flat(x - 1, 1, y, z)) for x, y, z in CHIPS if x > 0] + [
    (flat(x, 1, y, z), flat(x + 1, 0, y, z)) for x, y, z in CHIPS if x < 3
]


def send(value, pairs):
    return lax.ppermute(value, BOTH, pairs)


def gathered_near(piece):
    got = [send(piece, near(n)) for n in (3, 1, 2)]
    return jnp.concatenate([piece, got[1], got[2], got[0]], axis=0)


def gathered_far(group):
    got = [send(group, far(n)) for n in (3, 1, 2)]
    mine = [group, got[1], got[2], got[0]]
    return mine + [send(part, SWAP) for part in mine]


def scattered_sum(own, other):
    swapped = {n: send(other[n], SWAP) for n in (3, 1, 2, 0)}
    total = {n: (own[n].astype(F32) + swapped[n].astype(F32)).astype(BF16) for n in (3, 1, 2, 0)}
    got = [send(total[n], far(n)) for n in (3, 1, 2)]
    total = sum((g.astype(F32) for g in got), total[0].astype(F32)).astype(BF16).reshape(4, 8, 32, 128)
    got = [send(total[n], near(n)) for n in (3, 1, 2)]
    total = sum((g.astype(F32) for g in got), total[0].astype(F32)).astype(BF16)
    got = [send(total, shift_x(d)) for d in (2, 1, 3)]
    return sum((g.astype(F32) for g in got), total.astype(F32))


def to_wire(rows):
    cells = rows.reshape(-1, CELL, CELL)
    return jnp.concatenate([cells[:, :32, :], cells[:, 32:, :]], axis=2)


def from_wire(wire):
    return jnp.concatenate([wire[:, :, :64], wire[:, :, 64:]], axis=1)


def smooth(grids):
    framed = jnp.pad(grids, ((0, 0), (1, 1), (1, 1)))
    beside = framed[:, 2:, 1:-1] + framed[:, :-2, 1:-1] + framed[:, 1:-1, 2:] + framed[:, 1:-1, :-2]
    return 0.5 * grids + 0.125 * beside


def steps(axis):
    n = lax.axis_size(axis)
    up = [(i, i + 1) for i in range(n - 1)]
    return up, [(b, a) for a, b in up]


def per_device(masters, inst_master, inst_orient, owner_map, tile_free, target, spectra, weights):
    row, col = lax.axis_index("row"), lax.axis_index("col")
    core, y, z = row % 2, col // 4, col % 4
    own_cells = lax.dynamic_slice_in_dim(masters, core * 8, 8, 0)
    piece, tile_free_late = lax.optimization_barrier((to_wire(own_cells.astype(BF16)), tile_free))
    group = gathered_near(piece)

    edges = lax.optimization_barrier(
        (
            tile_free_late[:64],
            tile_free_late[SIDE - 64 :],
            tile_free_late[:, :64],
            tile_free_late[:, SIDE - 64 :],
        )
    )
    insts = jnp.stack([inst_master, inst_orient])

    def side(pixels, line):
        packed = jnp.concatenate([pixels[:512], pixels[512:]], 1).astype(BF16)
        lines = jnp.pad(insts[:, :, line].astype(BF16), ((0, 14), (0, 112)))
        return jnp.concatenate([packed, lines], 0)

    up, down = steps("col")
    before = lax.ppermute(side(edges[3], 15), "col", up)
    after = lax.ppermute(side(edges[2], 0), "col", down)

    def ints(a):
        return a.astype(F32).astype(jnp.int32)

    wide_insts = jnp.concatenate(
        [ints(before[512:514, :16])[:, :, None], insts, ints(after[512:514, :16])[:, :, None]], 2
    )

    def strip(pixels, rows, lanes, line):
        full = jnp.concatenate([pixels.astype(BF16), before[rows, lanes], after[rows, lanes]], 1)
        lines = jnp.pad(wide_insts[:, line, :].astype(BF16), ((0, 14), (0, SIDE + 128 - 18)))
        return jnp.concatenate([full, lines], 0)

    top = strip(edges[0], slice(0, 64), slice(0, 64), 0)
    bottom = strip(edges[1], slice(448, 512), slice(64, 128), 15)
    for_near, for_far = jnp.where(core == 0, bottom, top), jnp.where(core == 0, top, bottom)
    parts = gathered_far(group)
    _, for_near, for_far = lax.optimization_barrier((parts[1], for_near, for_far))
    near_strip, far_strip = send(for_near, SWAP), send(for_far, OVER)

    from_near, from_far = ints(near_strip[64:66, :18]), ints(far_strip[64:66, :18])
    above, below = jnp.where(core == 0, from_far, from_near), jnp.where(core == 0, from_near, from_far)
    all_insts = jnp.concatenate([above[:, None, :], wide_insts, below[:, None, :]], 1)
    all_master, all_orient = all_insts[0], all_insts[1]

    matches = all_master[..., None] == jnp.arange(owner_map.shape[0], dtype=jnp.int32)
    slots = jnp.sum(jnp.where(matches, owner_map, 0), axis=-1)
    dy, dz = y ^ (slots // 64), z ^ ((slots // 16) % 4)
    half, entry = (slots // 8) % 2, slots % 8
    high = (dy // 2) + 2 * (dz // 2)
    mixed = (dy // 2 ^ dy % 2) + 2 * (dz // 2 ^ dz % 2)
    outer, inner = jnp.where(half == 0, mixed, high), jnp.where(half == 0, high, mixed)
    locs = (jnp.where(half == core, 0, 1) * 16 + outer * 4 + inner) * 8 + entry
    inside = jnp.stack([row > 0, row < 7, col > 0, col < 15]).astype(jnp.int32)
    codes = jnp.concatenate([locs.reshape(-1), all_orient.reshape(-1), inside, core.reshape(1).astype(jnp.int32)])

    vmem, smem = pl.BlockSpec(memory_space=pltpu.VMEM), pl.BlockSpec(memory_space=pltpu.SMEM)
    anywhere = pl.BlockSpec(memory_space=pl.ANY)
    wide = jax.ShapeDtypeStruct((SIDE, SIDE), F32)
    sums_shape = jax.ShapeDtypeStruct((32, 32, 128), BF16)
    tables = [spectra.reshape(2, BAND, NK * BAND), *constant_tables()]
    resist, free_new, *sums = pl.pallas_call(
        main_kernel,
        out_shape=(wide, wide, *[sums_shape] * 8),
        in_specs=[smem] * 2 + [anywhere] * 8 + [vmem] * 4 + [anywhere] * (2 + len(tables)),
        out_specs=(anywhere, anywhere, *[vmem] * 8),
        scratch_shapes=[
            pltpu.VMEM((512, 32, 128), F32),
            pltpu.VMEM((1152, 1152), BF16),
            pltpu.VMEM((SIDE, SIDE), F32),
            pltpu.VMEM((NK, GRID, 2 * GRID), F32),
            pltpu.VMEM((256, 1024), BF16),
            pltpu.VMEM((512, 1024), BF16),
            pltpu.VMEM((512, 32, 128), F32),
            pltpu.VMEM((SIDE, SIDE), F32),
            pltpu.VMEM((SIDE, SIDE), F32),
            *(pltpu.VMEM(t.shape, t.dtype) for t in tables),
            *[pltpu.VMEM((32, 32, 128), BF16)] * 8,
            pltpu.SemaphoreType.DMA((4,)),
            pltpu.SemaphoreType.DMA((len(tables),)),
            pltpu.SemaphoreType.DMA((1,)),
            pltpu.SemaphoreType.DMA((4,)),
            pltpu.SemaphoreType.DMA((4,)),
            pltpu.SemaphoreType.DMA((8,)),
        ],
        compiler_params=pltpu.CompilerParams(vmem_limit_bytes=52 * 1024 * 1024),
        name="image_and_gradient",
    )(codes, weights, *parts, near_strip, far_strip, before, after, tile_free, target, *tables)

    summed = scattered_sum(sums[:4], sums[4:])
    fresh = smooth(own_cells.reshape(8, CELL, CELL) - 0.05 * from_wire(summed))
    fresh_wire = jnp.concatenate([fresh[:, :32, :], fresh[:, 32:, :]], axis=2).astype(BF16)
    parts = gathered_far(gathered_near(fresh_wire))
    new_mask = pl.pallas_call(
        final_kernel,
        out_shape=wide,
        in_specs=[smem] + [anywhere] * 9,
        out_specs=anywhere,
        scratch_shapes=[
            pltpu.VMEM((512, 32, 128), F32),
            pltpu.VMEM((SIDE, SIDE), F32),
            *[pltpu.VMEM((32, 32, 128), BF16)] * 8,
            *[pltpu.SemaphoreType.DMA((8,))] * 3,
        ],
        compiler_params=pltpu.CompilerParams(vmem_limit_bytes=52 * 1024 * 1024),
        name="final_mask",
    )(codes, *parts, free_new)
    mine = from_wire(parts[0][:8]).reshape(8, CELL * CELL).astype(F32)
    others = from_wire(parts[4][:8]).reshape(8, CELL * CELL).astype(F32)
    masters_out = jnp.where(core == 0, jnp.concatenate([mine, others], 0), jnp.concatenate([others, mine], 0))
    return resist, new_mask, masters_out


def solution(mesh):
    placed = (P("col", None), P(*BOTH), P(*BOTH), P(), P(*BOTH), P(*BOTH), P(), P())
    return jax.shard_map(
        per_device,
        mesh=mesh,
        in_specs=placed,
        out_specs=(P(*BOTH), P(*BOTH), P("col", None)),
        check_vma=False,
    )
```

```python
import functools

import jax
import jax.numpy as jnp
import numpy as np
from jax import lax
from jax.experimental import pallas as pl
from jax.experimental.pallas import tpu as pltpu
from jax.sharding import PartitionSpec as P

TILE, HALO, CELL, BAND, NK, PAD = 512, 64, 64, 128, 8, 640
GRID = 256
SIDE = 1024
BOTH = ("row", "col")
F32, BF16 = jnp.float32, jnp.bfloat16


def waves(positions, period):
    freqs = np.arange(BAND) - BAND // 2
    angles = 2.0 * np.pi * ((freqs[:, None] * positions[None, :]) % period) / period
    return np.cos(angles), np.sin(angles)


def mean_gain(cos, sin):
    rounded = [t.astype(jnp.bfloat16).astype(np.float64) for t in (cos, sin)]
    return (rounded[0] * cos + rounded[1] * sin).mean(1)


@functools.cache
def constant_tables():
    cos_c, sin_c = waves(np.arange(GRID), GRID)
    cos_p, sin_p = waves(np.arange(PAD), PAD)
    cos_i, sin_i = cos_p[:, HALO : HALO + TILE], sin_p[:, HALO : HALO + TILE]
    by_pixel = np.concatenate([cos_p.T, sin_p.T], 1)
    first = np.zeros((2, 768, 256))
    first[0, 0:576] = by_pixel[64:640]
    first[0, 640:704] = by_pixel[0:64]
    first[1, 64:640] = by_pixel[0:576]
    first[1, 704:768] = by_pixel[576:640]
    second = np.concatenate([cos_p, sin_p], 0)
    up_u = np.block([[cos_c.T, -sin_c.T], [sin_c.T, cos_c.T]])
    up_v = np.block([[cos_c, sin_c], [-sin_c, cos_c]])
    places = (HALO + np.arange(TILE)) / PAD
    orders = np.arange(1, BAND)
    shift = places[:, None] - np.arange(GRID)[None, :] / GRID
    fine = (1.0 + 2.0 * np.cos(2 * np.pi * shift[..., None] * orders).sum(-1)) / GRID
    out_v = np.block([[cos_i, -sin_i], [-sin_i, -cos_i]])
    out_u = np.concatenate([cos_i.T, -sin_i.T], 1)
    high = fine.astype(jnp.bfloat16)
    low = (fine - high.astype(np.float64)).astype(jnp.bfloat16)
    cast = lambda a: np.ascontiguousarray(a).astype(jnp.bfloat16)
    gain = mean_gain(cos_i, sin_i) / mean_gain(cos_c, sin_c)
    return [
        np.outer(gain, gain).astype(np.float32), cast(first), cast(second), cast(up_u), cast(up_u.T), cast(up_v), cast(up_v.T),
        high, low, cast(fine.T), cast(low.T), cast(out_v), cast(out_u),
    ]


def dot(a, b):
    return jnp.dot(a, b, preferred_element_type=F32)


def half_lanes():
    return lax.broadcasted_iota(jnp.int32, (8, 128), 1) < 64


def turned(groups, turn_a, turn_b):
    lane = lax.broadcasted_iota(jnp.int32, (8, 128), 1)
    sub = lax.broadcasted_iota(jnp.int32, (8, 128), 0)
    left = half_lanes()
    flip_cols = jnp.where(left, turn_a, turn_b) >= 2
    lanes = jnp.where(flip_cols, jnp.where(left, 63, 191) - lane, lane)
    flip_rows = jnp.where(left, lax.rem(turn_a, 2), lax.rem(turn_b, 2)) == 1
    subs = jnp.where(flip_rows, 7 - sub, sub)
    return [
        jnp.take_along_axis(jnp.take_along_axis(g, subs, axis=0), lanes, axis=1) for g in groups
    ]


def places(loc, turn, right):
    flip = lax.rem(turn, 2)
    upper = (1 - flip) if right else flip
    rows = [pl.ds(pl.multiple_of(8 * i + flip * (8 * (3 - 2 * i)), 8), 8) for i in range(4)]
    return loc + 256 * upper, loc + 256 * (1 - upper), rows


def pair_image(cells, loc_a, turn_a, loc_b, turn_b):
    left = half_lanes()
    top_a, low_a, rows_a = places(loc_a, turn_a, False)
    top_b, low_b, rows_b = places(loc_b, turn_b, True)
    groups = [
        jnp.where(left, cells[a, rows_a[i], :], cells[b, rows_b[i], :])
        for a, b in ((top_a, top_b), (low_a, low_b))
        for i in range(4)
    ]
    return jnp.concatenate(turned(groups, turn_a, turn_b), axis=0)


def fill_cells(parts, cells, loads):
    for n, part in enumerate(parts):
        loads[n].wait()
        value = part[...].astype(F32)
        cells[pl.ds(32 * n, 32)] = value
        cells[pl.ds(256 + 32 * n, 32)] = pltpu.roll(value.reshape(1024, 128), 64, 1).reshape(32, 32, 128)


def main_kernel(*refs):
    codes, weights = refs[0:2]
    part_in = refs[2:10]
    near_strip, far_strip, before, after = refs[10:14]
    free_in, target_in = refs[14:16]
    table_in = refs[16:30]
    resist_out, free_out = refs[30:32]
    sum_outs = refs[32:40]
    cells, mask, shading, fields, amps, halves, sums, free, target = refs[40:49]
    tables = refs[49:63]
    parts = refs[63:71]
    free_sems, table_sems, target_sem, resist_sems, out_sems, part_sems = refs[71:77]
    (spectra, gain, first, second, up_u, up_ut, up_v, up_vt, fine, fine_lo, fine_t, fine_tlo, out_v, out_u) = tables

    part_loads = [pltpu.make_async_copy(a, b, part_sems.at[n]) for n, (a, b) in enumerate(zip(part_in, parts))]
    for load in part_loads:
        load.start()
    loads = [
        pltpu.make_async_copy(free_in.at[pl.ds(256 * n, 256)], free.at[pl.ds(256 * n, 256)], free_sems.at[n])
        for n in range(4)
    ]
    for load in loads:
        load.start()
    table_loads = [pltpu.make_async_copy(a, b, table_sems.at[n]) for n, (a, b) in enumerate(zip(table_in, tables))]
    for load in table_loads:
        load.start()
    target_load = pltpu.make_async_copy(target_in, target, target_sem.at[0])
    target_load.start()

    def code(a, b):
        return codes[a * 18 + b], codes[324 + a * 18 + b]

    fill_cells(parts, cells, part_loads)
    core = codes[652]
    def edge_strip(lanes, own_core):
        return jnp.where(core == own_core, near_strip[0:64, lanes].astype(F32), far_strip[0:64, lanes].astype(F32))

    lane_w = lax.broadcasted_iota(jnp.int32, (64, 128), 1)
    inside_cols = jnp.where(lane_w < 64, codes[650], codes[651]) > 0
    for a, flag, own_core in ((0, 648, 1), (17, 649, 0)):
        for p in range(9):
            cols = slice(p * 128, p * 128 + 128)
            ends = (2 * p + 1, 2 * p + 2) if p < 8 else (0, 17)
            image = pair_image(cells, *code(a, ends[0]), *code(a, ends[1]))
            value = jnp.where(codes[flag] > 0, jnp.tanh(image + edge_strip(cols, own_core)), 0.0)
            if p == 8:
                value = jnp.where(inside_cols, value, 0.0)
            mask[a * 64 : a * 64 + 64, cols] = value.astype(BF16)

    def edge_cols(r, _):
        rows = pl.ds(pl.multiple_of(r * 64, 64), 64)
        left, right = before[rows, :].astype(F32), after[rows, :].astype(F32)
        strips = (
            jnp.where(lane_w < 64, left, pltpu.roll(right, 64, 1)),
            jnp.where(lane_w < 64, pltpu.roll(left, 64, 1), right),
        )
        for n in range(2):
            a = r + 8 * n + 1
            image = pair_image(cells, *code(a, 0), *code(a, 17))
            value = jnp.where(inside_cols, jnp.tanh(image + strips[n]), 0.0)
            mask[pl.ds(pl.multiple_of(a * 64, 64), 64), 1024:1152] = value.astype(BF16)
        return 0

    lax.fori_loop(0, 8, edge_cols, 0, unroll=2)

    def interior(a, _):
        rows = pl.ds(pl.multiple_of(a * 64, 64), 64)
        rows_m = pl.ds(pl.multiple_of(a * 64 + 64, 64), 64)
        for p in range(8):
            cols = slice(p * 128, p * 128 + 128)
            image = pair_image(cells, *code(a + 1, 2 * p + 1), *code(a + 1, 2 * p + 2))
            value = jnp.tanh(image + free[rows, cols])
            shading[rows, cols] = value
            mask[rows_m, cols] = value.astype(BF16)
        return 0

    for n in range(4):
        loads[n].wait()
        lax.fori_loop(4 * n, 4 * n + 4, interior, 0)
    for load in table_loads:
        load.wait()
    target_load.wait()

    def tile(t, _):
        i, j = t // 2, t % 2
        rows_w = pl.ds(pl.multiple_of(i * TILE, 128), PAD)
        window = jnp.concatenate(
            [mask[rows_w, pl.ds(pl.multiple_of(j * 384, 128), 640)], mask[rows_w, 1024:1152]], axis=1
        )
        forw = dot(window, first[j]).astype(BF16)
        spec = dot(second[...], forw)
        scale = gain[...] * (1.0 / PAD)
        spec_re = (spec[:128, :128] + spec[128:, 128:]) * scale
        spec_im = (spec[128:, :128] - spec[:128, 128:]) * scale
        for k in range(NK):
            at = slice(k * 128, k * 128 + 128)
            k_re, k_im = spectra[0, :, at], spectra[1, :, at]
            amps[0:128, at] = (k_re * spec_re - k_im * spec_im).astype(BF16)
            amps[128:256, at] = (k_re * spec_im + k_im * spec_re).astype(BF16)
        half = dot(up_u[...], amps[...]).astype(BF16)
        left = jnp.concatenate(
            [jnp.concatenate([half[0:256, k * 128 : k * 128 + 128], half[256:512, k * 128 : k * 128 + 128]], axis=1) for k in range(NK)],
            axis=0,
        )
        fields[...] = dot(left, up_v[...]).reshape(NK, GRID, 2 * GRID)
        intensity = jnp.zeros((GRID, GRID), F32)
        for k in range(NK):
            at = slice(k * 128, k * 128 + 128)
            re, im = fields[k, :, :256], fields[k, :, 256:]
            intensity = intensity + weights[k] * (re * re + im * im)
        coarse = (intensity * (1.0 / BAND**2)).astype(BF16)
        half_fine = dot(fine[...], coarse) + dot(fine_lo[...], coarse)
        half_fine = half_fine.astype(BF16)
        image = dot(half_fine, fine_t[...]) + dot(half_fine, fine_tlo[...])
        rows_t = pl.ds(pl.multiple_of(i * TILE, TILE), TILE)
        cols_t = pl.ds(pl.multiple_of(j * TILE, TILE), TILE)
        bend = jnp.tanh(image - 1.8)
        resist = 0.5 + 0.5 * bend
        slopes = ((resist - target[rows_t, cols_t]) * (1.0 - bend * bend)).astype(BF16)
        target[rows_t, cols_t] = resist
        pltpu.make_async_copy(
            target.at[rows_t, cols_t], resist_out.at[rows_t, cols_t], resist_sems.at[t]
        ).start()
        back = dot(fine_t[...], dot(slopes, fine[...]).astype(BF16))
        for k in range(NK):
            at = slice(k * 128, k * 128 + 128)
            scaled = back * (weights[k] * (2.0 / BAND**2))
            both = jnp.concatenate(
                [(scaled * fields[k, :, :256]).astype(BF16), (scaled * fields[k, :, 256:]).astype(BF16)], axis=1
            )
            low = dot(both, up_vt[...]).astype(BF16)
            halves[0:256, at] = low[:, :128]
            halves[256:512, at] = low[:, 128:]
        bspec_re = jnp.zeros((128, 128), F32)
        bspec_im = jnp.zeros((128, 128), F32)
        bamp = dot(up_ut[...], halves[...])
        for k in range(NK):
            at = slice(k * 128, k * 128 + 128)
            k_re, k_im = spectra[0, :, at], spectra[1, :, at]
            re, im = bamp[:128, at], bamp[128:, at]
            bspec_re = bspec_re + (k_re * re + k_im * im)
            bspec_im = bspec_im + (k_re * im - k_im * re)
        bspec = jnp.concatenate([bspec_re * scale, bspec_im * scale], axis=1)
        bforw = dot(bspec.astype(BF16), out_v[...]).astype(BF16)
        stacked = jnp.concatenate([bforw[:, :TILE], bforw[:, TILE:]], axis=0)
        gradient = dot(out_u[...], stacked)
        shade = shading[rows_t, cols_t]
        grad = gradient * (1.0 - shade * shade)
        shading[rows_t, cols_t] = grad
        free[rows_t, cols_t] = free[rows_t, cols_t] - grad
        pltpu.make_async_copy(free.at[rows_t, cols_t], free_out.at[rows_t, cols_t], out_sems.at[t]).start()
        return 0

    lax.fori_loop(0, 4, tile, 0)

    def clear(n, _):
        sums[pl.ds(n * 8, 8)] = jnp.zeros((8, 32, 128), F32)
        return 0

    lax.fori_loop(0, 64, clear, 0)

    def collect(a, _):
        rows = pl.multiple_of(a * 64, 64)
        left = half_lanes()
        for p in range(8):
            cols = slice(p * 128, p * 128 + 128)
            loc_a, turn_a = code(a + 1, 2 * p + 1)
            loc_b, turn_b = code(a + 1, 2 * p + 2)
            groups = turned([shading[pl.ds(rows + 8 * i, 8), cols] for i in range(8)], turn_a, turn_b)
            for loc, turn, right, keep in ((loc_a, turn_a, False, left), (loc_b, turn_b, True, ~left)):
                top, low, at = places(loc, turn, right)
                spots = [(top, at[i]) for i in range(4)] + [(low, at[i]) for i in range(4)]
                totals = [sums[n, r, :] + jnp.where(keep, g, 0.0) for (n, r), g in zip(spots, groups)]
                for (n, r), total in zip(spots, totals):
                    sums[n, r, :] = total
        return 0

    lax.fori_loop(0, 16, collect, 0)
    for part, out in enumerate(sum_outs):

        def join(n, _):
            at = part * 32 + n * 8
            rolled = pltpu.roll(sums[pl.ds(256 + at, 8)].reshape(256, 128), 64, 1)
            out[pl.ds(n * 8, 8)] = (sums[pl.ds(at, 8)].reshape(256, 128) + rolled).reshape(8, 32, 128).astype(BF16)
            return 0

        lax.fori_loop(0, 4, join, 0)

    for t in range(4):
        at = (pl.ds(t // 2 * TILE, TILE), pl.ds(t % 2 * TILE, TILE))
        pltpu.make_async_copy(target.at[at], resist_out.at[at], resist_sems.at[t]).wait()
        pltpu.make_async_copy(free.at[at], free_out.at[at], out_sems.at[t]).wait()


def final_kernel(*refs):
    codes = refs[0]
    part_in, (free_in, out), cells, free = refs[1:9], refs[9:11], refs[11], refs[12]
    parts, (part_sems, free_sems, out_sems) = refs[13:21], refs[21:24]
    part_loads = [pltpu.make_async_copy(a, b, part_sems.at[n]) for n, (a, b) in enumerate(zip(part_in, parts))]
    strips = [pl.ds(128 * n, 128) for n in range(8)]
    loads = [pltpu.make_async_copy(free_in.at[r], free.at[r], free_sems.at[n]) for n, r in enumerate(strips)]
    stores = [pltpu.make_async_copy(free.at[r], out.at[r], out_sems.at[n]) for n, r in enumerate(strips)]
    for load in part_loads + loads:
        load.start()
    fill_cells(parts, cells, part_loads)

    def interior(a, _):
        rows = pl.ds(pl.multiple_of(a * 64, 64), 64)
        for p in range(8):
            cols = slice(p * 128, p * 128 + 128)
            at = (a + 1) * 18 + 2 * p
            image = pair_image(cells, codes[at + 1], codes[325 + at], codes[at + 2], codes[326 + at])
            free[rows, cols] = jnp.tanh(image + free[rows, cols])
        return 0

    for n in range(8):
        loads[n].wait()
        lax.fori_loop(2 * n, 2 * n + 2, interior, 0)
        stores[n].start()
    for store in stores:
        store.wait()


def flat(x, c, y, z):
    return ((x % 4) * 2 + c) * 16 + (y % 4) * 4 + z % 4


CHIPS = [(x, y, z) for x in range(4) for y in range(4) for z in range(4)]


def mirrored(n, masks):
    return [
        (flat(x, c, y, z), flat(x, c, y ^ (masks[c] * (n % 2)), z ^ (masks[c] * (n // 2))))
        for x, y, z in CHIPS
        for c in range(2)
    ]


def near(n):
    return mirrored(n, (3, 1))


def far(n):
    return mirrored(n, (1, 3))


def shift_x(d):
    return [(flat(x, c, y, z), flat(x + d, c, y, z)) for x, y, z in CHIPS for c in range(2)]


SWAP = [(flat(x, c, y, z), flat(x, 1 - c, y, z)) for x, y, z in CHIPS for c in range(2)]


OVER = [(flat(x, 0, y, z), flat(x - 1, 1, y, z)) for x, y, z in CHIPS if x > 0] + [
    (flat(x, 1, y, z), flat(x + 1, 0, y, z)) for x, y, z in CHIPS if x < 3
]


def send(value, pairs):
    return lax.ppermute(value, BOTH, pairs)


def gathered_near(piece):
    got = [send(piece, near(n)) for n in (3, 1, 2)]
    return jnp.concatenate([piece, got[1], got[2], got[0]], axis=0)


def gathered_far(group):
    got = [send(group, far(n)) for n in (3, 1, 2)]
    mine = [group, got[1], got[2], got[0]]
    return mine + [send(part, SWAP) for part in mine]


def scattered_sum(own, other):
    swapped = {n: send(other[n], SWAP) for n in (3, 1, 2, 0)}
    total = {n: (own[n].astype(F32) + swapped[n].astype(F32)).astype(BF16) for n in (3, 1, 2, 0)}
    got = [send(total[n], far(n)) for n in (3, 1, 2)]
    total = sum((g.astype(F32) for g in got), total[0].astype(F32)).astype(BF16).reshape(4, 8, 32, 128)
    got = [send(total[n], near(n)) for n in (3, 1, 2)]
    total = sum((g.astype(F32) for g in got), total[0].astype(F32)).astype(BF16)
    got = [send(total, shift_x(d)) for d in (2, 1, 3)]
    return sum((g.astype(F32) for g in got), total.astype(F32))


def to_wire(rows):
    cells = rows.reshape(-1, CELL, CELL)
    return jnp.concatenate([cells[:, :32, :], cells[:, 32:, :]], axis=2)


def from_wire(wire):
    return jnp.concatenate([wire[:, :, :64], wire[:, :, 64:]], axis=1)


def smooth(grids):
    framed = jnp.pad(grids, ((0, 0), (1, 1), (1, 1)))
    beside = framed[:, 2:, 1:-1] + framed[:, :-2, 1:-1] + framed[:, 1:-1, 2:] + framed[:, 1:-1, :-2]
    return 0.5 * grids + 0.125 * beside


def steps(axis):
    n = lax.axis_size(axis)
    up = [(i, i + 1) for i in range(n - 1)]
    return up, [(b, a) for a, b in up]


def per_device(masters, inst_master, inst_orient, owner_map, tile_free, target, spectra, weights):
    row, col = lax.axis_index("row"), lax.axis_index("col")
    core, y, z = row % 2, col // 4, col % 4
    own_cells = lax.dynamic_slice_in_dim(masters, core * 8, 8, 0)
    piece, tile_free_late = lax.optimization_barrier((to_wire(own_cells.astype(BF16)), tile_free))
    group = gathered_near(piece)

    edges = lax.optimization_barrier(
        (
            tile_free_late[:64],
            tile_free_late[SIDE - 64 :],
            tile_free_late[:, :64],
            tile_free_late[:, SIDE - 64 :],
        )
    )
    insts = jnp.stack([inst_master, inst_orient])

    def side(pixels, line):
        packed = jnp.concatenate([pixels[:512], pixels[512:]], 1).astype(BF16)
        lines = jnp.pad(insts[:, :, line].astype(BF16), ((0, 14), (0, 112)))
        return jnp.concatenate([packed, lines], 0)

    up, down = steps("col")
    before = lax.ppermute(side(edges[3], 15), "col", up)
    after = lax.ppermute(side(edges[2], 0), "col", down)

    def ints(a):
        return a.astype(F32).astype(jnp.int32)

    wide_insts = jnp.concatenate(
        [ints(before[512:514, :16])[:, :, None], insts, ints(after[512:514, :16])[:, :, None]], 2
    )

    def strip(pixels, rows, lanes, line):
        full = jnp.concatenate([pixels.astype(BF16), before[rows, lanes], after[rows, lanes]], 1)
        lines = jnp.pad(wide_insts[:, line, :].astype(BF16), ((0, 14), (0, SIDE + 128 - 18)))
        return jnp.concatenate([full, lines], 0)

    top = strip(edges[0], slice(0, 64), slice(0, 64), 0)
    bottom = strip(edges[1], slice(448, 512), slice(64, 128), 15)
    for_near, for_far = jnp.where(core == 0, bottom, top), jnp.where(core == 0, top, bottom)
    parts = gathered_far(group)
    _, for_near, for_far = lax.optimization_barrier((parts[1], for_near, for_far))
    near_strip, far_strip = send(for_near, SWAP), send(for_far, OVER)

    from_near, from_far = ints(near_strip[64:66, :18]), ints(far_strip[64:66, :18])
    above, below = jnp.where(core == 0, from_far, from_near), jnp.where(core == 0, from_near, from_far)
    all_insts = jnp.concatenate([above[:, None, :], wide_insts, below[:, None, :]], 1)
    all_master, all_orient = all_insts[0], all_insts[1]

    matches = all_master[..., None] == jnp.arange(owner_map.shape[0], dtype=jnp.int32)
    slots = jnp.sum(jnp.where(matches, owner_map, 0), axis=-1)
    dy, dz = y ^ (slots // 64), z ^ ((slots // 16) % 4)
    half, entry = (slots // 8) % 2, slots % 8
    high = (dy // 2) + 2 * (dz // 2)
    mixed = (dy // 2 ^ dy % 2) + 2 * (dz // 2 ^ dz % 2)
    outer, inner = jnp.where(half == 0, mixed, high), jnp.where(half == 0, high, mixed)
    locs = (jnp.where(half == core, 0, 1) * 16 + outer * 4 + inner) * 8 + entry
    inside = jnp.stack([row > 0, row < 7, col > 0, col < 15]).astype(jnp.int32)
    codes = jnp.concatenate([locs.reshape(-1), all_orient.reshape(-1), inside, core.reshape(1).astype(jnp.int32)])

    vmem, smem = pl.BlockSpec(memory_space=pltpu.VMEM), pl.BlockSpec(memory_space=pltpu.SMEM)
    anywhere = pl.BlockSpec(memory_space=pl.ANY)
    wide = jax.ShapeDtypeStruct((SIDE, SIDE), F32)
    sums_shape = jax.ShapeDtypeStruct((32, 32, 128), BF16)
    tables = [spectra.reshape(2, BAND, NK * BAND), *constant_tables()]
    resist, free_new, *sums = pl.pallas_call(
        main_kernel,
        out_shape=(wide, wide, *[sums_shape] * 8),
        in_specs=[smem] * 2 + [anywhere] * 8 + [vmem] * 4 + [anywhere] * (2 + len(tables)),
        out_specs=(anywhere, anywhere, *[vmem] * 8),
        scratch_shapes=[
            pltpu.VMEM((512, 32, 128), F32),
            pltpu.VMEM((1152, 1152), BF16),
            pltpu.VMEM((SIDE, SIDE), F32),
            pltpu.VMEM((NK, GRID, 2 * GRID), F32),
            pltpu.VMEM((256, 1024), BF16),
            pltpu.VMEM((512, 1024), BF16),
            pltpu.VMEM((512, 32, 128), F32),
            pltpu.VMEM((SIDE, SIDE), F32),
            pltpu.VMEM((SIDE, SIDE), F32),
            *(pltpu.VMEM(t.shape, t.dtype) for t in tables),
            *[pltpu.VMEM((32, 32, 128), BF16)] * 8,
            pltpu.SemaphoreType.DMA((4,)),
            pltpu.SemaphoreType.DMA((len(tables),)),
            pltpu.SemaphoreType.DMA((1,)),
            pltpu.SemaphoreType.DMA((4,)),
            pltpu.SemaphoreType.DMA((4,)),
            pltpu.SemaphoreType.DMA((8,)),
        ],
        compiler_params=pltpu.CompilerParams(vmem_limit_bytes=52 * 1024 * 1024),
        name="image_and_gradient",
    )(codes, weights, *parts, near_strip, far_strip, before, after, tile_free, target, *tables)

    summed = scattered_sum(sums[:4], sums[4:])
    fresh = smooth(own_cells.reshape(8, CELL, CELL) - 0.05 * from_wire(summed))
    fresh_wire = jnp.concatenate([fresh[:, :32, :], fresh[:, 32:, :]], axis=2).astype(BF16)
    parts = gathered_far(gathered_near(fresh_wire))
    new_mask = pl.pallas_call(
        final_kernel,
        out_shape=wide,
        in_specs=[smem] + [anywhere] * 9,
        out_specs=anywhere,
        scratch_shapes=[
            pltpu.VMEM((512, 32, 128), F32),
            pltpu.VMEM((SIDE, SIDE), F32),
            *[pltpu.VMEM((32, 32, 128), BF16)] * 8,
            *[pltpu.SemaphoreType.DMA((8,))] * 3,
        ],
        compiler_params=pltpu.CompilerParams(vmem_limit_bytes=52 * 1024 * 1024),
        name="final_mask",
    )(codes, *parts, free_new)
    mine = from_wire(parts[0][:8]).reshape(8, CELL * CELL).astype(F32)
    others = from_wire(parts[4][:8]).reshape(8, CELL * CELL).astype(F32)
    masters_out = jnp.where(core == 0, jnp.concatenate([mine, others], 0), jnp.concatenate([others, mine], 0))
    return resist, new_mask, masters_out


def solution(mesh):
    placed = (P("col", None), P(*BOTH), P(*BOTH), P(), P(*BOTH), P(*BOTH), P(), P())
    return jax.shard_map(
        per_device,
        mesh=mesh,
        in_specs=placed,
        out_specs=(P(*BOTH), P(*BOTH), P("col", None)),
        check_vma=False,
    )
```
